512 devices in a mesh: gx: 32 (over z, x), gy: 16 (over y, core).
Axes of the slice: x: 4, y: 8, z: 8, core: 2. Of those that a mesh axis runs over, the one named last changes fastest.
Arguments:
- probes: bfloat16 [48, 4, 512, 4096], P(None, None, 'gx', 'gy'), may hold values from -6 to 6
- classes: int32 [4, 512, 4096], P(None, 'gx', 'gy'), may hold values from 0 to 7
- class_table: float32 [8], replicated, may hold values from 0.3 to 3
- weights: float32 [4, 512, 4096], P(None, 'gx', 'gy'), may hold values from 5 to 500
- prior_block: float32 [4096, 256], P('gy'), may hold values from -0.1875 to 0.1875
- prior_left: float32 [8, 16, 4096], P(None, None, 'gy'), may hold values from -1.5 to 1.5
- prior_right: float32 [8, 16, 4096], P(None, None, 'gy'), may hold values from -6 to 6
- block_ranks: int32 [8], replicated, may hold values from 4 to 16
Outputs:
- basis: float32 [48, 4, 512, 4096], P(None, None, 'gx', 'gy')
- projected: float32 [48, 48], replicated
The draws below stay inside these ranges and needn't reach their ends.
All inputs are finite; a program needn't handle non-finite values.
Results may differ from the reference program's by a relative error of at most 0.0018.
Values may be sent and summed in bfloat16 or wider, within the bound.
A program may use at most 64 MiB of HBM per device.

```python
import math
import jax
import jax.numpy as jnp
from jax import lax

K = 48
NZ = 4
CY = 256
NCLASS = 8
R = 16
LEVMAX = 8
NX = 512
NY = 4096
CELLS = 8388608
N_GY = 16


def place_ends(values, rng, smallest, top_value):
    extent = values.shape
    spot = [jax.random.randint(jax.random.fold_in(rng, axis), (), 0, extent[axis]) for axis in range(len(extent))]
    values = values.at[tuple(spot)].set(smallest)
    longest = extent.index(max(extent))
    spot[longest] = (spot[longest] + 1) % extent[longest]
    return values.at[tuple(spot)].set(top_value)


def block_scale(own_key, shape, pieces, least, largest):
    factor_of = 1.0
    for position, shards_of in pieces:
        draws = jax.random.uniform(jax.random.fold_in(jax.random.fold_in(own_key, 6), position), (shards_of,), jnp.float32, least / len(pieces), largest / len(pieces))
        factor_of = factor_of * jnp.repeat(jnp.exp(draws), shape[position] // shards_of).reshape((-1,) + (1,) * (len(shape) - 1 - position))
    return factor_of


def centred(rng, shape, spread, reach, pieces=(), kind=jnp.bfloat16):
    gain = block_scale(rng, shape, pieces, -0.22, 0.18) if pieces else 1.0
    values = jax.random.normal(rng, shape, jnp.float32) * spread * gain
    return jnp.minimum(jnp.maximum(values, -reach), reach).astype(kind)


def setup_inputs(seed: int = 0) -> dict:
    streams_of = jax.random.split(jax.random.key(seed), 9)
    return {
        "probes": centred(streams_of[0], (K, NZ, NX, NY), 1.0, 6.0, ((2, 32), (3, 16))),
        "classes": place_ends(jax.random.randint(streams_of[1], (NZ, NX, NY), 0, NCLASS), jax.random.fold_in(streams_of[1], 1), 0, NCLASS - 1).astype(jnp.int32),
        "class_table": jnp.clip(jnp.exp(jax.random.uniform(streams_of[2], (NCLASS,), jnp.float32, math.log(0.3), math.log(3.0))), 0.3, 3.0),
        "weights": jnp.clip(jnp.exp(math.log(500.0) - 4.6051702 * jax.random.uniform(streams_of[3], (NZ, NX, NY), jnp.float32) ** block_scale(streams_of[3], (NZ, NX, NY), ((1, 32), (2, 16)), -0.2, 0.2)), 5.0, 500.0),
        "prior_block": centred(streams_of[4], (NY, CY), (4 * CY) ** -0.5, 0.1875, ((0, 16),), jnp.float32),
        "prior_left": centred(streams_of[5], (LEVMAX, R, NY), R ** -0.5, 1.5, ((2, 16),), jnp.float32),
        "prior_right": centred(streams_of[6], (LEVMAX, R, NY), 1.0, 6.0, ((2, 16),), jnp.float32),
        "block_ranks": place_ends(jax.random.randint(streams_of[7], (LEVMAX,), R // 4, R + 1), jax.random.fold_in(streams_of[7], 1), R // 4, R).astype(jnp.int32),
    }


HIGH = lax.Precision.HIGHEST

def face_parts(cond_ext):
    centre = cond_ext[:, 1:-1, 1:-1]
    padded_z = jnp.pad(centre, ((1, 1), (0, 0), (0, 0)))
    face_terms = [0.5 * (centre + cond_ext[:, 2:, 1:-1]), 0.5 * (centre + cond_ext[:, :-2, 1:-1]), 0.5 * (centre + cond_ext[:, 1:-1, 2:]), 0.5 * (centre + cond_ext[:, 1:-1, :-2]), 0.5 * (centre + padded_z[2:]), 0.5 * (centre + padded_z[:-2])]
    diagonal_part = 1.0 + face_terms[0] + face_terms[1] + face_terms[2] + face_terms[3] + face_terms[4] + face_terms[5]
    return (face_terms, diagonal_part)

def neighbour_sum(values_ext, face_terms):
    padded_z = jnp.pad(values_ext[:, :, 1:-1, 1:-1], ((0, 0), (1, 1), (0, 0), (0, 0)))
    others = [values_ext[:, :, 2:, 1:-1], values_ext[:, :, :-2, 1:-1], values_ext[:, :, 1:-1, 2:], values_ext[:, :, 1:-1, :-2], padded_z[:, 2:], padded_z[:, :-2]]
    total = face_terms[0] * others[0]
    for index in range(1, 6):
        total = total + face_terms[index] * others[index]
    return total

def pad_plane(values):
    return jnp.pad(values, ((0, 0), (0, 0), (1, 1), (1, 1)))

def prior_apply(field, prior_block, prior_left, prior_right, block_ranks):
    line_rows = field.reshape(NZ * NX, NY)
    row_count = NZ * NX
    leaf_count = NY // CY
    blocks = line_rows.reshape(row_count, leaf_count, CY)
    full_block = prior_block.reshape(leaf_count, CY, CY) + jnp.eye(CY, dtype=jnp.float32)[None]
    result = jnp.einsum('pbj,bij->pbi', blocks, full_block, precision=HIGH).reshape(row_count, NY)
    level_count = N_GY.bit_length() - 1
    rank_index = jnp.arange(R, dtype=jnp.int32)
    for level_index in range(level_count):
        group = CY * 2 ** (level_index + 1)
        half = group // 2
        groups = NY // group
        split_rows = line_rows.reshape(row_count, groups, 2, half)
        right_part = prior_right[level_index].reshape(R, groups, 2, half)
        left_part = prior_left[level_index].reshape(R, groups, 2, half)
        rank_mask = (rank_index < block_ranks[level_index]).astype(jnp.float32) * float(CY * 2 ** level_index) ** (-0.5)
        coefficients = jnp.einsum('pgah,rgah->pgar', split_rows, right_part, precision=HIGH) * rank_mask
        swapped = coefficients[:, :, ::-1, :]
        result = result + jnp.einsum('pgar,rgah->pgah', swapped, left_part, precision=HIGH).reshape(row_count, NY)
    return result.reshape(NZ, NX, NY)

def reference(probes, classes, class_table, weights, prior_block, prior_left, prior_right, block_ranks):
    conductivity = class_table[classes]
    cond_pad = jnp.pad(conductivity, ((0, 0), (1, 1), (1, 1)))
    face_terms, diagonal_part = face_parts(cond_pad)

    def sketch_one(probe):
        source = probe.astype(jnp.float32)[None]
        first_fwd = source / diagonal_part
        second_fwd = (source + neighbour_sum(pad_plane(first_fwd), face_terms)) / diagonal_part
        misfit = weights * second_fwd
        first_adj = misfit / diagonal_part
        second_adj = (misfit + neighbour_sum(pad_plane(first_adj), face_terms)) / diagonal_part
        return (second_adj + source)[0]
    sketch = lax.map(sketch_one, probes)
    flattened = sketch.reshape(K, -1)
    gram_matrix = jnp.dot(flattened, flattened.T, precision=HIGH) / float(CELLS)
    lower_factor = jnp.linalg.cholesky(gram_matrix)
    inverse = jax.scipy.linalg.solve_triangular(lower_factor, jnp.eye(K, dtype=jnp.float32), lower=True)
    basis_flat = jnp.dot(inverse, flattened, precision=HIGH)
    basis = basis_flat.reshape(K, NZ, NX, NY)

    def project_one(field):
        applied = prior_apply(field, prior_block, prior_left, prior_right, block_ranks)
        return jnp.dot(basis_flat, applied.reshape(-1), precision=HIGH)
    rows = lax.map(project_one, basis)
    projected = rows.T / float(CELLS)
    return (basis, projected)
```

```python
import functools

import jax
import jax.numpy as jnp
from jax import lax
from jax.experimental import pallas as pl
from jax.experimental.pallas import tpu as pltpu
from jax.sharding import PartitionSpec as P

MESH = pl.DeviceIdType.MESH
HIGH = lax.Precision.HIGHEST
F32 = jnp.float32
BF16 = jnp.bfloat16
LANES = 128
VMEM = pl.BlockSpec(memory_space=pltpu.VMEM)
SMEM = pl.BlockSpec(memory_space=pltpu.SMEM)
ANY = pl.BlockSpec(memory_space=pl.ANY)
NT = (((1,), (1,)), ((), ()))


def signal_all(devices):
    barrier = pltpu.get_barrier_semaphore()
    for device in devices:
        pl.semaphore_signal(barrier, inc=1, device_id=device, device_id_type=MESH)
    return barrier, len(devices)


def remote(src, dst, send, recv, device):
    copy = pltpu.make_async_remote_copy(
        src_ref=src, dst_ref=dst, send_sem=send, recv_sem=recv, device_id=device, device_id_type=MESH
    )
    copy.start()
    return copy


def halo_kernel(
    ng, ny, k, nz, nx,
    probes, classes, table, weights,
    pt, xh, hy, cx, cy, cond,
    pf, hs, cxs, cys, send_sem, recv_sem,
):
    gx, gy = lax.axis_index("gx"), lax.axis_index("gy")
    east, west = lax.rem(gx + 1, ng), lax.rem(gx + ng - 1, ng)
    north, south = lax.rem(gy + 1, ny), lax.rem(gy + ny - 1, ny)
    around = [(west, gy), (east, gy)]
    for column in (south, north):
        for row in (west, gx, east):
            around.append((row, column))
    barrier, count = signal_all(around)

    lines = nz * nx
    chunk = 512

    def widen(i, carry):
        rows = pl.ds(pl.multiple_of(i * chunk, chunk), chunk)
        value = probes[rows, :].astype(F32)
        pf[0, rows, :] = value[:, :LANES]
        pf[1, rows, :] = value[:, LANES:]
        return carry

    lax.fori_loop(0, k * lines // chunk, widen, 0)

    for z in range(nz):
        picked = classes[z]
        value = jnp.zeros(picked.shape, F32)
        for index in range(table.shape[0]):
            value = jnp.where(picked == index, table[index], value)
        cond[z] = value
        cxs[0, 4 * z : 4 * z + 3, :] = value[0:3, :]
        cxs[1, 4 * z : 4 * z + 3, :] = value[nx - 3 : nx, :]
        cxs[0, 4 * z + 3 : 4 * z + 4, :] = weights[z, 0:1, :]
        cxs[1, 4 * z + 3 : 4 * z + 4, :] = weights[z, nx - 1 : nx, :]
    lane = lax.broadcasted_iota(jnp.int32, (nx, LANES), 1)
    low = jnp.zeros((nx, LANES), F32)
    high = jnp.zeros((nx, LANES), F32)
    for z in range(nz):
        here = lane // 4 == z
        last = lane % 4 == 3
        first_tile, last_tile = cond[z, :, :LANES], cond[z, :, LANES:]
        w_first, w_last = weights[z, :, :LANES], weights[z, :, LANES:]
        own = jnp.where(last, pltpu.roll(w_first, 4 * z + 3, 1), pltpu.roll(first_tile, 4 * z, 1))
        low = jnp.where(here, own, low)
        own = jnp.where(last, pltpu.roll(w_last, 4 * z + 4, 1), pltpu.roll(last_tile, 4 * z + 3, 1))
        high = jnp.where(here, own, high)
    cys[0] = low
    cys[1] = high

    def turn(line):
        lo = pf[0, pl.ds(line, k, stride=lines), :]
        hi = pf[1, pl.ds(line, k, stride=lines), :]
        pt[line // nx, lax.rem(line, nx)] = jnp.concatenate([lo, hi], axis=1).astype(BF16)
        return lo, hi

    place = lax.broadcasted_iota(jnp.int32, (k, LANES), 1) // 2

    def edge_of(line, carry):
        low, high = carry
        lo, hi = turn(line)
        low = jnp.where(place == line, pltpu.roll(lo, 2 * line, 1), low)
        high = jnp.where(place == line, pltpu.roll(hi, lax.rem(2 * line + 2, LANES), 1), high)
        return low, high

    def outer(i, carry):
        part = lax.rem(i, 4)
        return edge_of((i // 4) * nx + jnp.where(part < 2, part, nx - 4 + part), carry)

    def inner(i, carry):
        return edge_of((i // (nx - 4)) * nx + 2 + lax.rem(i, nx - 4), carry)

    zero = jnp.zeros((k, LANES), F32)
    carry = lax.fori_loop(0, nz * 4, outer, (zero, zero))
    pl.semaphore_wait(barrier, count)
    copies = [
        remote(pt.at[:, nx - 2 : nx], xh.at[0], send_sem.at[0], recv_sem.at[0], (east, gy)),
        remote(pt.at[:, 0:2], xh.at[1], send_sem.at[1], recv_sem.at[1], (west, gy)),
        remote(cxs.at[1], cx.at[0], send_sem.at[2], recv_sem.at[2], (east, gy)),
        remote(cxs.at[0], cx.at[1], send_sem.at[3], recv_sem.at[3], (west, gy)),
    ]
    low, high = lax.fori_loop(0, nz * (nx - 4), inner, carry)
    hs[0] = low.astype(BF16)
    hs[1] = high.astype(BF16)
    used = 4
    for side, column in ((0, north), (1, south)):
        for which, row in ((2, west), (1, gx), (0, east)):
            slot = side * 3 + which
            source = 1 - side
            copies.append(
                remote(hs.at[source], hy.at[slot], send_sem.at[used], recv_sem.at[used], (row, column))
            )
            copies.append(
                remote(
                    cys.at[source], cy.at[slot], send_sem.at[used + 1], recv_sem.at[used + 1], (row, column)
                )
            )
            used += 2
    for copy in copies:
        copy.wait()


def sketch_kernel(
    ng, ny, k, nz, nx, levels, leaf,
    pt, xh, hy, cx, cy, cond, weights, block, left, right, ranks,
    shl, gram, leafpart, uc,
    ce, dg, dd, wd, fx, fyp, fym, fz, f1, a1, wt, acc, cuf,
):
    gx, gy = lax.axis_index("gx"), lax.axis_index("gy")
    has_west = (gx > 0).astype(F32)
    has_east = (gx < ng - 1).astype(F32)
    has_south = (gy > 0).astype(F32)
    has_north = (gy < ny - 1).astype(F32)
    has_x = (has_west, 1.0, has_east)
    has_y = (has_south, has_north)
    rank = left.shape[1]

    wt[0:leaf, :] = block[...].astype(BF16)
    row = lax.broadcasted_iota(jnp.int32, (rank, leaf), 0)
    for level in range(levels):
        gain = jnp.where(row < ranks[level], float(leaf * 2**level) ** -0.5, 0.0)
        at = leaf + 2 * level * rank
        wt[at : at + rank, :] = (right[level] * gain).astype(BF16)
        wt[at + rank : at + 2 * rank, :] = left[level].astype(BF16)

    tall = nx + 16
    wide = 3 * LANES
    lane = lax.broadcasted_iota(jnp.int32, (nx, LANES), 1)
    for z in range(nz):
        ce[z] = jnp.zeros((tall, wide), F32)
        wd[z] = jnp.zeros((tall, wide), F32)
        ce[z, 8 : 8 + nx, 0 : 2 * LANES] = cond[z]
        wd[z, 8 : 8 + nx, 0 : 2 * LANES] = weights[z]
        ce[z, 5:8, 0 : 2 * LANES] = cx[0, 4 * z : 4 * z + 3, :] * has_west
        wd[z, 7:8, 0 : 2 * LANES] = cx[0, 4 * z + 3 : 4 * z + 4, :] * has_west
        ce[z, 8 + nx : 11 + nx, 0 : 2 * LANES] = cx[1, 4 * z : 4 * z + 3, :] * has_east
        wd[z, 8 + nx : 9 + nx, 0 : 2 * LANES] = cx[1, 4 * z + 3 : 4 * z + 4, :] * has_east
        for which in range(3):
            above = cy[3 + which] * (has_x[which] * has_y[1])
            below = cy[which] * (has_x[which] * has_y[0])
            value = jnp.where(lane < 3, pltpu.roll(above, (LANES - 4 * z) % LANES, 1), 0.0)
            value = jnp.where(lane > LANES - 4, pltpu.roll(below, LANES - 3 - 4 * z, 1), value)
            if which == 0:
                ce[z, 0:8, 2 * LANES :] = value[nx - 8 :, :]
            elif which == 2:
                ce[z, 8 + nx :, 2 * LANES :] = value[:8, :]
            else:
                ce[z, 8 : 8 + nx, 2 * LANES :] = value
                value = jnp.where(lane == 0, pltpu.roll(above, LANES - 3 - 4 * z, 1), 0.0)
                value = jnp.where(lane == LANES - 1, pltpu.roll(below, LANES - 4 - 4 * z, 1), value)
                wd[z, 8 : 8 + nx, 2 * LANES :] = value
    for z in range(nz):
        centre = ce[z]
        upper = ce[z + 1] if z + 1 < nz else jnp.zeros_like(centre)
        lower = ce[z - 1] if z > 0 else jnp.zeros_like(centre)
        face_x = 0.5 * (centre + pltpu.roll(centre, tall - 1, 0))
        face_y = 0.5 * (centre + pltpu.roll(centre, wide - 1, 1))
        back_y = pltpu.roll(face_y, 1, 1)
        face_z = 0.5 * (centre + upper)
        total = 1.0 + face_x + pltpu.roll(face_x, 1, 0) + face_y + back_y
        total = total + face_z + 0.5 * (centre + lower)
        inverse = 1.0 / total
        fx[z] = face_x
        fyp[z] = face_y
        fym[z] = back_y
        fz[z] = face_z
        dg[z] = total
        dd[z] = inverse
        wd[z] = wd[z] * inverse

    tile_lane = lax.broadcasted_iota(jnp.int32, (k, LANES), 1)

    def tiles(ref, z, x):
        whole = ref[z, pl.ds(x + 8, 1), :]
        return [whole[:, i * LANES : (i + 1) * LANES] for i in range(3)]

    def split(value):
        return [value[:, i * LANES : (i + 1) * LANES] for i in range(value.shape[1] // LANES)]

    def store(ref, z, x, parts):
        for i in range(len(parts)):
            ref[z, x, :, i * LANES : (i + 1) * LANES] = parts[i]

    def edge_tile(z, x, which):
        line = z * nx + x
        above = hy[3 + which].astype(F32) * (has_x[which] * has_y[1])
        below = hy[which].astype(F32) * (has_x[which] * has_y[0])
        above = pltpu.roll(above, lax.rem(LANES - 2 * line + LANES, LANES), 1)
        below = pltpu.roll(below, lax.rem(2 * LANES - 2 - 2 * line, LANES), 1)
        value = jnp.where(tile_lane < 2, above, 0.0)
        return jnp.where(tile_lane >= LANES - 2, below, value)

    def forward(z, x, value, edge):
        inverse = tiles(dd, z, x)
        parts = split(value) + [edge]
        store(f1, z, x + 2, [parts[i] * inverse[i] for i in range(3)])

    def forward_inner(x, carry):
        for z in range(nz):
            forward(z, x, pt[z, x].astype(F32), edge_tile(z, x, 1))
        return carry

    lax.fori_loop(0, nx, forward_inner, 0)
    for z in range(nz):
        for i in range(2):
            forward(z, i - 2, xh[0, z, i].astype(F32) * has_west, edge_tile(z, nx - 2 + i, 0))
            forward(z, nx + i, xh[1, z, i].astype(F32) * has_east, edge_tile(z, i, 2))

    def near(ref, z, x, row, count):
        centre = split(ref[z, row])
        ahead = [pltpu.roll(part, LANES - 1, 1) for part in centre]
        behind = [pltpu.roll(part, 1, 1) for part in centre]
        east, west = split(ref[z, row + 1]), split(ref[z, row - 1])
        face_e, face_w = tiles(fx, z, x), tiles(fx, z, x - 1)
        face_n, face_s = tiles(fyp, z, x), tiles(fym, z, x)
        if z + 1 < nz:
            upper, face_u = split(ref[z + 1, row]), tiles(fz, z, x)
        if z > 0:
            lower, face_d = split(ref[z - 1, row]), tiles(fz, z - 1, x)
        sums = []
        for i in range(count):
            north = jnp.where(tile_lane == LANES - 1, ahead[(i + 1) % 3], ahead[i])
            south = jnp.where(tile_lane == 0, behind[(i + 2) % 3], behind[i])
            total = face_e[i] * east[i] + face_w[i] * west[i]
            total = total + (face_n[i] * north + face_s[i] * south)
            if z + 1 < nz:
                total = total + face_u[i] * upper[i]
            if z > 0:
                total = total + face_d[i] * lower[i]
            sums.append(total)
        return centre, sums

    def adjoint(i, carry):
        x = i - 1
        for z in range(nz):
            centre, sums = near(f1, z, x, x + 2, 3)
            diagonal, inverse, gain = tiles(dg, z, x), tiles(dd, z, x), tiles(wd, z, x)
            parts = [
                (centre[i] * diagonal[i] + sums[i]) * gain[i] * inverse[i] for i in range(3)
            ]
            store(a1, z, x + 1, parts)
        return carry

    lax.fori_loop(0, nx + 2, adjoint, 0)

    acc[...] = jnp.zeros_like(acc)

    def finish(x, carry):
        whole_high, whole_low = [], []
        for z in range(nz):
            centre, sums = near(a1, z, x, x + 1, 2)
            diagonal, inverse = tiles(dg, z, x), tiles(dd, z, x)
            source = split(pt[z, x].astype(F32))
            sketch = jnp.concatenate(
                [
                    (centre[i] * diagonal[i] + sums[i]) * inverse[i] + source[i]
                    for i in range(2)
                ],
                axis=1,
            )
            high = sketch.astype(BF16)
            low = (sketch - high.astype(F32)).astype(BF16)
            shl[z * nx + x, 0:k, :] = high
            shl[z * nx + x, k : 2 * k, :] = low
            whole_high.append(high)
            whole_low.append(low)
        applied = lax.dot_general(
            jnp.concatenate(whole_high, axis=0), wt[...], NT, preferred_element_type=F32
        )
        rows = []
        for z in range(nz):
            part = applied[z * k : (z + 1) * k]
            cuf[z * nx + x] = part[:, leaf:]
            rows.append(part[:, :leaf].astype(BF16))
        high = jnp.concatenate(whole_high, axis=1)
        low = jnp.concatenate(whole_low, axis=1)
        lhs = jnp.concatenate([high, low], axis=0)
        rhs = jnp.concatenate([high, low, jnp.concatenate(rows, axis=1)], axis=0)
        acc[...] += lax.dot_general(lhs, rhs, NT, preferred_element_type=F32)
        return carry

    lax.fori_loop(0, nx, finish, 0)

    pad = jnp.zeros((k, LANES - k), F32)
    value = acc[...]
    total = value[0:k, 0:k] + (value[0:k, k : 2 * k] + value[k : 2 * k, 0:k]) + value[k:, k : 2 * k]
    gram[...] = jnp.concatenate([total, pad], axis=1)
    total = value[0:k, 2 * k :] + value[k:, 2 * k :]
    leafpart[...] = jnp.concatenate([total, pad], axis=1)

    count = LANES // rank
    slot = tile_lane // rank

    def gather(group, carry):
        parts = [cuf[group * count + j] for j in range(count)]
        step = 1
        while step < count:
            bit = (slot // step) % 2 == 0
            for i in range(count):
                if (i // step) % 2 == 0:
                    one, two = parts[i], parts[i + step]
                    parts[i] = jnp.where(bit, one, pltpu.roll(two, step * rank, 1))
                    parts[i + step] = jnp.where(bit, pltpu.roll(one, LANES - step * rank, 1), two)
            step *= 2
        for index in range(2 * levels):
            uc[index, group] = parts[index].astype(BF16)
        return carry

    lax.fori_loop(0, nz * nx // count, gather, 0)


def reduce_kernel(
    ng, ny, k, levels, groups, cells,
    gram, leafpart, uc,
    linv, projected,
    pieces, rs, sums, ar, totals, ag, trees, sems,
):
    gx, gy = lax.axis_index("gx"), lax.axis_index("gy")
    rows = k // ny
    column = [lax.rem(gy + d, ny) for d in range(1, ny)]
    across = [lax.rem(gx + d, ng) for d in range(1, ng)]
    barrier, count = signal_all([(gx, e) for e in column] + [(e, gy) for e in across])
    send_sem, recv_sem, tree_send, tree_recv = sems

    def scatter(which, value):
        for i in range(k):
            pieces[which, i // rows, i % rows, :] = value[i, :]
        rs[which, gy] = pieces[which, gy]
        return [
            remote(
                pieces.at[which, e], rs.at[which, gy],
                send_sem.at[which, 0, d], recv_sem.at[which, 0, d], (gx, e),
            )
            for d, e in enumerate(column)
        ]

    def added(ref, which, count):
        parts = [ref[which, i] for i in range(count)]
        while len(parts) > 1:
            parts = [
                parts[i] + parts[i + 1] if i + 1 < len(parts) else parts[i]
                for i in range(0, len(parts), 2)
            ]
        return parts[0]

    def exchange(which, copies):
        for copy in copies:
            copy.wait()
        sums[which] = added(rs, which, ny)
        ar[which, gx] = sums[which]
        return [
            remote(
                sums.at[which], ar.at[which, gx],
                send_sem.at[which, 1, d], recv_sem.at[which, 1, d], (e, gy),
            )
            for d, e in enumerate(across)
        ]

    def spread(which, copies):
        for copy in copies:
            copy.wait()
        totals[which] = added(ar, which, ng)
        ag[which, gy] = totals[which]
        return [
            remote(
                totals.at[which], ag.at[which, gy],
                send_sem.at[which, 2, d], recv_sem.at[which, 2, d], (gx, e),
            )
            for d, e in enumerate(column)
        ]

    def collect(which, copies):
        for copy in copies:
            copy.wait()
        parts = [ag[which, i // rows, i % rows : i % rows + 1, :] for i in range(k)]
        return jnp.concatenate(parts, axis=0) * (1.0 / cells)

    pl.semaphore_wait(barrier, count)
    flight = scatter(0, gram[...])

    def flipped(bits):
        device = gy
        for b in range(levels):
            if bits >> b & 1:
                device = device + (1 - 2 * lax.rem(device // 2**b, 2)) * 2**b
        return device

    tree = []
    for level in range(levels):
        half = 2**level
        share = groups // half
        for bits in range(1, 2 * half):
            peer = flipped(bits)
            kind = 2 * level + (1 if bits < half else 0)
            begin = lax.rem(peer, half) * share
            tree.append(
                remote(
                    uc.at[kind, pl.ds(begin, share)], trees[level].at[bits - 1],
                    tree_send.at[2 * half - 2 - level + bits], tree_recv.at[2 * half - 2 - level + bits],
                    (gx, peer),
                )
            )

    flight = exchange(0, flight)
    for copy in tree:
        copy.wait()
    total = leafpart[:, 0:k]
    for level in range(levels):
        half = 2**level
        share = groups // half
        begin = lax.rem(gy, half) * share
        for j in range(share):
            own = uc[2 * level + 1, begin + j].astype(F32)
            for bits in range(1, half):
                own = own + trees[level][bits - 1, j].astype(F32)
            other = trees[level][half - 1, j].astype(F32)
            for bits in range(half + 1, 2 * half):
                other = other + trees[level][bits - 1, j].astype(F32)
            total = total + lax.dot_general(
                own.astype(BF16), other.astype(BF16), NT, preferred_element_type=F32
            )
    total = jnp.concatenate([total, jnp.zeros((k, LANES - k), F32)], axis=1)
    flight = spread(0, flight)
    second = scatter(1, total)
    matrix = collect(0, flight)

    row = lax.broadcasted_iota(jnp.int32, (k, LANES), 0)
    lane = lax.broadcasted_iota(jnp.int32, (k, LANES), 1)
    start = LANES // 2
    whole = jnp.where(lane < k, matrix, jnp.where(lane == row + start, 1.0, 0.0))
    blocks = [whole[8 * t : 8 * t + 8] for t in range(k // 8)]
    inner = lax.broadcasted_iota(jnp.int32, (8, LANES), 0)
    for j in range(k):
        t, s = divmod(j, 8)
        pivot_row = blocks[t][s : s + 1, :]
        scaled = pivot_row * (1.0 / pivot_row[:, j : j + 1])
        for i in range(t, k // 8):
            factor = blocks[i][:, j : j + 1]
            change = factor * scaled
            if i == t:
                change = jnp.where(inner > s, change, 0.0)
            blocks[i] = blocks[i] - change
        if j == k // 3:
            second = exchange(1, second)
        if j == k - k // 6:
            second = spread(1, second)
    whole = jnp.concatenate(blocks, axis=0)
    pivots = jnp.sum(jnp.where(lane == row, whole, 0.0), axis=1, keepdims=True)
    inverse = whole[:, start : start + k] / jnp.sqrt(pivots)
    linv[...] = inverse
    middle = collect(1, second)[:, 0:k]
    product = jnp.dot(inverse, middle, precision=HIGH, preferred_element_type=F32)
    product = lax.dot_general(product, inverse, NT, precision=HIGH, preferred_element_type=F32)
    projected[...] = product + jnp.where(lane[:, 0:k] == row[:, 0:k], 1.0, 0.0)


def basis_kernel(k, nz, nx, shl, linv, out, buffer, sem):
    inverse = linv[...]
    high = inverse.astype(BF16)
    low = (inverse - high.astype(F32)).astype(BF16)
    lhs = jnp.concatenate(
        [
            jnp.concatenate([high, high], axis=1),
            jnp.concatenate([low, jnp.zeros_like(low)], axis=1),
        ],
        axis=0,
    )
    copies = []
    for z in range(nz):

        def one(x, carry):
            value = jnp.dot(lhs, shl[z * nx + x], preferred_element_type=F32)
            value = value[0:k] + value[k:]
            buffer[z, 0, pl.ds(x, k, stride=nx), :] = value[:, :LANES]
            buffer[z, 1, pl.ds(x, k, stride=nx), :] = value[:, LANES:]
            return carry

        lax.fori_loop(0, nx, one, 0, unroll=4)
        for i in range(2):
            copy = pltpu.make_async_copy(
                buffer.at[z, i].reshape(k, nx, LANES),
                out.at[:, z, :, i * LANES : (i + 1) * LANES],
                sem.at[z, i],
            )
            copy.start()
            copies.append(copy)
    for copy in copies:
        copy.wait()


def params(**more):
    return pltpu.CompilerParams(vmem_limit_bytes=40 * 2**20, **more)


def shards(
    probes, classes, class_table, weights, prior_block, prior_left, prior_right, block_ranks
):
    ng, ny = lax.axis_size("gx"), lax.axis_size("gy")
    k, nz, nx, leaf = probes.shape
    levels = ny.bit_length() - 1
    rank = prior_left.shape[1]
    lines = nz * nx
    groups = lines * rank // LANES
    cells = float(nz * nx * leaf * ng * ny)
    shape = jax.ShapeDtypeStruct
    dma = pltpu.SemaphoreType.DMA

    pt, xh, hy, cx, cy, cond = pl.pallas_call(
        functools.partial(halo_kernel, ng, ny, k, nz, nx),
        out_shape=(
            shape((nz, nx, k, leaf), BF16),
            shape((2, nz, 2, k, leaf), BF16),
            shape((6, k, LANES), BF16),
            shape((2, 4 * nz, leaf), F32),
            shape((6, nx, LANES), F32),
            shape((nz, nx, leaf), F32),
        ),
        in_specs=[VMEM, VMEM, SMEM, VMEM],
        out_specs=(VMEM,) * 6,
        scratch_shapes=[
            pltpu.VMEM((2, k * lines, LANES), F32),
            pltpu.VMEM((2, k, LANES), BF16),
            pltpu.VMEM((2, 4 * nz, leaf), F32),
            pltpu.VMEM((2, nx, LANES), F32),
            dma((16,)),
            dma((16,)),
        ],
        compiler_params=params(collective_id=0, has_side_effects=True),
    )(probes.reshape(k * lines, leaf), classes, class_table, weights)

    field = pltpu.VMEM((nz, nx + 16, 3 * LANES), F32)
    shl, gram, leafpart, uc = pl.pallas_call(
        functools.partial(sketch_kernel, ng, ny, k, nz, nx, levels, leaf),
        out_shape=(
            shape((lines, 2 * k, leaf), BF16),
            shape((k, LANES), F32),
            shape((k, LANES), F32),
            shape((2 * levels, groups, k, LANES), BF16),
        ),
        in_specs=[VMEM] * 10 + [SMEM],
        out_specs=(VMEM,) * 4,
        scratch_shapes=[field] * 8
        + [
            pltpu.VMEM((nz, nx + 4, k, 3 * LANES), F32),
            pltpu.VMEM((nz, nx + 2, k, 3 * LANES), F32),
            pltpu.VMEM((leaf + LANES, leaf), BF16),
            pltpu.VMEM((2 * k, 3 * k), F32),
            pltpu.VMEM((lines, k, LANES), F32),
        ],
        compiler_params=params(),
    )(
        pt, xh, hy, cx, cy, cond, weights, prior_block, prior_left[:levels],
        prior_right[:levels], block_ranks,
    )

    rows = k // ny
    edges = 2 * ny
    linv, projected = pl.pallas_call(
        functools.partial(reduce_kernel, ng, ny, k, levels, groups, cells),
        out_shape=(shape((k, k), F32), shape((k, k), F32)),
        in_specs=[VMEM] * 3,
        out_specs=(VMEM, VMEM),
        scratch_shapes=[
            pltpu.VMEM((2, ny, rows, LANES), F32),
            pltpu.VMEM((2, ny, rows, LANES), F32),
            pltpu.VMEM((2, rows, LANES), F32),
            pltpu.VMEM((2, ng, rows, LANES), F32),
            pltpu.VMEM((2, rows, LANES), F32),
            pltpu.VMEM((2, ny, rows, LANES), F32),
            [
                pltpu.VMEM((2 ** (level + 1) - 1, groups >> level, k, LANES), BF16)
                for level in range(levels)
            ],
            [
                dma((2, 3, max(ny, ng))),
                dma((2, 3, max(ny, ng))),
                dma((edges,)),
                dma((edges,)),
            ],
        ],
        compiler_params=params(collective_id=1, has_side_effects=True),
    )(gram, leafpart, uc)

    basis = pl.pallas_call(
        functools.partial(basis_kernel, k, nz, nx),
        out_shape=shape((k, nz, nx, leaf), F32),
        in_specs=[VMEM, VMEM],
        out_specs=ANY,
        scratch_shapes=[
            pltpu.VMEM((nz, 2, k * nx, LANES), F32),
            dma((nz, 2)),
        ],
        compiler_params=params(),
    )(shl, linv)
    return basis, projected


def solution(mesh):
    return jax.shard_map(
        shards,
        mesh=mesh,
        in_specs=(
            P(None, None, "gx", "gy"),
            P(None, "gx", "gy"),
            P(),
            P(None, "gx", "gy"),
            P("gy", None),
            P(None, None, "gy"),
            P(None, None, "gy"),
            P(),
        ),
        out_specs=(P(None, None, "gx", "gy"), P()),
        check_vma=False,
    )
```

```python
import functools

import jax
import jax.numpy as jnp
from jax import lax
from jax.experimental import pallas as pl
from jax.experimental.pallas import tpu as pltpu
from jax.sharding import PartitionSpec as P

MESH = pl.DeviceIdType.MESH
HIGH = lax.Precision.HIGHEST
F32 = jnp.float32
BF16 = jnp.bfloat16
LANES = 128
VMEM = pl.BlockSpec(memory_space=pltpu.VMEM)
SMEM = pl.BlockSpec(memory_space=pltpu.SMEM)
ANY = pl.BlockSpec(memory_space=pl.ANY)
HBM = pl.BlockSpec(memory_space=pltpu.HBM)
NT = (((1,), (1,)), ((), ()))


def signal_all(devices):
    barrier = pltpu.get_barrier_semaphore()
    for device in devices:
        pl.semaphore_signal(barrier, inc=1, device_id=device, device_id_type=MESH)
    return barrier, len(devices)


def remote(src, dst, send, recv, device):
    copy = pltpu.make_async_remote_copy(
        src_ref=src, dst_ref=dst, send_sem=send, recv_sem=recv, device_id=device, device_id_type=MESH
    )
    copy.start()
    return copy


def sketch_kernel(
    ng, ny, k, nz, nx, levels, leaf, groups, cells,
    probes_in, classes_in, table_in, weights_in, block_in, left_in, right_in, ranks_in,
    shl_out, small_out,
    shl, small, store_sem, probes, classes, table, weights, block, left, right, ranks, load_sem,
    pt, cond, pf, xh, hy, cx, cy, hs, cxs, cys, send_sem, recv_sem,
    ce, dg, dd, wd, fx, fyp, fym, fz, f1, a1, wt, acc, cuf, uc,
    trees, tree_send, tree_recv, packed, gathered, sum_send, sum_recv,
):
    gx, gy = lax.axis_index("gx"), lax.axis_index("gy")
    east, west = lax.rem(gx + 1, ng), lax.rem(gx + ng - 1, ng)
    north, south = lax.rem(gy + 1, ny), lax.rem(gy + ny - 1, ny)
    around = [(west, gy), (east, gy)]
    for column in (south, north):
        for row in (west, gx, east):
            around.append((row, column))

    across, pair = min(4, ng), min(2, ny)
    deep, high_y = ng // across, ny // pair
    at_z, at_x = gx // across, lax.rem(gx, across)
    at_y, at_c = gy // pair, lax.rem(gy, pair)
    stages = [
        (
            [
                (
                    at_z * across + lax.rem(at_x + d % across, across),
                    at_y * pair + lax.rem(at_c + d // across, pair),
                )
                for d in range(1, across * pair)
            ],
            at_c * across + at_x,
        ),
        ([(gx, lax.rem(at_y + d, high_y) * pair + at_c) for d in range(1, high_y)], at_y),
        ([(lax.rem(at_z + d, deep) * across + at_x, gy) for d in range(1, deep)], at_z),
    ]
    column = [(gx, lax.rem(gy + d, ny)) for d in range(1, ny)]
    barrier, count = signal_all(around + stages[0][0] + stages[2][0] + column)

    loads = [
        pltpu.make_async_copy(source, target, load_sem.at[i])
        for i, (source, target) in enumerate(
            [
                (classes_in, classes),
                (weights_in, weights),
                (table_in, table),
                (probes_in, probes),
                (block_in, block),
                (left_in.at[0:levels], left),
                (right_in.at[0:levels], right),
                (ranks_in, ranks),
            ]
        )
    ]
    for load in loads:
        load.start()

    lines = nz * nx
    for load in loads[:3]:
        load.wait()

    for z in range(nz):
        picked = classes[z]
        value = jnp.zeros(picked.shape, F32)
        for index in range(table.shape[0]):
            value = jnp.where(picked == index, table[index], value)
        cond[z] = value
        cxs[0, 4 * z : 4 * z + 3, :] = value[0:3, :]
        cxs[1, 4 * z : 4 * z + 3, :] = value[nx - 3 : nx, :]
        cxs[0, 4 * z + 3 : 4 * z + 4, :] = weights[z, 0:1, :]
        cxs[1, 4 * z + 3 : 4 * z + 4, :] = weights[z, nx - 1 : nx, :]
    lane = lax.broadcasted_iota(jnp.int32, (nx, LANES), 1)
    low = jnp.zeros((nx, LANES), F32)
    high = jnp.zeros((nx, LANES), F32)
    for z in range(nz):
        here = lane // 4 == z
        last = lane % 4 == 3
        first_tile, last_tile = cond[z, :, :LANES], cond[z, :, LANES:]
        w_first, w_last = weights[z, :, :LANES], weights[z, :, LANES:]
        own = jnp.where(last, pltpu.roll(w_first, 4 * z + 3, 1), pltpu.roll(first_tile, 4 * z, 1))
        low = jnp.where(here, own, low)
        own = jnp.where(last, pltpu.roll(w_last, 4 * z + 4, 1), pltpu.roll(last_tile, 4 * z + 3, 1))
        high = jnp.where(here, own, high)
    cys[0] = low
    cys[1] = high

    loads[3].wait()
    chunk = 512

    def widen(i, carry):
        rows = pl.ds(pl.multiple_of(i * chunk, chunk), chunk)
        value = probes[rows, :].astype(F32)
        pf[0, rows, :] = value[:, :LANES]
        pf[1, rows, :] = value[:, LANES:]
        return carry

    lax.fori_loop(0, k * lines // chunk, widen, 0)

    place = lax.broadcasted_iota(jnp.int32, (k, LANES), 1) // 2

    def turn(line, carry):
        low, high = carry
        lo = pf[0, pl.ds(line, k, stride=lines), :]
        hi = pf[1, pl.ds(line, k, stride=lines), :]
        pt[line // nx, lax.rem(line, nx)] = jnp.concatenate([lo, hi], axis=1).astype(BF16)
        low = jnp.where(place == line, pltpu.roll(lo, 2 * line, 1), low)
        high = jnp.where(place == line, pltpu.roll(hi, lax.rem(2 * line + 2, LANES), 1), high)
        return low, high

    zero = jnp.zeros((k, LANES), F32)
    low, high = lax.fori_loop(0, lines, turn, (zero, zero), unroll=4)
    hs[0] = low.astype(BF16)
    hs[1] = high.astype(BF16)

    pl.semaphore_wait(barrier, count)
    field_copies = [
        remote(cxs.at[1], cx.at[0], send_sem.at[2], recv_sem.at[2], (east, gy)),
        remote(cxs.at[0], cx.at[1], send_sem.at[3], recv_sem.at[3], (west, gy)),
    ]
    probe_copies = []
    used = 4
    arrivals = [
        (side, which, row, column)
        for side, column in ((0, north), (1, south))
        for which, row in ((2, west), (1, gx), (0, east))
    ]
    for i, (side, which, row, column) in enumerate(arrivals):
        slot = side * 3 + which
        field_copies.append(
            remote(
                cys.at[1 - side], cy.at[slot], send_sem.at[4 + i], recv_sem.at[4 + i], (row, column)
            )
        )
    for i, (side, which, row, column) in enumerate(arrivals):
        slot = side * 3 + which
        probe_copies.append(
            remote(
                hs.at[1 - side], hy.at[slot], send_sem.at[10 + i], recv_sem.at[10 + i], (row, column)
            )
        )
    probe_copies += [
        remote(pt.at[:, nx - 2 : nx], xh.at[0], send_sem.at[0], recv_sem.at[0], (east, gy)),
        remote(pt.at[:, 0:2], xh.at[1], send_sem.at[1], recv_sem.at[1], (west, gy)),
    ]

    has_west = (gx > 0).astype(F32)
    has_east = (gx < ng - 1).astype(F32)
    has_south = (gy > 0).astype(F32)
    has_north = (gy < ny - 1).astype(F32)
    has_x = (has_west, 1.0, has_east)
    has_y = (has_south, has_north)
    rank = left.shape[1]
    for load in loads[4:]:
        load.wait()

    wt[0:leaf, :] = block[...].astype(BF16)
    row = lax.broadcasted_iota(jnp.int32, (rank, leaf), 0)
    for level in range(levels):
        gain = jnp.where(row < ranks[level], float(leaf * 2**level) ** -0.5, 0.0)
        at = leaf + 2 * level * rank
        wt[at : at + rank, :] = (right[level] * gain).astype(BF16)
        wt[at + rank : at + 2 * rank, :] = left[level].astype(BF16)

    for copy in field_copies:
        copy.wait_recv()

    tall = nx + 16
    wide = 3 * LANES
    lane = lax.broadcasted_iota(jnp.int32, (nx, LANES), 1)
    for z in range(nz):
        ce[z] = jnp.zeros((tall, wide), F32)
        wd[z] = jnp.zeros((tall, wide), F32)
        ce[z, 8 : 8 + nx, 0 : 2 * LANES] = cond[z]
        wd[z, 8 : 8 + nx, 0 : 2 * LANES] = weights[z]
        ce[z, 5:8, 0 : 2 * LANES] = cx[0, 4 * z : 4 * z + 3, :] * has_west
        wd[z, 7:8, 0 : 2 * LANES] = cx[0, 4 * z + 3 : 4 * z + 4, :] * has_west
        ce[z, 8 + nx : 11 + nx, 0 : 2 * LANES] = cx[1, 4 * z : 4 * z + 3, :] * has_east
        wd[z, 8 + nx : 9 + nx, 0 : 2 * LANES] = cx[1, 4 * z + 3 : 4 * z + 4, :] * has_east
        for which in range(3):
            above = cy[3 + which] * (has_x[which] * has_y[1])
            below = cy[which] * (has_x[which] * has_y[0])
            value = jnp.where(lane < 3, pltpu.roll(above, (LANES - 4 * z) % LANES, 1), 0.0)
            value = jnp.where(lane > LANES - 4, pltpu.roll(below, LANES - 3 - 4 * z, 1), value)
            if which == 0:
                ce[z, 0:8, 2 * LANES :] = value[nx - 8 :, :]
            elif which == 2:
                ce[z, 8 + nx :, 2 * LANES :] = value[:8, :]
            else:
                ce[z, 8 : 8 + nx, 2 * LANES :] = value
                value = jnp.where(lane == 0, pltpu.roll(above, LANES - 3 - 4 * z, 1), 0.0)
                value = jnp.where(lane == LANES - 1, pltpu.roll(below, LANES - 4 - 4 * z, 1), value)
                wd[z, 8 : 8 + nx, 2 * LANES :] = value
    for z in range(nz):
        centre = ce[z]
        upper = ce[z + 1] if z + 1 < nz else jnp.zeros_like(centre)
        lower = ce[z - 1] if z > 0 else jnp.zeros_like(centre)
        face_x = 0.5 * (centre + pltpu.roll(centre, tall - 1, 0))
        face_y = 0.5 * (centre + pltpu.roll(centre, wide - 1, 1))
        back_y = pltpu.roll(face_y, 1, 1)
        face_z = 0.5 * (centre + upper)
        total = 1.0 + face_x + pltpu.roll(face_x, 1, 0) + face_y + back_y
        total = total + face_z + 0.5 * (centre + lower)
        inverse = 1.0 / total
        fx[z] = face_x
        fyp[z] = face_y
        fym[z] = back_y
        fz[z] = face_z
        dg[z] = total
        dd[z] = inverse
        wd[z] = wd[z] * inverse

    tile_lane = lax.broadcasted_iota(jnp.int32, (k, LANES), 1)

    def tiles(ref, z, x):
        whole = ref[z, pl.ds(x + 8, 1), :]
        return [whole[:, i * LANES : (i + 1) * LANES] for i in range(3)]

    def split(value):
        return [value[:, i * LANES : (i + 1) * LANES] for i in range(value.shape[1] // LANES)]

    def store(ref, z, x, parts):
        for i in range(len(parts)):
            ref[z, x, :, i * LANES : (i + 1) * LANES] = parts[i]

    def edge_tile(z, x, which):
        line = z * nx + x
        above = hy[3 + which].astype(F32) * (has_x[which] * has_y[1])
        below = hy[which].astype(F32) * (has_x[which] * has_y[0])
        above = pltpu.roll(above, lax.rem(LANES - 2 * line + LANES, LANES), 1)
        below = pltpu.roll(below, lax.rem(2 * LANES - 2 - 2 * line, LANES), 1)
        value = jnp.where(tile_lane < 2, above, 0.0)
        return jnp.where(tile_lane >= LANES - 2, below, value)

    def inner_tiles(z, x, value):
        inverse = tiles(dd, z, x)
        parts = split(value)
        store(f1, z, x + 2, [parts[i] * inverse[i] for i in range(2)])

    def edge_tiles(z, x, edge):
        f1[z, x + 2, :, 2 * LANES :] = edge * tiles(dd, z, x)[2]

    def forward_inner(x, carry):
        for z in range(nz):
            inner_tiles(z, x, pt[z, x].astype(F32))
        return carry

    lax.fori_loop(0, nx, forward_inner, 0)
    for copy in probe_copies:
        copy.wait_recv()

    def forward_edges(x, carry):
        for z in range(nz):
            edge_tiles(z, x, edge_tile(z, x, 1))
        return carry

    lax.fori_loop(0, nx, forward_edges, 0)
    for z in range(nz):
        for i in range(2):
            inner_tiles(z, i - 2, xh[0, z, i].astype(F32) * has_west)
            edge_tiles(z, i - 2, edge_tile(z, nx - 2 + i, 0))
            inner_tiles(z, nx + i, xh[1, z, i].astype(F32) * has_east)
            edge_tiles(z, nx + i, edge_tile(z, i, 2))

    def near(ref, z, x, row, count):
        centre = split(ref[z, row])
        ahead = [pltpu.roll(part, LANES - 1, 1) for part in centre]
        behind = [pltpu.roll(part, 1, 1) for part in centre]
        east, west = split(ref[z, row + 1]), split(ref[z, row - 1])
        face_e, face_w = tiles(fx, z, x), tiles(fx, z, x - 1)
        face_n, face_s = tiles(fyp, z, x), tiles(fym, z, x)
        if z + 1 < nz:
            upper, face_u = split(ref[z + 1, row]), tiles(fz, z, x)
        if z > 0:
            lower, face_d = split(ref[z - 1, row]), tiles(fz, z - 1, x)
        sums = []
        for i in range(count):
            north = jnp.where(tile_lane == LANES - 1, ahead[(i + 1) % 3], ahead[i])
            south = jnp.where(tile_lane == 0, behind[(i + 2) % 3], behind[i])
            total = face_e[i] * east[i] + face_w[i] * west[i]
            total = total + (face_n[i] * north + face_s[i] * south)
            if z + 1 < nz:
                total = total + face_u[i] * upper[i]
            if z > 0:
                total = total + face_d[i] * lower[i]
            sums.append(total)
        return centre, sums

    def adjoint(i, carry):
        x = i - 1
        for z in range(nz):
            centre, sums = near(f1, z, x, x + 2, 3)
            diagonal, inverse, gain = tiles(dg, z, x), tiles(dd, z, x), tiles(wd, z, x)
            parts = [
                (centre[i] * diagonal[i] + sums[i]) * gain[i] * inverse[i] for i in range(3)
            ]
            store(a1, z, x + 1, parts)
        return carry

    lax.fori_loop(0, nx + 2, adjoint, 0)

    acc[...] = jnp.zeros_like(acc)

    def finish(x, carry):
        whole_high, whole_low = [], []
        for z in range(nz):
            centre, sums = near(a1, z, x, x + 1, 2)
            diagonal, inverse = tiles(dg, z, x), tiles(dd, z, x)
            source = split(pt[z, x].astype(F32))
            sketch = jnp.concatenate(
                [
                    (centre[i] * diagonal[i] + sums[i]) * inverse[i] + source[i]
                    for i in range(2)
                ],
                axis=1,
            )
            high = sketch.astype(BF16)
            low = (sketch - high.astype(F32)).astype(BF16)
            shl[z * nx + x, 0:k, :] = high
            shl[z * nx + x, k : 2 * k, :] = low
            whole_high.append(high)
            whole_low.append(low)
        applied = lax.dot_general(
            jnp.concatenate(whole_high, axis=0), wt[...], NT, preferred_element_type=F32
        )
        rows = []
        for z in range(nz):
            part = applied[z * k : (z + 1) * k]
            cuf[z * nx + x] = part[:, leaf:]
            rows.append(part[:, :leaf].astype(BF16))
        high = jnp.concatenate(whole_high, axis=1)
        low = jnp.concatenate(whole_low, axis=1)
        lhs = jnp.concatenate([high, low], axis=0)
        rhs = jnp.concatenate([high, low, jnp.concatenate(rows, axis=1)], axis=0)
        acc[...] += lax.dot_general(lhs, rhs, NT, preferred_element_type=F32)
        return carry

    lax.fori_loop(0, nx, finish, 0)

    half_k, half_lanes = k // 2, LANES // 2
    half_lane = lax.broadcasted_iota(jnp.int32, (half_k, LANES), 1)
    pad = jnp.zeros((k, LANES - k), F32)

    def fold(value):
        value = jnp.concatenate([value, pad], axis=1)
        return value[:half_k] + pltpu.roll(value[half_k:], half_lanes, 1)

    def unfold(value):
        first = jnp.where(half_lane < half_lanes, value, 0.0)
        second = pltpu.roll(jnp.where(half_lane < half_lanes, 0.0, value), half_lanes, 1)
        return jnp.concatenate([first, second], axis=0) * (1.0 / cells)

    pending = []

    def send(which, stage, value):
        peers, me = stages[stage]
        packed[which, stage] = value
        gathered[which, stage, me] = value
        copies = [
            remote(
                packed.at[which, stage], gathered.at[which, stage, me],
                sum_send.at[which, stage, d], sum_recv.at[which, stage, d], peer,
            )
            for d, peer in enumerate(peers)
        ]
        pending.extend(copies)
        return copies

    def receive(which, stage, copies):
        for copy in copies:
            copy.wait_recv()
        parts = [gathered[which, stage, i] for i in range(len(copies) + 1)]
        while len(parts) > 1:
            parts = [
                parts[i] + parts[i + 1] if i + 1 < len(parts) else parts[i]
                for i in range(0, len(parts), 2)
            ]
        return parts[0]

    store = pltpu.make_async_copy(shl, shl_out, store_sem.at[0])
    store.start()
    value = acc[...]
    total = value[0:k, 0:k] + (value[0:k, k : 2 * k] + value[k : 2 * k, 0:k]) + value[k:, k : 2 * k]
    first = send(0, 0, fold(total))
    leafpart = value[0:k, 2 * k :] + value[k:, 2 * k :]

    count = LANES // rank
    slot = tile_lane // rank

    def gather(group, carry):
        parts = [cuf[group * count + j] for j in range(count)]
        step = 1
        while step < count:
            bit = (slot // step) % 2 == 0
            for i in range(count):
                if (i // step) % 2 == 0:
                    one, two = parts[i], parts[i + step]
                    parts[i] = jnp.where(bit, one, pltpu.roll(two, step * rank, 1))
                    parts[i + step] = jnp.where(bit, pltpu.roll(one, LANES - step * rank, 1), two)
            step *= 2
        for index in range(2 * levels):
            uc[index, group] = parts[index].astype(BF16)
        return carry

    lax.fori_loop(0, nz * nx // count, gather, 0)

    def flipped(bits):
        device = gy
        for b in range(levels):
            if bits >> b & 1:
                device = device + (1 - 2 * lax.rem(device // 2**b, 2)) * 2**b
        return device

    tree = []
    for level in range(levels):
        half = 2**level
        share = groups // half
        for bits in range(1, 2 * half):
            peer = flipped(bits)
            kind = 2 * level + (1 if bits < half else 0)
            begin = lax.rem(peer, half) * share
            tree.append(
                remote(
                    uc.at[kind, pl.ds(begin, share)], trees[level].at[bits - 1],
                    tree_send.at[2 * half - 2 - level + bits], tree_recv.at[2 * half - 2 - level + bits],
                    (gx, peer),
                )
            )

    first = send(0, 1, receive(0, 0, first))
    for copy in tree:
        copy.wait_recv()
    total = leafpart
    for level in range(levels):
        half = 2**level
        share = groups // half
        begin = lax.rem(gy, half) * share
        for j in range(share):
            own = uc[2 * level + 1, begin + j].astype(F32)
            for bits in range(1, half):
                own = own + trees[level][bits - 1, j].astype(F32)
            other = trees[level][half - 1, j].astype(F32)
            for bits in range(half + 1, 2 * half):
                other = other + trees[level][bits - 1, j].astype(F32)
            total = total + lax.dot_general(
                own.astype(BF16), other.astype(BF16), NT, preferred_element_type=F32
            )
    second = send(1, 0, fold(total))
    first = send(0, 2, receive(0, 1, first))
    second = send(1, 1, receive(1, 0, second))
    matrix = unfold(receive(0, 2, first))

    row = lax.broadcasted_iota(jnp.int32, (k, LANES), 0)
    lane = lax.broadcasted_iota(jnp.int32, (k, LANES), 1)
    start = LANES // 2
    whole = jnp.where(lane < k, matrix, jnp.where(lane == row + start, 1.0, 0.0))
    blocks = [whole[8 * t : 8 * t + 8] for t in range(k // 8)]
    inner = lax.broadcasted_iota(jnp.int32, (8, LANES), 0)
    for j in range(k):
        t, s = divmod(j, 8)
        pivot_row = blocks[t][s : s + 1, :]
        scaled = pivot_row * (1.0 / pivot_row[:, j : j + 1])
        for i in range(t, k // 8):
            factor = blocks[i][:, j : j + 1]
            change = factor * scaled
            if i == t:
                change = jnp.where(inner > s, change, 0.0)
            blocks[i] = blocks[i] - change
        if j == k // 4:
            second = send(1, 2, receive(1, 1, second))
    whole = jnp.concatenate(blocks, axis=0)
    pivots = jnp.sum(jnp.where(lane == row, whole, 0.0), axis=1, keepdims=True)
    inverse = whole[:, start : start + k] / jnp.sqrt(pivots)
    small[0] = inverse
    small[1] = unfold(receive(1, 2, second))[:, 0:k]
    last = pltpu.make_async_copy(small, small_out, store_sem.at[1])
    last.start()
    for copy in field_copies + probe_copies + tree + pending:
        copy.wait_send()
    store.wait()
    last.wait()


def basis_kernel(k, nz, nx, shl_in, small_in, out, projected, shl, small, buffer, load_sem, sem):
    loads = [pltpu.make_async_copy(small_in, small, load_sem.at[nz])]
    for z in range(nz):
        lines = pl.ds(z * nx, nx)
        loads.append(pltpu.make_async_copy(shl_in.at[lines], shl.at[lines], load_sem.at[z]))
    for load in loads:
        load.start()
    loads[0].wait()
    inverse = small[0]
    high = inverse.astype(BF16)
    low = (inverse - high.astype(F32)).astype(BF16)
    lhs = jnp.concatenate(
        [
            jnp.concatenate([high, high], axis=1),
            jnp.concatenate([low, jnp.zeros_like(low)], axis=1),
        ],
        axis=0,
    )
    copies = []
    for z in range(nz):
        loads[z + 1].wait()

        def one(x, carry):
            value = jnp.dot(lhs, shl[z * nx + x], preferred_element_type=F32)
            value = value[0:k] + value[k:]
            buffer[z, 0, pl.ds(x, k, stride=nx), :] = value[:, :LANES]
            buffer[z, 1, pl.ds(x, k, stride=nx), :] = value[:, LANES:]
            return carry

        lax.fori_loop(0, nx, one, 0, unroll=4)
        for i in range(2):
            copy = pltpu.make_async_copy(
                buffer.at[z, i].reshape(k, nx, LANES),
                out.at[:, z, :, i * LANES : (i + 1) * LANES],
                sem.at[z, i],
            )
            copy.start()
            copies.append(copy)
    product = jnp.dot(inverse, small[1], precision=HIGH, preferred_element_type=F32)
    product = lax.dot_general(product, inverse, NT, precision=HIGH, preferred_element_type=F32)
    row = lax.broadcasted_iota(jnp.int32, (k, k), 0)
    lane = lax.broadcasted_iota(jnp.int32, (k, k), 1)
    projected[...] = product + jnp.where(lane == row, 1.0, 0.0)
    for copy in copies:
        copy.wait()


def params(**more):
    return pltpu.CompilerParams(vmem_limit_bytes=56 * 2**20, **more)


def shards(
    probes, classes, class_table, weights, prior_block, prior_left, prior_right, block_ranks
):
    ng, ny = lax.axis_size("gx"), lax.axis_size("gy")
    k, nz, nx, leaf = probes.shape
    levels = ny.bit_length() - 1
    rank = prior_left.shape[1]
    lines = nz * nx
    groups = lines * rank // LANES
    cells = float(nz * nx * leaf * ng * ny)
    shape = jax.ShapeDtypeStruct
    dma = pltpu.SemaphoreType.DMA
    vmem = pltpu.VMEM
    edges = 2 * ny
    most = 8
    while most < max(ng // min(4, ng), ny // min(2, ny)):
        most *= 2

    field = vmem((nz, nx + 16, 3 * LANES), F32)
    shl, small = pl.pallas_call(
        functools.partial(
            sketch_kernel, ng, ny, k, nz, nx, levels, leaf, groups, cells
        ),
        out_shape=(
            shape((lines, 2 * k, leaf), BF16),
            shape((2, k, k), F32),
        ),
        in_specs=[HBM] * 8,
        out_specs=(HBM,) * 2,
        scratch_shapes=[
            vmem((lines, 2 * k, leaf), BF16),
            vmem((2, k, k), F32),
            dma((2,)),
            vmem((k * lines, leaf), BF16),
            vmem(classes.shape, classes.dtype),
            pltpu.SMEM(class_table.shape, F32),
            vmem(weights.shape, F32),
            vmem(prior_block.shape, F32),
            vmem((levels, rank, leaf), F32),
            vmem((levels, rank, leaf), F32),
            pltpu.SMEM(block_ranks.shape, block_ranks.dtype),
            dma((8,)),
            vmem((nz, nx, k, leaf), BF16),
            vmem((nz, nx, leaf), F32),
            vmem((2, k * lines, LANES), F32),
            vmem((2, nz, 2, k, leaf), BF16),
            vmem((6, k, LANES), BF16),
            vmem((2, 4 * nz, leaf), F32),
            vmem((6, nx, LANES), F32),
            vmem((2, k, LANES), BF16),
            vmem((2, 4 * nz, leaf), F32),
            vmem((2, nx, LANES), F32),
            dma((16,)),
            dma((16,)),
        ]
        + [field] * 8
        + [
            vmem((nz, nx + 4, k, 3 * LANES), F32),
            vmem((nz, nx + 2, k, 3 * LANES), F32),
            vmem((leaf + LANES, leaf), BF16),
            vmem((2 * k, 3 * k), F32),
            vmem((lines, k, LANES), F32),
            vmem((2 * levels, groups, k, LANES), BF16),
            [
                vmem((2 ** (level + 1) - 1, groups >> level, k, LANES), BF16)
                for level in range(levels)
            ],
            dma((edges,)),
            dma((edges,)),
            vmem((2, 3, k // 2, LANES), F32),
            vmem((2, 3, most, k // 2, LANES), F32),
            dma((2, 3, most)),
            dma((2, 3, most)),
        ],
        compiler_params=params(collective_id=0, has_side_effects=True),
    )(
        probes.reshape(k * lines, leaf), classes, class_table, weights, prior_block, prior_left,
        prior_right, block_ranks,
    )

    basis, projected = pl.pallas_call(
        functools.partial(basis_kernel, k, nz, nx),
        out_shape=(shape((k, nz, nx, leaf), F32), shape((k, k), F32)),
        in_specs=[HBM] * 2,
        out_specs=(HBM, VMEM),
        scratch_shapes=[
            vmem((lines, 2 * k, leaf), BF16),
            vmem((2, k, k), F32),
            vmem((nz, 2, k * nx, LANES), F32),
            dma((nz + 1,)),
            dma((nz, 2)),
        ],
        compiler_params=params(),
    )(shl, small)
    return basis, projected


def solution(mesh):
    return jax.shard_map(
        shards,
        mesh=mesh,
        in_specs=(
            P(None, None, "gx", "gy"),
            P(None, "gx", "gy"),
            P(),
            P(None, "gx", "gy"),
            P("gy", None),
            P(None, None, "gy"),
            P(None, None, "gy"),
            P(),
        ),
        out_specs=(P(None, None, "gx", "gy"), P()),
        check_vma=False,
    )
```

```python
import functools

import jax
import jax.numpy as jnp
from jax import lax
from jax.experimental import pallas as pl
from jax.experimental.pallas import tpu as pltpu
from jax.sharding import PartitionSpec as P

MESH = pl.DeviceIdType.MESH
HIGH = lax.Precision.HIGHEST
F32 = jnp.float32
BF16 = jnp.bfloat16
LANES = 128
VMEM = pl.BlockSpec(memory_space=pltpu.VMEM)
SMEM = pl.BlockSpec(memory_space=pltpu.SMEM)
ANY = pl.BlockSpec(memory_space=pl.ANY)
HBM = pl.BlockSpec(memory_space=pltpu.HBM)
NT = (((1,), (1,)), ((), ()))


def signal_all(devices):
    barrier = pltpu.get_barrier_semaphore()
    for device in devices:
        pl.semaphore_signal(barrier, inc=1, device_id=device, device_id_type=MESH)
    return barrier, len(devices)


def remote(src, dst, send, recv, device):
    copy = pltpu.make_async_remote_copy(
        src_ref=src, dst_ref=dst, send_sem=send, recv_sem=recv, device_id=device, device_id_type=MESH
    )
    copy.start()
    return copy


def sketch_kernel(
    ng, ny, k, nz, nx, levels, leaf, groups, cells,
    probes_in, classes_in, table_in, weights_in, block_in, left_in, right_in, ranks_in,
    out, projected,
    shl, buffer, store_sem, probes, classes, table, weights, block, left, right, ranks, load_sem,
    pt, cond, pf, xh, hy, cx, cy, hs, cxs, cys, send_sem, recv_sem,
    ce, dg, dd, wd, fx, fyp, fym, fz, f1, a1, wt, acc, cuf, uc,
    trees, tree_send, tree_recv, packed, gathered, sum_send, sum_recv,
):
    gx, gy = lax.axis_index("gx"), lax.axis_index("gy")
    east, west = lax.rem(gx + 1, ng), lax.rem(gx + ng - 1, ng)
    north, south = lax.rem(gy + 1, ny), lax.rem(gy + ny - 1, ny)
    around = [(west, gy), (east, gy)]
    for column in (south, north):
        for row in (west, gx, east):
            around.append((row, column))

    across, pair = min(4, ng), min(2, ny)
    deep, high_y = ng // across, ny // pair
    at_z, at_x = gx // across, lax.rem(gx, across)
    at_y, at_c = gy // pair, lax.rem(gy, pair)
    stages = [
        (
            [
                (
                    at_z * across + lax.rem(at_x + d % across, across),
                    at_y * pair + lax.rem(at_c + d // across, pair),
                )
                for d in range(1, across * pair)
            ],
            at_c * across + at_x,
        ),
        ([(lax.rem(at_z + d, deep) * across + at_x, gy) for d in range(1, deep)], at_z),
        ([(gx, lax.rem(at_y + d, high_y) * pair + at_c) for d in range(1, high_y)], at_y),
    ]
    column = [(gx, lax.rem(gy + d, ny)) for d in range(1, ny)]
    barrier, count = signal_all(around + stages[0][0] + stages[1][0] + column)

    loads = [
        pltpu.make_async_copy(source, target, load_sem.at[i])
        for i, (source, target) in enumerate(
            [
                (classes_in, classes),
                (weights_in, weights),
                (table_in, table),
                (probes_in, probes),
                (block_in, block),
                (left_in.at[0:levels], left),
                (right_in.at[0:levels], right),
                (ranks_in, ranks),
            ]
        )
    ]
    for load in loads:
        load.start()

    lines = nz * nx
    for load in loads[:3]:
        load.wait()

    for z in range(nz):
        picked = classes[z]
        value = jnp.zeros(picked.shape, F32)
        for index in range(table.shape[0]):
            value = jnp.where(picked == index, table[index], value)
        cond[z] = value
        cxs[0, 4 * z : 4 * z + 3, :] = value[0:3, :]
        cxs[1, 4 * z : 4 * z + 3, :] = value[nx - 3 : nx, :]
        cxs[0, 4 * z + 3 : 4 * z + 4, :] = weights[z, 0:1, :]
        cxs[1, 4 * z + 3 : 4 * z + 4, :] = weights[z, nx - 1 : nx, :]
    lane = lax.broadcasted_iota(jnp.int32, (nx, LANES), 1)
    low = jnp.zeros((nx, LANES), F32)
    high = jnp.zeros((nx, LANES), F32)
    for z in range(nz):
        here = lane // 4 == z
        last = lane % 4 == 3
        first_tile, last_tile = cond[z, :, :LANES], cond[z, :, LANES:]
        w_first, w_last = weights[z, :, :LANES], weights[z, :, LANES:]
        own = jnp.where(last, pltpu.roll(w_first, 4 * z + 3, 1), pltpu.roll(first_tile, 4 * z, 1))
        low = jnp.where(here, own, low)
        own = jnp.where(last, pltpu.roll(w_last, 4 * z + 4, 1), pltpu.roll(last_tile, 4 * z + 3, 1))
        high = jnp.where(here, own, high)
    cys[0] = low
    cys[1] = high

    loads[3].wait()
    chunk = 512

    def widen(i, carry):
        rows = pl.ds(pl.multiple_of(i * chunk, chunk), chunk)
        value = probes[rows, :].astype(F32)
        pf[0, rows, :] = value[:, :LANES]
        pf[1, rows, :] = value[:, LANES:]
        return carry

    lax.fori_loop(0, k * lines // chunk, widen, 0)

    place = lax.broadcasted_iota(jnp.int32, (k, LANES), 1) // 2

    def turn(line, carry):
        low, high = carry
        lo = pf[0, pl.ds(line, k, stride=lines), :]
        hi = pf[1, pl.ds(line, k, stride=lines), :]
        pt[line // nx, lax.rem(line, nx)] = jnp.concatenate([lo, hi], axis=1).astype(BF16)
        low = jnp.where(place == line, pltpu.roll(lo, 2 * line, 1), low)
        high = jnp.where(place == line, pltpu.roll(hi, lax.rem(2 * line + 2, LANES), 1), high)
        return low, high

    zero = jnp.zeros((k, LANES), F32)
    low, high = lax.fori_loop(0, lines, turn, (zero, zero), unroll=4)
    hs[0] = low.astype(BF16)
    hs[1] = high.astype(BF16)

    pl.semaphore_wait(barrier, count)
    field_copies = [
        remote(cxs.at[1], cx.at[0], send_sem.at[2], recv_sem.at[2], (east, gy)),
        remote(cxs.at[0], cx.at[1], send_sem.at[3], recv_sem.at[3], (west, gy)),
    ]
    probe_copies = []
    used = 4
    arrivals = [
        (side, which, row, column)
        for side, column in ((0, north), (1, south))
        for which, row in ((2, west), (1, gx), (0, east))
    ]
    for i, (side, which, row, column) in enumerate(arrivals):
        slot = side * 3 + which
        field_copies.append(
            remote(
                cys.at[1 - side], cy.at[slot], send_sem.at[4 + i], recv_sem.at[4 + i], (row, column)
            )
        )
    for i, (side, which, row, column) in enumerate(arrivals):
        slot = side * 3 + which
        probe_copies.append(
            remote(
                hs.at[1 - side], hy.at[slot], send_sem.at[10 + i], recv_sem.at[10 + i], (row, column)
            )
        )
    probe_copies += [
        remote(pt.at[:, nx - 2 : nx], xh.at[0], send_sem.at[0], recv_sem.at[0], (east, gy)),
        remote(pt.at[:, 0:2], xh.at[1], send_sem.at[1], recv_sem.at[1], (west, gy)),
    ]

    has_west = (gx > 0).astype(F32)
    has_east = (gx < ng - 1).astype(F32)
    has_south = (gy > 0).astype(F32)
    has_north = (gy < ny - 1).astype(F32)
    has_x = (has_west, 1.0, has_east)
    has_y = (has_south, has_north)
    rank = left.shape[1]
    for load in loads[4:]:
        load.wait()

    wt[0:leaf, :] = block[...].astype(BF16)
    row = lax.broadcasted_iota(jnp.int32, (rank, leaf), 0)
    for level in range(levels):
        gain = jnp.where(row < ranks[level], float(leaf * 2**level) ** -0.5, 0.0)
        at = leaf + 2 * level * rank
        wt[at : at + rank, :] = (right[level] * gain).astype(BF16)
        wt[at + rank : at + 2 * rank, :] = left[level].astype(BF16)

    for copy in field_copies:
        copy.wait_recv()

    tall = nx + 16
    wide = 3 * LANES
    lane = lax.broadcasted_iota(jnp.int32, (nx, LANES), 1)
    for z in range(nz):
        ce[z] = jnp.zeros((tall, wide), F32)
        wd[z] = jnp.zeros((tall, wide), F32)
        ce[z, 8 : 8 + nx, 0 : 2 * LANES] = cond[z]
        wd[z, 8 : 8 + nx, 0 : 2 * LANES] = weights[z]
        ce[z, 5:8, 0 : 2 * LANES] = cx[0, 4 * z : 4 * z + 3, :] * has_west
        wd[z, 7:8, 0 : 2 * LANES] = cx[0, 4 * z + 3 : 4 * z + 4, :] * has_west
        ce[z, 8 + nx : 11 + nx, 0 : 2 * LANES] = cx[1, 4 * z : 4 * z + 3, :] * has_east
        wd[z, 8 + nx : 9 + nx, 0 : 2 * LANES] = cx[1, 4 * z + 3 : 4 * z + 4, :] * has_east
        for which in range(3):
            above = cy[3 + which] * (has_x[which] * has_y[1])
            below = cy[which] * (has_x[which] * has_y[0])
            value = jnp.where(lane < 3, pltpu.roll(above, (LANES - 4 * z) % LANES, 1), 0.0)
            value = jnp.where(lane > LANES - 4, pltpu.roll(below, LANES - 3 - 4 * z, 1), value)
            if which == 0:
                ce[z, 0:8, 2 * LANES :] = value[nx - 8 :, :]
            elif which == 2:
                ce[z, 8 + nx :, 2 * LANES :] = value[:8, :]
            else:
                ce[z, 8 : 8 + nx, 2 * LANES :] = value
                value = jnp.where(lane == 0, pltpu.roll(above, LANES - 3 - 4 * z, 1), 0.0)
                value = jnp.where(lane == LANES - 1, pltpu.roll(below, LANES - 4 - 4 * z, 1), value)
                wd[z, 8 : 8 + nx, 2 * LANES :] = value
    for z in range(nz):
        centre = ce[z]
        upper = ce[z + 1] if z + 1 < nz else jnp.zeros_like(centre)
        lower = ce[z - 1] if z > 0 else jnp.zeros_like(centre)
        face_x = 0.5 * (centre + pltpu.roll(centre, tall - 1, 0))
        face_y = 0.5 * (centre + pltpu.roll(centre, wide - 1, 1))
        back_y = pltpu.roll(face_y, 1, 1)
        face_z = 0.5 * (centre + upper)
        total = 1.0 + face_x + pltpu.roll(face_x, 1, 0) + face_y + back_y
        total = total + face_z + 0.5 * (centre + lower)
        inverse = 1.0 / total
        fx[z] = face_x
        fyp[z] = face_y
        fym[z] = back_y
        fz[z] = face_z
        dg[z] = total
        dd[z] = inverse
        wd[z] = wd[z] * inverse

    tile_lane = lax.broadcasted_iota(jnp.int32, (k, LANES), 1)

    def tiles(ref, z, x):
        whole = ref[z, pl.ds(x + 8, 1), :]
        return [whole[:, i * LANES : (i + 1) * LANES] for i in range(3)]

    def split(value):
        return [value[:, i * LANES : (i + 1) * LANES] for i in range(value.shape[1] // LANES)]

    def store(ref, z, x, parts):
        for i in range(len(parts)):
            ref[z, x, :, i * LANES : (i + 1) * LANES] = parts[i]

    def edge_tile(z, x, which):
        line = z * nx + x
        above = hy[3 + which].astype(F32) * (has_x[which] * has_y[1])
        below = hy[which].astype(F32) * (has_x[which] * has_y[0])
        above = pltpu.roll(above, lax.rem(LANES - 2 * line + LANES, LANES), 1)
        below = pltpu.roll(below, lax.rem(2 * LANES - 2 - 2 * line, LANES), 1)
        value = jnp.where(tile_lane < 2, above, 0.0)
        return jnp.where(tile_lane >= LANES - 2, below, value)

    def inner_tiles(z, x, value):
        inverse = tiles(dd, z, x)
        parts = split(value)
        store(f1, z, x + 2, [parts[i] * inverse[i] for i in range(2)])

    def edge_tiles(z, x, edge):
        f1[z, x + 2, :, 2 * LANES :] = edge * tiles(dd, z, x)[2]

    def forward_inner(x, carry):
        for z in range(nz):
            inner_tiles(z, x, pt[z, x].astype(F32))
        return carry

    lax.fori_loop(0, nx, forward_inner, 0)
    for copy in probe_copies[:6]:
        copy.wait_recv()

    def forward_edges(x, carry):
        for z in range(nz):
            edge_tiles(z, x, edge_tile(z, x, 1))
        return carry

    lax.fori_loop(0, nx, forward_edges, 0)
    def near(ref, z, x, row, count):
        centre = split(ref[z, row])
        ahead = [pltpu.roll(part, LANES - 1, 1) for part in centre]
        behind = [pltpu.roll(part, 1, 1) for part in centre]
        east, west = split(ref[z, row + 1]), split(ref[z, row - 1])
        face_e, face_w = tiles(fx, z, x), tiles(fx, z, x - 1)
        face_n, face_s = tiles(fyp, z, x), tiles(fym, z, x)
        if z + 1 < nz:
            upper, face_u = split(ref[z + 1, row]), tiles(fz, z, x)
        if z > 0:
            lower, face_d = split(ref[z - 1, row]), tiles(fz, z - 1, x)
        sums = []
        for i in range(count):
            north = jnp.where(tile_lane == LANES - 1, ahead[(i + 1) % 3], ahead[i])
            south = jnp.where(tile_lane == 0, behind[(i + 2) % 3], behind[i])
            total = face_e[i] * east[i] + face_w[i] * west[i]
            total = total + (face_n[i] * north + face_s[i] * south)
            if z + 1 < nz:
                total = total + face_u[i] * upper[i]
            if z > 0:
                total = total + face_d[i] * lower[i]
            sums.append(total)
        return centre, sums

    def adjoint(i, carry):
        x = i - 1
        for z in range(nz):
            centre, sums = near(f1, z, x, x + 2, 3)
            diagonal, inverse, gain = tiles(dg, z, x), tiles(dd, z, x), tiles(wd, z, x)
            parts = [
                (centre[i] * diagonal[i] + sums[i]) * gain[i] * inverse[i] for i in range(3)
            ]
            store(a1, z, x + 1, parts)
        return carry

    acc[...] = jnp.zeros_like(acc)

    def finish(x, carry):
        whole_high, whole_low = [], []
        for z in range(nz):
            centre, sums = near(a1, z, x, x + 1, 2)
            diagonal, inverse = tiles(dg, z, x), tiles(dd, z, x)
            source = split(pt[z, x].astype(F32))
            sketch = jnp.concatenate(
                [
                    (centre[i] * diagonal[i] + sums[i]) * inverse[i] + source[i]
                    for i in range(2)
                ],
                axis=1,
            )
            high = sketch.astype(BF16)
            low = (sketch - high.astype(F32)).astype(BF16)
            shl[z * nx + x, 0:k, :] = high
            shl[z * nx + x, k : 2 * k, :] = low
            whole_high.append(high)
            whole_low.append(low)
        applied = lax.dot_general(
            jnp.concatenate(whole_high, axis=0), wt[...], NT, preferred_element_type=F32
        )
        rows = []
        for z in range(nz):
            part = applied[z * k : (z + 1) * k]
            cuf[z * nx + x] = part[:, leaf:]
            rows.append(part[:, :leaf].astype(BF16))
        high = jnp.concatenate(whole_high, axis=1)
        low = jnp.concatenate(whole_low, axis=1)
        lhs = jnp.concatenate([high, low], axis=0)
        rhs = jnp.concatenate([high, low, jnp.concatenate(rows, axis=1)], axis=0)
        acc[...] += lax.dot_general(lhs, rhs, NT, preferred_element_type=F32)
        return carry

    lax.fori_loop(2, nx, adjoint, 0)
    lax.fori_loop(2, nx - 2, finish, 0)
    for copy in probe_copies[6:]:
        copy.wait_recv()
    for z in range(nz):
        for i in range(2):
            inner_tiles(z, i - 2, xh[0, z, i].astype(F32) * has_west)
            edge_tiles(z, i - 2, edge_tile(z, nx - 2 + i, 0))
            inner_tiles(z, nx + i, xh[1, z, i].astype(F32) * has_east)
            edge_tiles(z, nx + i, edge_tile(z, i, 2))

    def adjoint_outer(i, carry):
        return adjoint(jnp.where(i < 2, i, nx - 2 + i), carry)

    def finish_outer(i, carry):
        return finish(jnp.where(i < 2, i, nx - 4 + i), carry)

    lax.fori_loop(0, 4, adjoint_outer, 0)
    lax.fori_loop(0, 4, finish_outer, 0)

    half_k, half_lanes = k // 2, LANES // 2
    half_lane = lax.broadcasted_iota(jnp.int32, (half_k, LANES), 1)
    pad = jnp.zeros((k, LANES - k), F32)

    def fold(value):
        value = jnp.concatenate([value, pad], axis=1)
        return value[:half_k] + pltpu.roll(value[half_k:], half_lanes, 1)

    def unfold(value):
        first = jnp.where(half_lane < half_lanes, value, 0.0)
        second = pltpu.roll(jnp.where(half_lane < half_lanes, 0.0, value), half_lanes, 1)
        return jnp.concatenate([first, second], axis=0) * (1.0 / cells)

    pending = []

    def send(which, stage, value):
        peers, me = stages[stage]
        packed[which, stage] = value
        gathered[which, stage, me] = value
        copies = [
            remote(
                packed.at[which, stage], gathered.at[which, stage, me],
                sum_send.at[which, stage, d], sum_recv.at[which, stage, d], peer,
            )
            for d, peer in enumerate(peers)
        ]
        pending.extend(copies)
        return copies

    def receive(which, stage, copies):
        for copy in copies:
            copy.wait_recv()
        parts = [gathered[which, stage, i] for i in range(len(copies) + 1)]
        while len(parts) > 1:
            parts = [
                parts[i] + parts[i + 1] if i + 1 < len(parts) else parts[i]
                for i in range(0, len(parts), 2)
            ]
        return parts[0]

    value = acc[...]
    total = value[0:k, 0:k] + (value[0:k, k : 2 * k] + value[k : 2 * k, 0:k]) + value[k:, k : 2 * k]
    first = send(0, 0, fold(total))
    leafpart = value[0:k, 2 * k :] + value[k:, 2 * k :]

    count = LANES // rank
    slot = tile_lane // rank

    def gather(group, carry):
        parts = [cuf[group * count + j] for j in range(count)]
        step = 1
        while step < count:
            bit = (slot // step) % 2 == 0
            for i in range(count):
                if (i // step) % 2 == 0:
                    one, two = parts[i], parts[i + step]
                    parts[i] = jnp.where(bit, one, pltpu.roll(two, step * rank, 1))
                    parts[i + step] = jnp.where(bit, pltpu.roll(one, LANES - step * rank, 1), two)
            step *= 2
        for index in range(2 * levels):
            uc[index, group] = parts[index].astype(BF16)
        return carry

    lax.fori_loop(0, nz * nx // count, gather, 0)

    def flipped(bits):
        device = gy
        for b in range(levels):
            if bits >> b & 1:
                device = device + (1 - 2 * lax.rem(device // 2**b, 2)) * 2**b
        return device

    tree = []
    for level in range(levels):
        half = 2**level
        share = groups // half
        for bits in range(1, 2 * half):
            peer = flipped(bits)
            kind = 2 * level + (1 if bits < half else 0)
            begin = lax.rem(peer, half) * share
            tree.append(
                remote(
                    uc.at[kind, pl.ds(begin, share)], trees[level].at[bits - 1],
                    tree_send.at[2 * half - 2 - level + bits], tree_recv.at[2 * half - 2 - level + bits],
                    (gx, peer),
                )
            )

    first = send(0, 1, receive(0, 0, first))
    first = send(0, 2, receive(0, 1, first))
    for copy in tree:
        copy.wait_recv()
    total = leafpart
    for level in range(levels):
        half = 2**level
        share = groups // half
        begin = lax.rem(gy, half) * share
        for j in range(share):
            own = uc[2 * level + 1, begin + j].astype(F32)
            for bits in range(1, half):
                own = own + trees[level][bits - 1, j].astype(F32)
            other = trees[level][half - 1, j].astype(F32)
            for bits in range(half + 1, 2 * half):
                other = other + trees[level][bits - 1, j].astype(F32)
            total = total + lax.dot_general(
                own.astype(BF16), other.astype(BF16), NT, preferred_element_type=F32
            )
    second = send(1, 0, fold(total))
    matrix = unfold(receive(0, 2, first))

    row = lax.broadcasted_iota(jnp.int32, (k, LANES), 0)
    lane = lax.broadcasted_iota(jnp.int32, (k, LANES), 1)
    start = LANES // 2
    whole = jnp.where(lane < k, matrix, jnp.where(lane == row + start, 1.0, 0.0))
    blocks = [whole[8 * t : 8 * t + 8] for t in range(k // 8)]
    inner = lax.broadcasted_iota(jnp.int32, (8, LANES), 0)
    for j in range(k):
        t, s = divmod(j, 8)
        pivot_row = blocks[t][s : s + 1, :]
        scaled = pivot_row * (1.0 / pivot_row[:, j : j + 1])
        for i in range(t, k // 8):
            factor = blocks[i][:, j : j + 1]
            change = factor * scaled
            if i == t:
                change = jnp.where(inner > s, change, 0.0)
            blocks[i] = blocks[i] - change
        if j == k // 2:
            second = send(1, 1, receive(1, 0, second))
    whole = jnp.concatenate(blocks, axis=0)
    pivots = jnp.sum(jnp.where(lane == row, whole, 0.0), axis=1, keepdims=True)
    inverse = whole[:, start : start + k] / jnp.sqrt(pivots)

    high = inverse.astype(BF16)
    low = (inverse - high.astype(F32)).astype(BF16)
    lhs = jnp.concatenate(
        [
            jnp.concatenate([high, high], axis=1),
            jnp.concatenate([low, jnp.zeros_like(low)], axis=1),
        ],
        axis=0,
    )
    stores = []
    for z in range(nz):

        def one(x, carry):
            value = jnp.dot(lhs, shl[z * nx + x], preferred_element_type=F32)
            value = value[0:k] + value[k:]
            buffer[z, 0, pl.ds(x, k, stride=nx), :] = value[:, :LANES]
            buffer[z, 1, pl.ds(x, k, stride=nx), :] = value[:, LANES:]
            return carry

        lax.fori_loop(0, nx, one, 0, unroll=4)
        for i in range(2):
            copy = pltpu.make_async_copy(
                buffer.at[z, i].reshape(k, nx, LANES),
                out.at[:, z, :, i * LANES : (i + 1) * LANES],
                store_sem.at[z, i],
            )
            copy.start()
            stores.append(copy)
        if z == nz // 2:
            second = send(1, 2, receive(1, 1, second))
    middle = unfold(receive(1, 2, second))[:, 0:k]
    product = jnp.dot(inverse, middle, precision=HIGH, preferred_element_type=F32)
    product = lax.dot_general(product, inverse, NT, precision=HIGH, preferred_element_type=F32)
    projected[...] = product + jnp.where(lane[:, 0:k] == row[:, 0:k], 1.0, 0.0)
    for copy in field_copies + probe_copies + tree + pending:
        copy.wait_send()
    for copy in stores:
        copy.wait()


def params(**more):
    return pltpu.CompilerParams(vmem_limit_bytes=56 * 2**20, **more)


def shards(
    probes, classes, class_table, weights, prior_block, prior_left, prior_right, block_ranks
):
    ng, ny = lax.axis_size("gx"), lax.axis_size("gy")
    k, nz, nx, leaf = probes.shape
    levels = ny.bit_length() - 1
    rank = prior_left.shape[1]
    lines = nz * nx
    groups = lines * rank // LANES
    cells = float(nz * nx * leaf * ng * ny)
    shape = jax.ShapeDtypeStruct
    dma = pltpu.SemaphoreType.DMA
    vmem = pltpu.VMEM
    edges = 2 * ny
    most = 8
    while most < max(ng // min(4, ng), ny // min(2, ny)):
        most *= 2

    field = vmem((nz, nx + 16, 3 * LANES), F32)
    basis, projected = pl.pallas_call(
        functools.partial(
            sketch_kernel, ng, ny, k, nz, nx, levels, leaf, groups, cells
        ),
        out_shape=(
            shape((k, nz, nx, leaf), F32),
            shape((k, k), F32),
        ),
        in_specs=[HBM] * 8,
        out_specs=(HBM, VMEM),
        scratch_shapes=[
            vmem((lines, 2 * k, leaf), BF16),
            vmem((nz, 2, k * nx, LANES), F32),
            dma((nz, 2)),
            vmem((k * lines, leaf), BF16),
            vmem(classes.shape, classes.dtype),
            pltpu.SMEM(class_table.shape, F32),
            vmem(weights.shape, F32),
            vmem(prior_block.shape, F32),
            vmem((levels, rank, leaf), F32),
            vmem((levels, rank, leaf), F32),
            pltpu.SMEM(block_ranks.shape, block_ranks.dtype),
            dma((8,)),
            vmem((nz, nx, k, leaf), BF16),
            vmem((nz, nx, leaf), F32),
            vmem((2, k * lines, LANES), F32),
            vmem((2, nz, 2, k, leaf), BF16),
            vmem((6, k, LANES), BF16),
            vmem((2, 4 * nz, leaf), F32),
            vmem((6, nx, LANES), F32),
            vmem((2, k, LANES), BF16),
            vmem((2, 4 * nz, leaf), F32),
            vmem((2, nx, LANES), F32),
            dma((16,)),
            dma((16,)),
        ]
        + [field] * 8
        + [
            vmem((nz, nx + 4, k, 3 * LANES), F32),
            vmem((nz, nx + 2, k, 3 * LANES), F32),
            vmem((leaf + LANES, leaf), BF16),
            vmem((2 * k, 3 * k), F32),
            vmem((lines, k, LANES), F32),
            vmem((2 * levels, groups, k, LANES), BF16),
            [
                vmem((2 ** (level + 1) - 1, groups >> level, k, LANES), BF16)
                for level in range(levels)
            ],
            dma((edges,)),
            dma((edges,)),
            vmem((2, 3, k // 2, LANES), F32),
            vmem((2, 3, most, k // 2, LANES), F32),
            dma((2, 3, most)),
            dma((2, 3, most)),
        ],
        compiler_params=params(collective_id=0, has_side_effects=True),
    )(
        probes.reshape(k * lines, leaf), classes, class_table, weights, prior_block, prior_left,
        prior_right, block_ranks,
    )
    return basis, projected


def solution(mesh):
    return jax.shard_map(
        shards,
        mesh=mesh,
        in_specs=(
            P(None, None, "gx", "gy"),
            P(None, "gx", "gy"),
            P(),
            P(None, "gx", "gy"),
            P("gy", None),
            P(None, None, "gy"),
            P(None, None, "gy"),
            P(),
        ),
        out_specs=(P(None, None, "gx", "gy"), P()),
        check_vma=False,
    )
```

```python
import functools

import jax
import jax.numpy as jnp
from jax import lax
from jax.experimental import pallas as pl
from jax.experimental.pallas import tpu as pltpu
from jax.sharding import PartitionSpec as P

MESH = pl.DeviceIdType.MESH
HIGH = lax.Precision.HIGHEST
F32 = jnp.float32
BF16 = jnp.bfloat16
LANES = 128
VMEM = pl.BlockSpec(memory_space=pltpu.VMEM)
SMEM = pl.BlockSpec(memory_space=pltpu.SMEM)
ANY = pl.BlockSpec(memory_space=pl.ANY)
HBM = pl.BlockSpec(memory_space=pltpu.HBM)
NT = (((1,), (1,)), ((), ()))


def signal_all(devices):
    barrier = pltpu.get_barrier_semaphore()
    for device in devices:
        pl.semaphore_signal(barrier, inc=1, device_id=device, device_id_type=MESH)
    return barrier, len(devices)


def remote(src, dst, send, recv, device):
    copy = pltpu.make_async_remote_copy(
        src_ref=src, dst_ref=dst, send_sem=send, recv_sem=recv, device_id=device, device_id_type=MESH
    )
    copy.start()
    return copy


def sketch_kernel(
    ng, ny, k, nz, nx, levels, leaf, groups, cells,
    probes_in, classes_in, table_in, weights_in, block_in, left_in, right_in, ranks_in,
    out, projected,
    shl, buffer, store_sem, probes, classes, table, weights, block, left, right, ranks, load_sem,
    pt, cond, pf, xh, hy, cx, cy, hs, cxs, cys, send_sem, recv_sem,
    ce, dg, dd, wd, fx, fyp, fym, fz, f1, a1, wt, acc, cuf, uc,
    trees, tree_send, tree_recv, packed, gathered, sum_send, sum_recv,
):
    gx, gy = lax.axis_index("gx"), lax.axis_index("gy")
    east, west = lax.rem(gx + 1, ng), lax.rem(gx + ng - 1, ng)
    north, south = lax.rem(gy + 1, ny), lax.rem(gy + ny - 1, ny)
    around = [(west, gy), (east, gy)]
    for column in (south, north):
        for row in (west, gx, east):
            around.append((row, column))

    across, pair = min(4, ng), min(2, ny)
    deep, high_y = ng // across, ny // pair
    at_z, at_x = gx // across, lax.rem(gx, across)
    at_y, at_c = gy // pair, lax.rem(gy, pair)
    stages = [
        (
            [
                (
                    at_z * across + lax.rem(at_x + d % across, across),
                    at_y * pair + lax.rem(at_c + d // across, pair),
                )
                for d in range(1, across * pair)
            ],
            at_c * across + at_x,
        ),
        ([(lax.rem(at_z + d, deep) * across + at_x, gy) for d in range(1, deep)], at_z),
        ([(gx, lax.rem(at_y + d, high_y) * pair + at_c) for d in range(1, high_y)], at_y),
    ]
    column = [(gx, lax.rem(gy + d, ny)) for d in range(1, ny)]
    barrier, count = signal_all(around + stages[0][0] + stages[1][0] + column)

    loads = [
        pltpu.make_async_copy(source, target, load_sem.at[i])
        for i, (source, target) in enumerate(
            [
                (classes_in, classes),
                (weights_in, weights),
                (table_in, table),
                (probes_in, probes),
                (block_in, block),
                (left_in.at[0:levels], left),
                (right_in.at[0:levels], right),
                (ranks_in, ranks),
            ]
        )
    ]
    for load in loads:
        load.start()

    lines = nz * nx
    for load in loads[:3]:
        load.wait()

    for z in range(nz):
        picked = classes[z]
        value = jnp.zeros(picked.shape, F32)
        for index in range(table.shape[0]):
            value = jnp.where(picked == index, table[index], value)
        cond[z] = value
        cxs[0, 4 * z : 4 * z + 3, :] = value[0:3, :]
        cxs[1, 4 * z : 4 * z + 3, :] = value[nx - 3 : nx, :]
        cxs[0, 4 * z + 3 : 4 * z + 4, :] = weights[z, 0:1, :]
        cxs[1, 4 * z + 3 : 4 * z + 4, :] = weights[z, nx - 1 : nx, :]
    lane = lax.broadcasted_iota(jnp.int32, (nx, LANES), 1)
    low = jnp.zeros((nx, LANES), F32)
    high = jnp.zeros((nx, LANES), F32)
    for z in range(nz):
        here = lane // 4 == z
        last = lane % 4 == 3
        first_tile, last_tile = cond[z, :, :LANES], cond[z, :, LANES:]
        w_first, w_last = weights[z, :, :LANES], weights[z, :, LANES:]
        own = jnp.where(last, pltpu.roll(w_first, 4 * z + 3, 1), pltpu.roll(first_tile, 4 * z, 1))
        low = jnp.where(here, own, low)
        own = jnp.where(last, pltpu.roll(w_last, 4 * z + 4, 1), pltpu.roll(last_tile, 4 * z + 3, 1))
        high = jnp.where(here, own, high)
    cys[0] = low
    cys[1] = high

    loads[3].wait()
    chunk = 512

    def widen(i, carry):
        rows = pl.ds(pl.multiple_of(i * chunk, chunk), chunk)
        value = probes[rows, :].astype(F32)
        pf[0, rows, :] = value[:, :LANES]
        pf[1, rows, :] = value[:, LANES:]
        return carry

    lax.fori_loop(0, k * lines // chunk, widen, 0)

    place = lax.broadcasted_iota(jnp.int32, (k, LANES), 1) // 2

    def turn(line, carry):
        low, high = carry
        lo = pf[0, pl.ds(line, k, stride=lines), :]
        hi = pf[1, pl.ds(line, k, stride=lines), :]
        pt[line // nx, lax.rem(line, nx)] = jnp.concatenate([lo, hi], axis=1).astype(BF16)
        low = jnp.where(place == line, pltpu.roll(lo, 2 * line, 1), low)
        high = jnp.where(place == line, pltpu.roll(hi, lax.rem(2 * line + 2, LANES), 1), high)
        return low, high

    zero = jnp.zeros((k, LANES), F32)
    low, high = lax.fori_loop(0, lines, turn, (zero, zero), unroll=4)
    hs[0] = low.astype(BF16)
    hs[1] = high.astype(BF16)

    pl.semaphore_wait(barrier, count)
    field_copies = [
        remote(cxs.at[1], cx.at[0], send_sem.at[2], recv_sem.at[2], (east, gy)),
        remote(cxs.at[0], cx.at[1], send_sem.at[3], recv_sem.at[3], (west, gy)),
    ]
    probe_copies = []
    used = 4
    arrivals = [
        (side, which, row, column)
        for side, column in ((0, north), (1, south))
        for which, row in ((2, west), (1, gx), (0, east))
    ]
    for i, (side, which, row, column) in enumerate(arrivals):
        slot = side * 3 + which
        field_copies.append(
            remote(
                cys.at[1 - side], cy.at[slot], send_sem.at[4 + i], recv_sem.at[4 + i], (row, column)
            )
        )
    for i, (side, which, row, column) in enumerate(arrivals):
        slot = side * 3 + which
        probe_copies.append(
            remote(
                hs.at[1 - side], hy.at[slot], send_sem.at[10 + i], recv_sem.at[10 + i], (row, column)
            )
        )
    probe_copies += [
        remote(pt.at[:, nx - 2 : nx], xh.at[0], send_sem.at[0], recv_sem.at[0], (east, gy)),
        remote(pt.at[:, 0:2], xh.at[1], send_sem.at[1], recv_sem.at[1], (west, gy)),
    ]

    has_west = (gx > 0).astype(F32)
    has_east = (gx < ng - 1).astype(F32)
    has_south = (gy > 0).astype(F32)
    has_north = (gy < ny - 1).astype(F32)
    has_x = (has_west, 1.0, has_east)
    has_y = (has_south, has_north)
    rank = left.shape[1]
    for load in loads[4:]:
        load.wait()

    wt[0:leaf, :] = block[...].astype(BF16)
    row = lax.broadcasted_iota(jnp.int32, (rank, leaf), 0)
    for level in range(levels):
        gain = jnp.where(row < ranks[level], float(leaf * 2**level) ** -0.5, 0.0)
        at = leaf + 2 * level * rank
        wt[at : at + rank, :] = (right[level] * gain).astype(BF16)
        wt[at + rank : at + 2 * rank, :] = left[level].astype(BF16)

    for copy in field_copies:
        copy.wait_recv()

    tall = nx + 16
    wide = 3 * LANES
    lane = lax.broadcasted_iota(jnp.int32, (nx, LANES), 1)
    for z in range(nz):
        ce[z] = jnp.zeros((tall, wide), F32)
        wd[z] = jnp.zeros((tall, wide), F32)
        ce[z, 8 : 8 + nx, 0 : 2 * LANES] = cond[z]
        wd[z, 8 : 8 + nx, 0 : 2 * LANES] = weights[z]
        ce[z, 5:8, 0 : 2 * LANES] = cx[0, 4 * z : 4 * z + 3, :] * has_west
        wd[z, 7:8, 0 : 2 * LANES] = cx[0, 4 * z + 3 : 4 * z + 4, :] * has_west
        ce[z, 8 + nx : 11 + nx, 0 : 2 * LANES] = cx[1, 4 * z : 4 * z + 3, :] * has_east
        wd[z, 8 + nx : 9 + nx, 0 : 2 * LANES] = cx[1, 4 * z + 3 : 4 * z + 4, :] * has_east
        for which in range(3):
            above = cy[3 + which] * (has_x[which] * has_y[1])
            below = cy[which] * (has_x[which] * has_y[0])
            value = jnp.where(lane < 3, pltpu.roll(above, (LANES - 4 * z) % LANES, 1), 0.0)
            value = jnp.where(lane > LANES - 4, pltpu.roll(below, LANES - 3 - 4 * z, 1), value)
            if which == 0:
                ce[z, 0:8, 2 * LANES :] = value[nx - 8 :, :]
            elif which == 2:
                ce[z, 8 + nx :, 2 * LANES :] = value[:8, :]
            else:
                ce[z, 8 : 8 + nx, 2 * LANES :] = value
                value = jnp.where(lane == 0, pltpu.roll(above, LANES - 3 - 4 * z, 1), 0.0)
                value = jnp.where(lane == LANES - 1, pltpu.roll(below, LANES - 4 - 4 * z, 1), value)
                wd[z, 8 : 8 + nx, 2 * LANES :] = value
    for z in range(nz):
        centre = ce[z]
        upper = ce[z + 1] if z + 1 < nz else jnp.zeros_like(centre)
        lower = ce[z - 1] if z > 0 else jnp.zeros_like(centre)
        face_x = 0.5 * (centre + pltpu.roll(centre, tall - 1, 0))
        face_y = 0.5 * (centre + pltpu.roll(centre, wide - 1, 1))
        back_y = pltpu.roll(face_y, 1, 1)
        face_z = 0.5 * (centre + upper)
        total = 1.0 + face_x + pltpu.roll(face_x, 1, 0) + face_y + back_y
        total = total + face_z + 0.5 * (centre + lower)
        inverse = 1.0 / total
        fx[z] = face_x
        fyp[z] = face_y
        fym[z] = back_y
        fz[z] = face_z
        dg[z] = total
        dd[z] = inverse
        wd[z] = wd[z] * inverse

    tile_lane = lax.broadcasted_iota(jnp.int32, (k, LANES), 1)

    def tiles(ref, z, x):
        whole = ref[z, pl.ds(x + 8, 1), :]
        return [whole[:, i * LANES : (i + 1) * LANES] for i in range(3)]

    def split(value):
        return [value[:, i * LANES : (i + 1) * LANES] for i in range(value.shape[1] // LANES)]

    def store(ref, z, x, parts):
        for i in range(len(parts)):
            ref[z, x, :, i * LANES : (i + 1) * LANES] = parts[i]

    def edge_tile(z, x, which):
        line = z * nx + x
        above = hy[3 + which].astype(F32) * (has_x[which] * has_y[1])
        below = hy[which].astype(F32) * (has_x[which] * has_y[0])
        above = pltpu.roll(above, lax.rem(LANES - 2 * line + LANES, LANES), 1)
        below = pltpu.roll(below, lax.rem(2 * LANES - 2 - 2 * line, LANES), 1)
        value = jnp.where(tile_lane < 2, above, 0.0)
        return jnp.where(tile_lane >= LANES - 2, below, value)

    def inner_tiles(z, x, value):
        inverse = tiles(dd, z, x)
        parts = split(value)
        store(f1, z, x + 2, [parts[i] * inverse[i] for i in range(2)])

    def edge_tiles(z, x, edge):
        f1[z, x + 2, :, 2 * LANES :] = edge * tiles(dd, z, x)[2]

    def forward_inner(x, carry):
        for z in range(nz):
            inner_tiles(z, x, pt[z, x].astype(F32))
        return carry

    lax.fori_loop(0, nx, forward_inner, 0)
    for copy in probe_copies[:6]:
        copy.wait_recv()

    def forward_edges(x, carry):
        for z in range(nz):
            edge_tiles(z, x, edge_tile(z, x, 1))
        return carry

    lax.fori_loop(0, nx, forward_edges, 0)
    def near(ref, z, x, row, count):
        centre = split(ref[z, row])
        ahead = [pltpu.roll(part, LANES - 1, 1) for part in centre]
        behind = [pltpu.roll(part, 1, 1) for part in centre]
        east, west = split(ref[z, row + 1]), split(ref[z, row - 1])
        face_e, face_w = tiles(fx, z, x), tiles(fx, z, x - 1)
        face_n, face_s = tiles(fyp, z, x), tiles(fym, z, x)
        if z + 1 < nz:
            upper, face_u = split(ref[z + 1, row]), tiles(fz, z, x)
        if z > 0:
            lower, face_d = split(ref[z - 1, row]), tiles(fz, z - 1, x)
        sums = []
        for i in range(count):
            north = jnp.where(tile_lane == LANES - 1, ahead[(i + 1) % 3], ahead[i])
            south = jnp.where(tile_lane == 0, behind[(i + 2) % 3], behind[i])
            total = face_e[i] * east[i] + face_w[i] * west[i]
            total = total + (face_n[i] * north + face_s[i] * south)
            if z + 1 < nz:
                total = total + face_u[i] * upper[i]
            if z > 0:
                total = total + face_d[i] * lower[i]
            sums.append(total)
        return centre, sums

    def adjoint(i, carry):
        x = i - 1
        for z in range(nz):
            centre, sums = near(f1, z, x, x + 2, 3)
            diagonal, inverse, gain = tiles(dg, z, x), tiles(dd, z, x), tiles(wd, z, x)
            parts = [
                (centre[i] * diagonal[i] + sums[i]) * gain[i] * inverse[i] for i in range(3)
            ]
            store(a1, z, x + 1, parts)
        return carry

    acc[...] = jnp.zeros_like(acc)

    def finish(x, slot, apart):
        whole_high, whole_low = [], []
        for z in range(nz):
            centre, sums = near(a1, z, x, x + 1, 2)
            diagonal, inverse = tiles(dg, z, x), tiles(dd, z, x)
            source = split(pt[z, x].astype(F32))
            sketch = jnp.concatenate(
                [
                    (centre[i] * diagonal[i] + sums[i]) * inverse[i] + source[i]
                    for i in range(2)
                ],
                axis=1,
            )
            high = sketch.astype(BF16)
            low = (sketch - high.astype(F32)).astype(BF16)
            shl[z * nx + x, 0:k, :] = high
            shl[z * nx + x, k : 2 * k, :] = low
            whole_high.append(high)
            whole_low.append(low)
        applied = lax.dot_general(
            jnp.concatenate(whole_high, axis=0), wt[...], NT, preferred_element_type=F32
        )
        rows = []
        for z in range(nz):
            part = applied[z * k : (z + 1) * k]
            cuf[slot + z * apart] = part[:, leaf:]
            rows.append(part[:, :leaf].astype(BF16))
        high = jnp.concatenate(whole_high, axis=1)
        low = jnp.concatenate(whole_low, axis=1)
        lhs = jnp.concatenate([high, low], axis=0)
        rhs = jnp.concatenate([high, low, jnp.concatenate(rows, axis=1)], axis=0)
        acc[...] += lax.dot_general(lhs, rhs, NT, preferred_element_type=F32)

    lax.fori_loop(2, nx, adjoint, 0)
    inner_rows = nx - 4
    early = nz * inner_rows // (LANES // rank)

    def finish_inner(x, carry):
        finish(x, x - 2, inner_rows)
        return carry

    lax.fori_loop(2, nx - 2, finish_inner, 0)

    count = LANES // rank
    slot = tile_lane // rank

    def gather(group, carry):
        parts = [cuf[group * count + j] for j in range(count)]
        step = 1
        while step < count:
            bit = (slot // step) % 2 == 0
            for i in range(count):
                if (i // step) % 2 == 0:
                    one, two = parts[i], parts[i + step]
                    parts[i] = jnp.where(bit, one, pltpu.roll(two, step * rank, 1))
                    parts[i + step] = jnp.where(bit, pltpu.roll(one, LANES - step * rank, 1), two)
            step *= 2
        for index in range(2 * levels):
            uc[index, group] = parts[index].astype(BF16)
        return carry

    lax.fori_loop(0, early, gather, 0)

    def flipped(bits):
        device = gy
        for b in range(levels):
            if bits >> b & 1:
                device = device + (1 - 2 * lax.rem(device // 2**b, 2)) * 2**b
        return device

    tree = []
    for level in range(levels):
        half = 2**level
        share = groups // half
        for bits in range(1, 2 * half):
            peer = flipped(bits)
            kind = 2 * level + (1 if bits < half else 0)
            begin = lax.rem(peer, half) * share
            copy = pltpu.make_async_remote_copy(
                src_ref=uc.at[kind, pl.ds(begin, share)],
                dst_ref=trees[level].at[bits - 1],
                send_sem=tree_send.at[2 * half - 2 - level + bits],
                recv_sem=tree_recv.at[2 * half - 2 - level + bits],
                device_id=(gx, peer),
                device_id_type=MESH,
            )
            tree.append((copy, lax.rem(peer, half) < early // share, early < share))

    for copy, ready, never in tree:
        if not never:
            pl.when(ready)(copy.start)
    for copy in probe_copies[6:]:
        copy.wait_recv()
    for z in range(nz):
        for i in range(2):
            inner_tiles(z, i - 2, xh[0, z, i].astype(F32) * has_west)
            edge_tiles(z, i - 2, edge_tile(z, nx - 2 + i, 0))
            inner_tiles(z, nx + i, xh[1, z, i].astype(F32) * has_east)
            edge_tiles(z, nx + i, edge_tile(z, i, 2))

    def adjoint_outer(i, carry):
        return adjoint(jnp.where(i < 2, i, nx - 2 + i), carry)

    def finish_outer(i, carry):
        finish(jnp.where(i < 2, i, nx - 4 + i), nz * inner_rows + i, 4)
        return carry

    lax.fori_loop(0, 4, adjoint_outer, 0)
    lax.fori_loop(0, 4, finish_outer, 0)

    half_k, half_lanes = k // 2, LANES // 2
    half_lane = lax.broadcasted_iota(jnp.int32, (half_k, LANES), 1)
    pad = jnp.zeros((k, LANES - k), F32)

    def fold(value):
        value = jnp.concatenate([value, pad], axis=1)
        return value[:half_k] + pltpu.roll(value[half_k:], half_lanes, 1)

    def unfold(value):
        first = jnp.where(half_lane < half_lanes, value, 0.0)
        second = pltpu.roll(jnp.where(half_lane < half_lanes, 0.0, value), half_lanes, 1)
        return jnp.concatenate([first, second], axis=0) * (1.0 / cells)

    pending = []

    def send(which, stage, value):
        peers, me = stages[stage]
        packed[which, stage] = value
        gathered[which, stage, me] = value
        copies = [
            remote(
                packed.at[which, stage], gathered.at[which, stage, me],
                sum_send.at[which, stage, d], sum_recv.at[which, stage, d], peer,
            )
            for d, peer in enumerate(peers)
        ]
        pending.extend(copies)
        return copies

    def receive(which, stage, copies):
        for copy in copies:
            copy.wait_recv()
        parts = [gathered[which, stage, i] for i in range(len(copies) + 1)]
        while len(parts) > 1:
            parts = [
                parts[i] + parts[i + 1] if i + 1 < len(parts) else parts[i]
                for i in range(0, len(parts), 2)
            ]
        return parts[0]

    value = acc[...]
    total = value[0:k, 0:k] + (value[0:k, k : 2 * k] + value[k : 2 * k, 0:k]) + value[k:, k : 2 * k]
    first = send(0, 0, fold(total))
    leafpart = value[0:k, 2 * k :] + value[k:, 2 * k :]

    lax.fori_loop(early, groups, gather, 0)
    for copy, ready, never in tree:
        if never:
            copy.start()
        else:
            pl.when(jnp.logical_not(ready))(copy.start)

    first = send(0, 1, receive(0, 0, first))
    for copy, _, _ in tree:
        copy.wait_recv()
    lefts, rights = [], []
    for level in range(levels):
        half = 2**level
        share = groups // half
        begin = lax.rem(gy, half) * share
        for j in range(share):
            own = uc[2 * level + 1, begin + j].astype(F32)
            for bits in range(1, half):
                own = own + trees[level][bits - 1, j].astype(F32)
            other = trees[level][half - 1, j].astype(F32)
            for bits in range(half + 1, 2 * half):
                other = other + trees[level][bits - 1, j].astype(F32)
            lefts.append(own.astype(BF16))
            rights.append(other.astype(BF16))
    total = leafpart + lax.dot_general(
        jnp.concatenate(lefts, axis=1),
        jnp.concatenate(rights, axis=1),
        NT,
        preferred_element_type=F32,
    )
    second = send(1, 0, fold(total))
    first = send(0, 2, receive(0, 1, first))
    second = send(1, 1, receive(1, 0, second))
    matrix = unfold(receive(0, 2, first))

    row = lax.broadcasted_iota(jnp.int32, (k, LANES), 0)
    lane = lax.broadcasted_iota(jnp.int32, (k, LANES), 1)
    start = LANES // 2
    whole = jnp.where(lane < k, matrix, jnp.where(lane == row + start, 1.0, 0.0))
    blocks = [whole[8 * t : 8 * t + 8] for t in range(k // 8)]
    inner = lax.broadcasted_iota(jnp.int32, (8, LANES), 0)
    for j in range(0, k, 2):
        t, s = divmod(j, 8)
        one, two = blocks[t][s : s + 1, :], blocks[t][s + 1 : s + 2, :]
        cross = one[:, j + 1 : j + 2]
        below = two[:, j : j + 1]
        inverse_one = 1.0 / one[:, j : j + 1]
        below = below * inverse_one
        inverse_two = 1.0 / (two[:, j + 1 : j + 2] - below * cross)
        scaled_one = one * inverse_one
        scaled_two = (two - below * one) * inverse_two
        cross = cross * inverse_one
        for i in range(t, k // 8):
            left_one, left_two = blocks[i][:, j : j + 1], blocks[i][:, j + 1 : j + 2]
            left_two = left_two - left_one * cross
            change_one, change_two = left_one * scaled_one, left_two * scaled_two
            if i == t:
                change_one = jnp.where(inner > s, change_one, 0.0)
                change_two = jnp.where(inner > s + 1, change_two, 0.0)
            blocks[i] = blocks[i] - change_one - change_two
        if j == 3 * k // 4:
            second = send(1, 2, receive(1, 1, second))
    whole = jnp.concatenate(blocks, axis=0)
    pivots = jnp.sum(jnp.where(lane == row, whole, 0.0), axis=1, keepdims=True)
    inverse = whole[:, start : start + k] / jnp.sqrt(pivots)

    high = inverse.astype(BF16)
    low = (inverse - high.astype(F32)).astype(BF16)
    lhs = jnp.concatenate(
        [
            jnp.concatenate([high, high], axis=1),
            jnp.concatenate([low, jnp.zeros_like(low)], axis=1),
        ],
        axis=0,
    )
    stores = []
    for z in range(nz):

        def one(x, carry):
            value = jnp.dot(lhs, shl[z * nx + x], preferred_element_type=F32)
            value = value[0:k] + value[k:]
            buffer[z, 0, pl.ds(x, k, stride=nx), :] = value[:, :LANES]
            buffer[z, 1, pl.ds(x, k, stride=nx), :] = value[:, LANES:]
            return carry

        lax.fori_loop(0, nx, one, 0, unroll=4)
        for i in range(2):
            copy = pltpu.make_async_copy(
                buffer.at[z, i].reshape(k, nx, LANES),
                out.at[:, z, :, i * LANES : (i + 1) * LANES],
                store_sem.at[z, i],
            )
            copy.start()
            stores.append(copy)
    middle = unfold(receive(1, 2, second))[:, 0:k]
    product = jnp.dot(inverse, middle, precision=HIGH, preferred_element_type=F32)
    product = lax.dot_general(product, inverse, NT, precision=HIGH, preferred_element_type=F32)
    projected[...] = product + jnp.where(lane[:, 0:k] == row[:, 0:k], 1.0, 0.0)
    for copy in field_copies + probe_copies + [copy for copy, _, _ in tree] + pending:
        copy.wait_send()
    for copy in stores:
        copy.wait()


def copy_kernel(pieces, basis_in, projected_in, basis, projected, sem):
    size = basis.shape[0] // pieces
    copies = [pltpu.make_async_copy(projected_in, projected, sem.at[pieces])]
    for i in range(pieces):
        part = pl.ds(i * size, size)
        copies.append(pltpu.make_async_copy(basis_in.at[part], basis.at[part], sem.at[i]))
    for copy in copies:
        copy.start()
    for copy in copies:
        copy.wait()


def params(**more):
    return pltpu.CompilerParams(vmem_limit_bytes=56 * 2**20, **more)


def shards(
    probes, classes, class_table, weights, prior_block, prior_left, prior_right, block_ranks
):
    ng, ny = lax.axis_size("gx"), lax.axis_size("gy")
    k, nz, nx, leaf = probes.shape
    levels = ny.bit_length() - 1
    rank = prior_left.shape[1]
    lines = nz * nx
    groups = lines * rank // LANES
    cells = float(nz * nx * leaf * ng * ny)
    shape = jax.ShapeDtypeStruct
    dma = pltpu.SemaphoreType.DMA
    vmem = pltpu.VMEM
    edges = 2 * ny
    most = 8
    while most < max(ng // min(4, ng), ny // min(2, ny)):
        most *= 2

    field = vmem((nz, nx + 16, 3 * LANES), F32)
    basis, projected = pl.pallas_call(
        functools.partial(
            sketch_kernel, ng, ny, k, nz, nx, levels, leaf, groups, cells
        ),
        out_shape=(
            shape((k, nz, nx, leaf), F32),
            shape((k, k), F32),
        ),
        in_specs=[HBM] * 8,
        out_specs=(HBM, VMEM),
        scratch_shapes=[
            vmem((lines, 2 * k, leaf), BF16),
            vmem((nz, 2, k * nx, LANES), F32),
            dma((nz, 2)),
            vmem((k * lines, leaf), BF16),
            vmem(classes.shape, classes.dtype),
            pltpu.SMEM(class_table.shape, F32),
            vmem(weights.shape, F32),
            vmem(prior_block.shape, F32),
            vmem((levels, rank, leaf), F32),
            vmem((levels, rank, leaf), F32),
            pltpu.SMEM(block_ranks.shape, block_ranks.dtype),
            dma((8,)),
            vmem((nz, nx, k, leaf), BF16),
            vmem((nz, nx, leaf), F32),
            vmem((2, k * lines, LANES), F32),
            vmem((2, nz, 2, k, leaf), BF16),
            vmem((6, k, LANES), BF16),
            vmem((2, 4 * nz, leaf), F32),
            vmem((6, nx, LANES), F32),
            vmem((2, k, LANES), BF16),
            vmem((2, 4 * nz, leaf), F32),
            vmem((2, nx, LANES), F32),
            dma((16,)),
            dma((16,)),
        ]
        + [field] * 8
        + [
            vmem((nz, nx + 4, k, 3 * LANES), F32),
            vmem((nz, nx + 2, k, 3 * LANES), F32),
            vmem((leaf + LANES, leaf), BF16),
            vmem((2 * k, 3 * k), F32),
            vmem((lines, k, LANES), F32),
            vmem((2 * levels, groups, k, LANES), BF16),
            [
                vmem((2 ** (level + 1) - 1, groups >> level, k, LANES), BF16)
                for level in range(levels)
            ],
            dma((edges,)),
            dma((edges,)),
            vmem((2, 3, k // 2, LANES), F32),
            vmem((2, 3, most, k // 2, LANES), F32),
            dma((2, 3, most)),
            dma((2, 3, most)),
        ],
        compiler_params=params(collective_id=0, has_side_effects=True),
    )(
        probes.reshape(k * lines, leaf), classes, class_table, weights, prior_block, prior_left,
        prior_right, block_ranks,
    )
    pieces = 16
    return pl.pallas_call(
        functools.partial(copy_kernel, pieces),
        out_shape=(shape((k, nz, nx, leaf), F32), shape((k, k), F32)),
        in_specs=[HBM] * 2,
        out_specs=(HBM, HBM),
        scratch_shapes=[dma((pieces + 1,))],
        compiler_params=params(),
    )(basis, projected)


def solution(mesh):
    return jax.shard_map(
        shards,
        mesh=mesh,
        in_specs=(
            P(None, None, "gx", "gy"),
            P(None, "gx", "gy"),
            P(),
            P(None, "gx", "gy"),
            P("gy", None),
            P(None, None, "gy"),
            P(None, None, "gy"),
            P(),
        ),
        out_specs=(P(None, None, "gx", "gy"), P()),
        check_vma=False,
    )
```

```python
import functools

import jax
import jax.numpy as jnp
from jax import lax
from jax.experimental import pallas as pl
from jax.experimental.pallas import tpu as pltpu
from jax.sharding import PartitionSpec as P

MESH = pl.DeviceIdType.MESH
HIGH = lax.Precision.HIGHEST
F32 = jnp.float32
BF16 = jnp.bfloat16
LANES = 128
VMEM = pl.BlockSpec(memory_space=pltpu.VMEM)
SMEM = pl.BlockSpec(memory_space=pltpu.SMEM)
ANY = pl.BlockSpec(memory_space=pl.ANY)
HBM = pl.BlockSpec(memory_space=pltpu.HBM)
NT = (((1,), (1,)), ((), ()))


def signal_all(devices):
    barrier = pltpu.get_barrier_semaphore()
    for device in devices:
        pl.semaphore_signal(barrier, inc=1, device_id=device, device_id_type=MESH)
    return barrier, len(devices)


def remote(src, dst, send, recv, device):
    copy = pltpu.make_async_remote_copy(
        src_ref=src, dst_ref=dst, send_sem=send, recv_sem=recv, device_id=device, device_id_type=MESH
    )
    copy.start()
    return copy


def eliminate(blocks, t):
    inner = lax.broadcasted_iota(jnp.int32, (8, LANES), 0)

    def spread(value):
        return jnp.broadcast_to(value, (8, LANES))

    columns = [spread(blocks[t][:, 8 * t + c : 8 * t + c + 1]) for c in range(8)]
    entry = [[spread(columns[c][r : r + 1, :]) for c in range(r + 1)] for r in range(8)]
    rows = [spread(blocks[t][r : r + 1, :]) for r in range(8)]
    factor = [[None] * 8 for _ in range(8)]
    inverses = []
    for q in range(8):
        inverses.append(1.0 / entry[q][q])
        for r in range(q + 1, 8):
            factor[r][q] = entry[r][q] * inverses[q]
        for r in range(q + 1, 8):
            for c in range(q + 1, r + 1):
                entry[r][c] = entry[r][c] - factor[r][q] * entry[c][q]
    for r in range(8):
        for q in range(r):
            rows[r] = rows[r] - factor[r][q] * rows[q]
    scaled = [rows[q] * inverses[q] for q in range(8)]
    for i in range(t + 1, len(blocks)):
        lefts = [spread(blocks[i][:, 8 * t + q : 8 * t + q + 1]) for q in range(8)]
        for q in range(8):
            for p in range(q):
                lefts[q] = lefts[q] - lefts[p] * factor[q][p]
        changes = [lefts[q] * scaled[q] for q in range(8)]
        while len(changes) > 1:
            changes = [changes[n] + changes[n + 1] for n in range(0, len(changes), 2)]
        blocks[i] = blocks[i] - changes[0]
    done, pivots = rows[0], entry[0][0]
    for r in range(1, 8):
        done = jnp.where(inner == r, rows[r], done)
        pivots = jnp.where(inner == r, entry[r][r], pivots)
    return done, 1.0 / jnp.sqrt(pivots)


def sketch_kernel(
    ng, ny, k, nz, nx, levels, leaf, groups, cells,
    probes_in, classes_in, table_in, weights_in, block_in, left_in, right_in, ranks_in,
    out, projected,
    shl, buffer, store_sem, probes, classes, table, weights, block, left, right, ranks, load_sem,
    pt, cond, pf, xh, hy, hf, cx, cy, hs, cxs, cys, send_sem, recv_sem,
    ce, dg, dd, wd, fx, fyp, fym, fz, f1, a1, wt, acc, cuf, uc,
    trees, tree_send, tree_recv, packed, gathered, sum_send, sum_recv,
):
    gx, gy = lax.axis_index("gx"), lax.axis_index("gy")
    east, west = lax.rem(gx + 1, ng), lax.rem(gx + ng - 1, ng)
    north, south = lax.rem(gy + 1, ny), lax.rem(gy + ny - 1, ny)
    around = [(west, gy), (east, gy)]
    for column in (south, north):
        for row in (west, gx, east):
            around.append((row, column))

    across, pair = min(4, ng), min(2, ny)
    deep, high_y = ng // across, ny // pair
    at_z, at_x = gx // across, lax.rem(gx, across)
    at_y, at_c = gy // pair, lax.rem(gy, pair)
    stages = [
        (
            [
                (
                    at_z * across + lax.rem(at_x + d % across, across),
                    at_y * pair + lax.rem(at_c + d // across, pair),
                )
                for d in range(1, across * pair)
            ],
            at_c * across + at_x,
        ),
        ([(lax.rem(at_z + d, deep) * across + at_x, gy) for d in range(1, deep)], at_z),
        ([(gx, lax.rem(at_y + d, high_y) * pair + at_c) for d in range(1, high_y)], at_y),
    ]
    column = [(gx, lax.rem(gy + d, ny)) for d in range(1, ny)]
    barrier, count = signal_all(around + stages[0][0] + stages[1][0] + column)

    loads = [
        pltpu.make_async_copy(source, target, load_sem.at[i])
        for i, (source, target) in enumerate(
            [
                (classes_in, classes),
                (weights_in, weights),
                (table_in, table),
                (probes_in, probes),
                (block_in, block),
                (left_in.at[0:levels], left),
                (right_in.at[0:levels], right),
                (ranks_in, ranks),
            ]
        )
    ]
    for load in loads:
        load.start()

    lines = nz * nx
    for load in loads[:3]:
        load.wait()

    for z in range(nz):
        picked = classes[z]
        value = jnp.zeros(picked.shape, F32)
        for index in range(table.shape[0]):
            value = jnp.where(picked == index, table[index], value)
        cond[z] = value
        cxs[0, 4 * z : 4 * z + 3, :] = value[0:3, :]
        cxs[1, 4 * z : 4 * z + 3, :] = value[nx - 3 : nx, :]
        cxs[0, 4 * z + 3 : 4 * z + 4, :] = weights[z, 0:1, :]
        cxs[1, 4 * z + 3 : 4 * z + 4, :] = weights[z, nx - 1 : nx, :]
    lane = lax.broadcasted_iota(jnp.int32, (nx, LANES), 1)
    low = jnp.zeros((nx, LANES), F32)
    high = jnp.zeros((nx, LANES), F32)
    for z in range(nz):
        here = lane // 4 == z
        last = lane % 4 == 3
        first_tile, last_tile = cond[z, :, :LANES], cond[z, :, LANES:]
        w_first, w_last = weights[z, :, :LANES], weights[z, :, LANES:]
        own = jnp.where(last, pltpu.roll(w_first, 4 * z + 3, 1), pltpu.roll(first_tile, 4 * z, 1))
        low = jnp.where(here, own, low)
        own = jnp.where(last, pltpu.roll(w_last, 4 * z + 4, 1), pltpu.roll(last_tile, 4 * z + 3, 1))
        high = jnp.where(here, own, high)
    cys[0] = low
    cys[1] = high

    loads[3].wait()
    chunk = 512

    def widen(i, carry):
        rows = pl.ds(pl.multiple_of(i * chunk, chunk), chunk)
        value = probes[rows, :].astype(F32)
        pf[0, rows, :] = value[:, :LANES]
        pf[1, rows, :] = value[:, LANES:]
        return carry

    lax.fori_loop(0, k * lines // chunk, widen, 0)

    place = lax.broadcasted_iota(jnp.int32, (k, LANES), 1) // 2

    def turn(line, carry):
        low, high = carry
        lo = pf[0, pl.ds(line, k, stride=lines), :]
        hi = pf[1, pl.ds(line, k, stride=lines), :]
        pt[line // nx, lax.rem(line, nx)] = jnp.concatenate([lo, hi], axis=1).astype(BF16)
        low = jnp.where(place == line, pltpu.roll(lo, 2 * line, 1), low)
        high = jnp.where(place == line, pltpu.roll(hi, lax.rem(2 * line + 2, LANES), 1), high)
        return low, high

    zero = jnp.zeros((k, LANES), F32)
    low, high = lax.fori_loop(0, lines, turn, (zero, zero), unroll=4)
    hs[0] = low.astype(BF16)
    hs[1] = high.astype(BF16)

    pl.semaphore_wait(barrier, count)
    field_copies = [
        remote(cxs.at[1], cx.at[0], send_sem.at[2], recv_sem.at[2], (east, gy)),
        remote(cxs.at[0], cx.at[1], send_sem.at[3], recv_sem.at[3], (west, gy)),
    ]
    probe_copies = []
    used = 4
    arrivals = [
        (side, which, row, column)
        for side, column in ((0, north), (1, south))
        for which, row in ((2, west), (1, gx), (0, east))
    ]
    for i, (side, which, row, column) in enumerate(arrivals):
        slot = side * 3 + which
        field_copies.append(
            remote(
                cys.at[1 - side], cy.at[slot], send_sem.at[4 + i], recv_sem.at[4 + i], (row, column)
            )
        )
    for i, (side, which, row, column) in enumerate(arrivals):
        slot = side * 3 + which
        probe_copies.append(
            remote(
                hs.at[1 - side], hy.at[slot], send_sem.at[10 + i], recv_sem.at[10 + i], (row, column)
            )
        )
    probe_copies += [
        remote(pt.at[:, nx - 2 : nx], xh.at[0], send_sem.at[0], recv_sem.at[0], (east, gy)),
        remote(pt.at[:, 0:2], xh.at[1], send_sem.at[1], recv_sem.at[1], (west, gy)),
    ]

    has_west = (gx > 0).astype(F32)
    has_east = (gx < ng - 1).astype(F32)
    has_south = (gy > 0).astype(F32)
    has_north = (gy < ny - 1).astype(F32)
    has_x = (has_west, 1.0, has_east)
    has_y = (has_south, has_north)
    rank = left.shape[1]
    for load in loads[4:]:
        load.wait()

    wt[0:leaf, :] = block[...].astype(BF16)
    row = lax.broadcasted_iota(jnp.int32, (rank, leaf), 0)
    for level in range(levels):
        gain = jnp.where(row < ranks[level], float(leaf * 2**level) ** -0.5, 0.0)
        at = leaf + 2 * level * rank
        wt[at : at + rank, :] = (right[level] * gain).astype(BF16)
        wt[at + rank : at + 2 * rank, :] = left[level].astype(BF16)

    for copy in field_copies:
        copy.wait_recv()

    tall = nx + 16
    wide = 3 * LANES
    lane = lax.broadcasted_iota(jnp.int32, (nx, LANES), 1)
    for z in range(nz):
        ce[z] = jnp.zeros((tall, wide), F32)
        wd[z] = jnp.zeros((tall, wide), F32)
        ce[z, 8 : 8 + nx, 0 : 2 * LANES] = cond[z]
        wd[z, 8 : 8 + nx, 0 : 2 * LANES] = weights[z]
        ce[z, 5:8, 0 : 2 * LANES] = cx[0, 4 * z : 4 * z + 3, :] * has_west
        wd[z, 7:8, 0 : 2 * LANES] = cx[0, 4 * z + 3 : 4 * z + 4, :] * has_west
        ce[z, 8 + nx : 11 + nx, 0 : 2 * LANES] = cx[1, 4 * z : 4 * z + 3, :] * has_east
        wd[z, 8 + nx : 9 + nx, 0 : 2 * LANES] = cx[1, 4 * z + 3 : 4 * z + 4, :] * has_east
        for which in range(3):
            above = cy[3 + which] * (has_x[which] * has_y[1])
            below = cy[which] * (has_x[which] * has_y[0])
            value = jnp.where(lane < 3, pltpu.roll(above, (LANES - 4 * z) % LANES, 1), 0.0)
            value = jnp.where(lane > LANES - 4, pltpu.roll(below, LANES - 3 - 4 * z, 1), value)
            if which == 0:
                ce[z, 0:8, 2 * LANES :] = value[nx - 8 :, :]
            elif which == 2:
                ce[z, 8 + nx :, 2 * LANES :] = value[:8, :]
            else:
                ce[z, 8 : 8 + nx, 2 * LANES :] = value
                value = jnp.where(lane == 0, pltpu.roll(above, LANES - 3 - 4 * z, 1), 0.0)
                value = jnp.where(lane == LANES - 1, pltpu.roll(below, LANES - 4 - 4 * z, 1), value)
                wd[z, 8 : 8 + nx, 2 * LANES :] = value
    for z in range(nz):
        centre = ce[z]
        upper = ce[z + 1] if z + 1 < nz else jnp.zeros_like(centre)
        lower = ce[z - 1] if z > 0 else jnp.zeros_like(centre)
        face_x = 0.5 * (centre + pltpu.roll(centre, tall - 1, 0))
        face_y = 0.5 * (centre + pltpu.roll(centre, wide - 1, 1))
        back_y = pltpu.roll(face_y, 1, 1)
        face_z = 0.5 * (centre + upper)
        total = 1.0 + face_x + pltpu.roll(face_x, 1, 0) + face_y + back_y
        total = total + face_z + 0.5 * (centre + lower)
        inverse = 1.0 / total
        fx[z] = face_x
        fyp[z] = face_y
        fym[z] = back_y
        fz[z] = face_z
        dg[z] = total
        dd[z] = inverse
        wd[z] = wd[z] * inverse

    tile_lane = lax.broadcasted_iota(jnp.int32, (k, LANES), 1)

    def tiles(ref, z, x):
        whole = ref[z, pl.ds(x + 8, 1), :]
        return [whole[:, i * LANES : (i + 1) * LANES] for i in range(3)]

    def split(value):
        return [value[:, i * LANES : (i + 1) * LANES] for i in range(value.shape[1] // LANES)]

    def store(ref, z, x, parts):
        for i in range(len(parts)):
            ref[z, x, :, i * LANES : (i + 1) * LANES] = parts[i]

    def edge_tile(z, x, which):
        line = z * nx + x
        above = pltpu.roll(hf[3 + which], lax.rem(LANES - 2 * line + LANES, LANES), 1)
        below = pltpu.roll(hf[which], lax.rem(2 * LANES - 2 - 2 * line, LANES), 1)
        return jnp.where(tile_lane < LANES // 2, above, below)

    def inner_tiles(z, x, value):
        inverse = tiles(dd, z, x)
        parts = split(value)
        store(f1, z, x + 2, [parts[i] * inverse[i] for i in range(2)])

    def edge_tiles(z, x, edge):
        f1[z, x + 2, :, 2 * LANES :] = edge * tiles(dd, z, x)[2]

    def forward_inner(x, carry):
        for z in range(nz):
            inner_tiles(z, x, pt[z, x].astype(F32))
        return carry

    lax.fori_loop(0, nx, forward_inner, 0)
    for copy in probe_copies[:6]:
        copy.wait_recv()

    for which in range(3):
        hf[which] = hy[which].astype(F32) * (has_x[which] * has_y[0])
        hf[3 + which] = hy[3 + which].astype(F32) * (has_x[which] * has_y[1])

    def forward_edges(x, carry):
        for z in range(nz):
            edge_tiles(z, x, edge_tile(z, x, 1))
        return carry

    lax.fori_loop(0, nx, forward_edges, 0)
    def near(ref, z, x, row, count):
        centre = split(ref[z, row])
        ahead = [pltpu.roll(part, LANES - 1, 1) for part in centre]
        behind = [pltpu.roll(part, 1, 1) for part in centre]
        east, west = split(ref[z, row + 1]), split(ref[z, row - 1])
        face_e, face_w = tiles(fx, z, x), tiles(fx, z, x - 1)
        face_n, face_s = tiles(fyp, z, x), tiles(fym, z, x)
        if z + 1 < nz:
            upper, face_u = split(ref[z + 1, row]), tiles(fz, z, x)
        if z > 0:
            lower, face_d = split(ref[z - 1, row]), tiles(fz, z - 1, x)
        sums = []
        for i in range(count):
            north = jnp.where(tile_lane == LANES - 1, ahead[(i + 1) % 3], ahead[i])
            south = jnp.where(tile_lane == 0, behind[(i + 2) % 3], behind[i])
            total = face_e[i] * east[i] + face_w[i] * west[i]
            total = total + (face_n[i] * north + face_s[i] * south)
            if z + 1 < nz:
                total = total + face_u[i] * upper[i]
            if z > 0:
                total = total + face_d[i] * lower[i]
            sums.append(total)
        return centre, sums

    def adjoint(i, carry):
        x = i - 1
        for z in range(nz):
            centre, sums = near(f1, z, x, x + 2, 3)
            diagonal, inverse, gain = tiles(dg, z, x), tiles(dd, z, x), tiles(wd, z, x)
            parts = [
                (centre[i] * diagonal[i] + sums[i]) * gain[i] * inverse[i] for i in range(3)
            ]
            store(a1, z, x + 1, parts)
        return carry

    acc[...] = jnp.zeros_like(acc)

    def finish(x, slot, apart):
        whole_high, whole_low = [], []
        for z in range(nz):
            centre, sums = near(a1, z, x, x + 1, 2)
            diagonal, inverse = tiles(dg, z, x), tiles(dd, z, x)
            source = split(pt[z, x].astype(F32))
            sketch = jnp.concatenate(
                [
                    (centre[i] * diagonal[i] + sums[i]) * inverse[i] + source[i]
                    for i in range(2)
                ],
                axis=1,
            )
            high = sketch.astype(BF16)
            low = (sketch - high.astype(F32)).astype(BF16)
            shl[z * nx + x, 0:k, :] = high
            shl[z * nx + x, k : 2 * k, :] = low
            whole_high.append(high)
            whole_low.append(low)
        applied = lax.dot_general(
            jnp.concatenate(whole_high, axis=0), wt[...], NT, preferred_element_type=F32
        )
        rows = []
        for z in range(nz):
            part = applied[z * k : (z + 1) * k]
            cuf[slot + z * apart] = part[:, leaf:]
            rows.append(part[:, :leaf].astype(BF16))
        high = jnp.concatenate(whole_high, axis=1)
        low = jnp.concatenate(whole_low, axis=1)
        lhs = jnp.concatenate([high, low], axis=0)
        rhs = jnp.concatenate([high, low, jnp.concatenate(rows, axis=1)], axis=0)
        acc[...] += lax.dot_general(lhs, rhs, NT, preferred_element_type=F32)

    lax.fori_loop(2, nx, adjoint, 0)
    inner_rows = nx - 4
    early = nz * inner_rows // (LANES // rank)

    def finish_inner(x, carry):
        finish(x, x - 2, inner_rows)
        return carry

    lax.fori_loop(2, nx - 2, finish_inner, 0)

    count = LANES // rank
    slot = tile_lane // rank

    def gather(group, carry):
        parts = [cuf[group * count + j] for j in range(count)]
        step = 1
        while step < count:
            bit = (slot // step) % 2 == 0
            for i in range(count):
                if (i // step) % 2 == 0:
                    one, two = parts[i], parts[i + step]
                    parts[i] = jnp.where(bit, one, pltpu.roll(two, step * rank, 1))
                    parts[i + step] = jnp.where(bit, pltpu.roll(one, LANES - step * rank, 1), two)
            step *= 2
        for index in range(2 * levels):
            uc[index, group] = parts[index].astype(BF16)
        return carry

    lax.fori_loop(0, early, gather, 0)

    def flipped(bits):
        device = gy
        for b in range(levels):
            if bits >> b & 1:
                device = device + (1 - 2 * lax.rem(device // 2**b, 2)) * 2**b
        return device

    tree = []
    for level in range(levels):
        half = 2**level
        share = groups // half
        for bits in range(1, 2 * half):
            peer = flipped(bits)
            kind = 2 * level + (1 if bits < half else 0)
            begin = lax.rem(peer, half) * share
            copy = pltpu.make_async_remote_copy(
                src_ref=uc.at[kind, pl.ds(begin, share)],
                dst_ref=trees[level].at[bits - 1],
                send_sem=tree_send.at[2 * half - 2 - level + bits],
                recv_sem=tree_recv.at[2 * half - 2 - level + bits],
                device_id=(gx, peer),
                device_id_type=MESH,
            )
            tree.append((copy, lax.rem(peer, half) < early // share, early < share))

    for copy, ready, never in tree:
        if not never:
            pl.when(ready)(copy.start)
    for copy in probe_copies[6:]:
        copy.wait_recv()
    for z in range(nz):
        for i in range(2):
            inner_tiles(z, i - 2, xh[0, z, i].astype(F32) * has_west)
            edge_tiles(z, i - 2, edge_tile(z, nx - 2 + i, 0))
            inner_tiles(z, nx + i, xh[1, z, i].astype(F32) * has_east)
            edge_tiles(z, nx + i, edge_tile(z, i, 2))

    def adjoint_outer(i, carry):
        return adjoint(jnp.where(i < 2, i, nx - 2 + i), carry)

    def finish_outer(i, carry):
        finish(jnp.where(i < 2, i, nx - 4 + i), nz * inner_rows + i, 4)
        return carry

    lax.fori_loop(0, 4, adjoint_outer, 0)
    lax.fori_loop(0, 4, finish_outer, 0)

    half_k, half_lanes = k // 2, LANES // 2
    half_lane = lax.broadcasted_iota(jnp.int32, (half_k, LANES), 1)
    pad = jnp.zeros((k, LANES - k), F32)

    def fold(value):
        value = jnp.concatenate([value, pad], axis=1)
        return value[:half_k] + pltpu.roll(value[half_k:], half_lanes, 1)

    def unfold(value):
        first = jnp.where(half_lane < half_lanes, value, 0.0)
        second = pltpu.roll(jnp.where(half_lane < half_lanes, 0.0, value), half_lanes, 1)
        return jnp.concatenate([first, second], axis=0) * (1.0 / cells)

    pending = []

    def send(which, stage, value):
        peers, me = stages[stage]
        packed[which, stage] = value
        gathered[which, stage, me] = value
        copies = [
            remote(
                packed.at[which, stage], gathered.at[which, stage, me],
                sum_send.at[which, stage, d], sum_recv.at[which, stage, d], peer,
            )
            for d, peer in enumerate(peers)
        ]
        pending.extend(copies)
        return copies

    def receive(which, stage, copies):
        for copy in copies:
            copy.wait_recv()
        parts = [gathered[which, stage, i] for i in range(len(copies) + 1)]
        while len(parts) > 1:
            parts = [
                parts[i] + parts[i + 1] if i + 1 < len(parts) else parts[i]
                for i in range(0, len(parts), 2)
            ]
        return parts[0]

    value = acc[...]
    total = value[0:k, 0:k] + (value[0:k, k : 2 * k] + value[k : 2 * k, 0:k]) + value[k:, k : 2 * k]
    first = send(0, 0, fold(total))
    leafpart = value[0:k, 2 * k :] + value[k:, 2 * k :]

    lax.fori_loop(early, groups, gather, 0)
    for copy, ready, never in tree:
        if never:
            copy.start()
        else:
            pl.when(jnp.logical_not(ready))(copy.start)

    first = send(0, 1, receive(0, 0, first))
    for copy, _, _ in tree:
        copy.wait_recv()
    lefts, rights = [], []
    for level in range(levels):
        half = 2**level
        share = groups // half
        begin = lax.rem(gy, half) * share
        for j in range(share):
            own = uc[2 * level + 1, begin + j].astype(F32)
            for bits in range(1, half):
                own = own + trees[level][bits - 1, j].astype(F32)
            other = trees[level][half - 1, j].astype(F32)
            for bits in range(half + 1, 2 * half):
                other = other + trees[level][bits - 1, j].astype(F32)
            lefts.append(own.astype(BF16))
            rights.append(other.astype(BF16))
    total = leafpart + lax.dot_general(
        jnp.concatenate(lefts, axis=1),
        jnp.concatenate(rights, axis=1),
        NT,
        preferred_element_type=F32,
    )
    second = send(1, 0, fold(total))
    first = send(0, 2, receive(0, 1, first))
    second = send(1, 1, receive(1, 0, second))
    matrix = unfold(receive(0, 2, first))

    row = lax.broadcasted_iota(jnp.int32, (k, LANES), 0)
    lane = lax.broadcasted_iota(jnp.int32, (k, LANES), 1)
    start = LANES // 2
    whole = jnp.where(lane < k, matrix, jnp.where(lane == row + start, 1.0, 0.0))
    blocks = [whole[8 * t : 8 * t + 8] for t in range(k // 8)]
    inverse = []
    for t in range(k // 8):
        done, scale = eliminate(blocks, t)
        inverse.append(done[:, start : start + k] * scale[:, 0:k])
        if t == k // 16:
            second = send(1, 2, receive(1, 1, second))
    inverse = jnp.concatenate(inverse, axis=0)

    high = inverse.astype(BF16)
    low = (inverse - high.astype(F32)).astype(BF16)
    lhs = jnp.concatenate(
        [
            jnp.concatenate([high, high], axis=1),
            jnp.concatenate([low, jnp.zeros_like(low)], axis=1),
        ],
        axis=0,
    )
    stores = []
    for z in range(nz):

        def one(x, carry):
            value = jnp.dot(lhs, shl[z * nx + x], preferred_element_type=F32)
            value = value[0:k] + value[k:]
            buffer[z, 0, pl.ds(x, k, stride=nx), :] = value[:, :LANES]
            buffer[z, 1, pl.ds(x, k, stride=nx), :] = value[:, LANES:]
            return carry

        lax.fori_loop(0, nx, one, 0, unroll=4)
        for i in range(2):
            copy = pltpu.make_async_copy(
                buffer.at[z, i].reshape(k, nx, LANES),
                out.at[:, z, :, i * LANES : (i + 1) * LANES],
                store_sem.at[z, i],
            )
            copy.start()
            stores.append(copy)
    middle = unfold(receive(1, 2, second))[:, 0:k]
    product = jnp.dot(inverse, middle, precision=HIGH, preferred_element_type=F32)
    product = lax.dot_general(product, inverse, NT, precision=HIGH, preferred_element_type=F32)
    projected[...] = product + jnp.where(lane[:, 0:k] == row[:, 0:k], 1.0, 0.0)
    for copy in field_copies + probe_copies + [copy for copy, _, _ in tree] + pending:
        copy.wait_send()
    for copy in stores:
        copy.wait()


def copy_kernel(pieces, basis_in, projected_in, basis, projected, wide, small, load_sem, store_sem):
    size = basis.shape[0] // pieces
    parts = [pl.ds(i * size, size) for i in range(pieces)]
    loads = [
        pltpu.make_async_copy(basis_in.at[part], wide.at[part], load_sem.at[i])
        for i, part in enumerate(parts)
    ]
    loads.insert(1, pltpu.make_async_copy(projected_in, small, load_sem.at[pieces]))
    stores = [
        pltpu.make_async_copy(wide.at[part], basis.at[part], store_sem.at[i])
        for i, part in enumerate(parts)
    ]
    stores.insert(1, pltpu.make_async_copy(small, projected, store_sem.at[pieces]))
    for load in loads:
        load.start()
    for load, store in zip(loads, stores):
        load.wait()
        store.start()
    for store in stores:
        store.wait()


def params(**more):
    return pltpu.CompilerParams(vmem_limit_bytes=56 * 2**20, **more)


def shards(
    probes, classes, class_table, weights, prior_block, prior_left, prior_right, block_ranks
):
    ng, ny = lax.axis_size("gx"), lax.axis_size("gy")
    k, nz, nx, leaf = probes.shape
    levels = ny.bit_length() - 1
    rank = prior_left.shape[1]
    lines = nz * nx
    groups = lines * rank // LANES
    cells = float(nz * nx * leaf * ng * ny)
    shape = jax.ShapeDtypeStruct
    dma = pltpu.SemaphoreType.DMA
    vmem = pltpu.VMEM
    edges = 2 * ny
    most = 8
    while most < max(ng // min(4, ng), ny // min(2, ny)):
        most *= 2

    field = vmem((nz, nx + 16, 3 * LANES), F32)
    basis, projected = pl.pallas_call(
        functools.partial(
            sketch_kernel, ng, ny, k, nz, nx, levels, leaf, groups, cells
        ),
        out_shape=(
            shape((k, nz, nx, leaf), F32),
            shape((k, k), F32),
        ),
        in_specs=[HBM] * 8,
        out_specs=(HBM, VMEM),
        scratch_shapes=[
            vmem((lines, 2 * k, leaf), BF16),
            vmem((nz, 2, k * nx, LANES), F32),
            dma((nz, 2)),
            vmem((k * lines, leaf), BF16),
            vmem(classes.shape, classes.dtype),
            pltpu.SMEM(class_table.shape, F32),
            vmem(weights.shape, F32),
            vmem(prior_block.shape, F32),
            vmem((levels, rank, leaf), F32),
            vmem((levels, rank, leaf), F32),
            pltpu.SMEM(block_ranks.shape, block_ranks.dtype),
            dma((8,)),
            vmem((nz, nx, k, leaf), BF16),
            vmem((nz, nx, leaf), F32),
            vmem((2, k * lines, LANES), F32),
            vmem((2, nz, 2, k, leaf), BF16),
            vmem((6, k, LANES), BF16),
            vmem((6, k, LANES), F32),
            vmem((2, 4 * nz, leaf), F32),
            vmem((6, nx, LANES), F32),
            vmem((2, k, LANES), BF16),
            vmem((2, 4 * nz, leaf), F32),
            vmem((2, nx, LANES), F32),
            dma((16,)),
            dma((16,)),
        ]
        + [field] * 8
        + [
            vmem((nz, nx + 4, k, 3 * LANES), F32),
            vmem((nz, nx + 2, k, 3 * LANES), F32),
            vmem((leaf + LANES, leaf), BF16),
            vmem((2 * k, 3 * k), F32),
            vmem((lines, k, LANES), F32),
            vmem((2 * levels, groups, k, LANES), BF16),
            [
                vmem((2 ** (level + 1) - 1, groups >> level, k, LANES), BF16)
                for level in range(levels)
            ],
            dma((edges,)),
            dma((edges,)),
            vmem((2, 3, k // 2, LANES), F32),
            vmem((2, 3, most, k // 2, LANES), F32),
            dma((2, 3, most)),
            dma((2, 3, most)),
        ],
        compiler_params=params(collective_id=0, has_side_effects=True),
    )(
        probes.reshape(k * lines, leaf), classes, class_table, weights, prior_block, prior_left,
        prior_right, block_ranks,
    )
    pieces = 8
    return pl.pallas_call(
        functools.partial(copy_kernel, pieces),
        out_shape=(shape((k, nz, nx, leaf), F32), shape((k, k), F32)),
        in_specs=[HBM] * 2,
        out_specs=(HBM, HBM),
        scratch_shapes=[
            vmem((k, nz, nx, leaf), F32),
            vmem((k, k), F32),
            dma((pieces + 1,)),
            dma((pieces + 1,)),
        ],
        compiler_params=params(),
    )(basis, projected)


def solution(mesh):
    return jax.shard_map(
        shards,
        mesh=mesh,
        in_specs=(
            P(None, None, "gx", "gy"),
            P(None, "gx", "gy"),
            P(),
            P(None, "gx", "gy"),
            P("gy", None),
            P(None, None, "gy"),
            P(None, None, "gy"),
            P(),
        ),
        out_specs=(P(None, None, "gx", "gy"), P()),
        check_vma=False,
    )
```

```python
import functools

import jax
import jax.numpy as jnp
from jax import lax
from jax.experimental import pallas as pl
from jax.experimental.pallas import tpu as pltpu
from jax.sharding import PartitionSpec as P

MESH = pl.DeviceIdType.MESH
HIGH = lax.Precision.HIGHEST
F32 = jnp.float32
BF16 = jnp.bfloat16
LANES = 128
VMEM = pl.BlockSpec(memory_space=pltpu.VMEM)
SMEM = pl.BlockSpec(memory_space=pltpu.SMEM)
ANY = pl.BlockSpec(memory_space=pl.ANY)
HBM = pl.BlockSpec(memory_space=pltpu.HBM)
NT = (((1,), (1,)), ((), ()))


def signal_all(devices):
    barrier = pltpu.get_barrier_semaphore()
    for device in devices:
        pl.semaphore_signal(barrier, inc=1, device_id=device, device_id_type=MESH)
    return barrier, len(devices)


def remote(src, dst, send, recv, device):
    copy = pltpu.make_async_remote_copy(
        src_ref=src, dst_ref=dst, send_sem=send, recv_sem=recv, device_id=device, device_id_type=MESH
    )
    copy.start()
    return copy


def eliminate(blocks, t):
    inner = lax.broadcasted_iota(jnp.int32, (8, LANES), 0)

    def spread(value):
        return jnp.broadcast_to(value, (8, LANES))

    columns = [spread(blocks[t][:, 8 * t + c : 8 * t + c + 1]) for c in range(8)]
    entry = [[spread(columns[c][r : r + 1, :]) for c in range(r + 1)] for r in range(8)]
    rows = [spread(blocks[t][r : r + 1, :]) for r in range(8)]
    factor = [[None] * 8 for _ in range(8)]
    inverses = []
    for q in range(8):
        inverses.append(1.0 / entry[q][q])
        for r in range(q + 1, 8):
            factor[r][q] = entry[r][q] * inverses[q]
        for r in range(q + 1, 8):
            for c in range(q + 1, r + 1):
                entry[r][c] = entry[r][c] - factor[r][q] * entry[c][q]
    for r in range(8):
        for q in range(r):
            rows[r] = rows[r] - factor[r][q] * rows[q]
    scaled = [rows[q] * inverses[q] for q in range(8)]
    for i in range(t + 1, len(blocks)):
        lefts = [spread(blocks[i][:, 8 * t + q : 8 * t + q + 1]) for q in range(8)]
        for q in range(8):
            for p in range(q):
                lefts[q] = lefts[q] - lefts[p] * factor[q][p]
        changes = [lefts[q] * scaled[q] for q in range(8)]
        while len(changes) > 1:
            changes = [changes[n] + changes[n + 1] for n in range(0, len(changes), 2)]
        blocks[i] = blocks[i] - changes[0]
    done, pivots = rows[0], entry[0][0]
    for r in range(1, 8):
        done = jnp.where(inner == r, rows[r], done)
        pivots = jnp.where(inner == r, entry[r][r], pivots)
    return done, 1.0 / jnp.sqrt(pivots)


def sketch_kernel(
    ng, ny, k, nz, nx, levels, leaf, groups, cells,
    probes_in, classes_in, table_in, weights_in, block_in, left_in, right_in, ranks_in,
    out, projected,
    shl, buffer, store_sem, probes, classes, table, weights, block, left, right, ranks, load_sem,
    pt, cond, pf, xh, hy, hf, cx, cy, hs, cxs, cys, send_sem, recv_sem,
    ce, dg, dd, wd, fx, fyp, fym, fz, f1, a1, wt, acc, cuf, uc,
    trees, tree_send, tree_recv, packed, gathered, sum_send, sum_recv,
):
    gx, gy = lax.axis_index("gx"), lax.axis_index("gy")
    east, west = lax.rem(gx + 1, ng), lax.rem(gx + ng - 1, ng)
    north, south = lax.rem(gy + 1, ny), lax.rem(gy + ny - 1, ny)
    around = [(west, gy), (east, gy)]
    for column in (south, north):
        for row in (west, gx, east):
            around.append((row, column))

    across, pair = min(4, ng), min(2, ny)
    deep, high_y = ng // across, ny // pair
    at_z, at_x = gx // across, lax.rem(gx, across)
    at_y, at_c = gy // pair, lax.rem(gy, pair)
    stages = [
        (
            [
                (
                    at_z * across + lax.rem(at_x + d % across, across),
                    at_y * pair + lax.rem(at_c + d // across, pair),
                )
                for d in range(1, across * pair)
            ],
            at_c * across + at_x,
        ),
        ([(lax.rem(at_z + d, deep) * across + at_x, gy) for d in range(1, deep)], at_z),
        ([(gx, lax.rem(at_y + d, high_y) * pair + at_c) for d in range(1, high_y)], at_y),
    ]
    column = [(gx, lax.rem(gy + d, ny)) for d in range(1, ny)]
    loads = [
        pltpu.make_async_copy(source, target, load_sem.at[i])
        for i, (source, target) in enumerate(
            [
                (classes_in, classes),
                (weights_in, weights),
                (table_in, table),
                (probes_in, probes),
                (block_in, block),
                (left_in.at[0:levels], left),
                (right_in.at[0:levels], right),
                (ranks_in, ranks),
            ]
        )
    ]
    for load in loads:
        load.start()
    barrier, count = signal_all(around + stages[0][0] + stages[1][0] + column)

    lines = nz * nx
    for load in loads[:3]:
        load.wait()

    for z in range(nz):
        picked = classes[z]
        value = jnp.zeros(picked.shape, F32)
        for index in range(table.shape[0]):
            value = jnp.where(picked == index, table[index], value)
        cond[z] = value
        cxs[0, 4 * z : 4 * z + 3, :] = value[0:3, :]
        cxs[1, 4 * z : 4 * z + 3, :] = value[nx - 3 : nx, :]
        cxs[0, 4 * z + 3 : 4 * z + 4, :] = weights[z, 0:1, :]
        cxs[1, 4 * z + 3 : 4 * z + 4, :] = weights[z, nx - 1 : nx, :]
    lane = lax.broadcasted_iota(jnp.int32, (nx, LANES), 1)
    low = jnp.zeros((nx, LANES), F32)
    high = jnp.zeros((nx, LANES), F32)
    for z in range(nz):
        here = lane // 4 == z
        last = lane % 4 == 3
        first_tile, last_tile = cond[z, :, :LANES], cond[z, :, LANES:]
        w_first, w_last = weights[z, :, :LANES], weights[z, :, LANES:]
        own = jnp.where(last, pltpu.roll(w_first, 4 * z + 3, 1), pltpu.roll(first_tile, 4 * z, 1))
        low = jnp.where(here, own, low)
        own = jnp.where(last, pltpu.roll(w_last, 4 * z + 4, 1), pltpu.roll(last_tile, 4 * z + 3, 1))
        high = jnp.where(here, own, high)
    cys[0] = low
    cys[1] = high

    pl.semaphore_wait(barrier, count)
    field_copies = [
        remote(cxs.at[1], cx.at[0], send_sem.at[2], recv_sem.at[2], (east, gy)),
        remote(cxs.at[0], cx.at[1], send_sem.at[3], recv_sem.at[3], (west, gy)),
    ]
    probe_copies = []
    arrivals = [
        (side, which, row, column)
        for side, column in ((0, north), (1, south))
        for which, row in ((2, west), (1, gx), (0, east))
    ]
    for i, (side, which, row, column) in enumerate(arrivals):
        slot = side * 3 + which
        field_copies.append(
            remote(
                cys.at[1 - side], cy.at[slot], send_sem.at[4 + i], recv_sem.at[4 + i], (row, column)
            )
        )
    loads[3].wait()
    chunk = 512

    def widen(i, carry):
        rows = pl.ds(pl.multiple_of(i * chunk, chunk), chunk)
        value = probes[rows, :].astype(F32)
        pf[0, rows, :] = value[:, :LANES]
        pf[1, rows, :] = value[:, LANES:]
        return carry

    lax.fori_loop(0, k * lines // chunk, widen, 0)

    place = lax.broadcasted_iota(jnp.int32, (k, LANES), 1) // 2

    def turn(line, carry):
        low, high = carry
        lo = pf[0, pl.ds(line, k, stride=lines), :]
        hi = pf[1, pl.ds(line, k, stride=lines), :]
        pt[line // nx, lax.rem(line, nx)] = jnp.concatenate([lo, hi], axis=1).astype(BF16)
        low = jnp.where(place == line, pltpu.roll(lo, 2 * line, 1), low)
        high = jnp.where(place == line, pltpu.roll(hi, lax.rem(2 * line + 2, LANES), 1), high)
        return low, high

    zero = jnp.zeros((k, LANES), F32)
    low, high = lax.fori_loop(0, lines, turn, (zero, zero), unroll=4)
    hs[0] = low.astype(BF16)
    hs[1] = high.astype(BF16)

    for i, (side, which, row, column) in enumerate(arrivals):
        slot = side * 3 + which
        probe_copies.append(
            remote(
                hs.at[1 - side], hy.at[slot], send_sem.at[10 + i], recv_sem.at[10 + i], (row, column)
            )
        )
    probe_copies += [
        remote(pt.at[:, nx - 2 : nx], xh.at[0], send_sem.at[0], recv_sem.at[0], (east, gy)),
        remote(pt.at[:, 0:2], xh.at[1], send_sem.at[1], recv_sem.at[1], (west, gy)),
    ]

    has_west = (gx > 0).astype(F32)
    has_east = (gx < ng - 1).astype(F32)
    has_south = (gy > 0).astype(F32)
    has_north = (gy < ny - 1).astype(F32)
    has_x = (has_west, 1.0, has_east)
    has_y = (has_south, has_north)
    rank = left.shape[1]
    for load in loads[4:]:
        load.wait()

    wt[0:leaf, :] = block[...].astype(BF16)
    row = lax.broadcasted_iota(jnp.int32, (rank, leaf), 0)
    for level in range(levels):
        gain = jnp.where(row < ranks[level], float(leaf * 2**level) ** -0.5, 0.0)
        at = leaf + 2 * level * rank
        wt[at : at + rank, :] = (right[level] * gain).astype(BF16)
        wt[at + rank : at + 2 * rank, :] = left[level].astype(BF16)

    for copy in field_copies:
        copy.wait_recv()

    tall = nx + 16
    wide = 3 * LANES
    lane = lax.broadcasted_iota(jnp.int32, (nx, LANES), 1)
    for z in range(nz):
        ce[z] = jnp.zeros((tall, wide), F32)
        wd[z] = jnp.zeros((tall, wide), F32)
        ce[z, 8 : 8 + nx, 0 : 2 * LANES] = cond[z]
        wd[z, 8 : 8 + nx, 0 : 2 * LANES] = weights[z]
        ce[z, 5:8, 0 : 2 * LANES] = cx[0, 4 * z : 4 * z + 3, :] * has_west
        wd[z, 7:8, 0 : 2 * LANES] = cx[0, 4 * z + 3 : 4 * z + 4, :] * has_west
        ce[z, 8 + nx : 11 + nx, 0 : 2 * LANES] = cx[1, 4 * z : 4 * z + 3, :] * has_east
        wd[z, 8 + nx : 9 + nx, 0 : 2 * LANES] = cx[1, 4 * z + 3 : 4 * z + 4, :] * has_east
        for which in range(3):
            above = cy[3 + which] * (has_x[which] * has_y[1])
            below = cy[which] * (has_x[which] * has_y[0])
            value = jnp.where(lane < 3, pltpu.roll(above, (LANES - 4 * z) % LANES, 1), 0.0)
            value = jnp.where(lane > LANES - 4, pltpu.roll(below, LANES - 3 - 4 * z, 1), value)
            if which == 0:
                ce[z, 0:8, 2 * LANES :] = value[nx - 8 :, :]
            elif which == 2:
                ce[z, 8 + nx :, 2 * LANES :] = value[:8, :]
            else:
                ce[z, 8 : 8 + nx, 2 * LANES :] = value
                value = jnp.where(lane == 0, pltpu.roll(above, LANES - 3 - 4 * z, 1), 0.0)
                value = jnp.where(lane == LANES - 1, pltpu.roll(below, LANES - 4 - 4 * z, 1), value)
                wd[z, 8 : 8 + nx, 2 * LANES :] = value
    for z in range(nz):
        centre = ce[z]
        upper = ce[z + 1] if z + 1 < nz else jnp.zeros_like(centre)
        lower = ce[z - 1] if z > 0 else jnp.zeros_like(centre)
        face_x = 0.5 * (centre + pltpu.roll(centre, tall - 1, 0))
        face_y = 0.5 * (centre + pltpu.roll(centre, wide - 1, 1))
        back_y = pltpu.roll(face_y, 1, 1)
        face_z = 0.5 * (centre + upper)
        total = 1.0 + face_x + pltpu.roll(face_x, 1, 0) + face_y + back_y
        total = total + face_z + 0.5 * (centre + lower)
        inverse = 1.0 / total
        fx[z] = face_x
        fyp[z] = face_y
        fym[z] = back_y
        fz[z] = face_z
        dg[z] = total
        dd[z] = inverse
        wd[z] = wd[z] * inverse

    tile_lane = lax.broadcasted_iota(jnp.int32, (k, LANES), 1)

    def tiles(ref, z, x):
        whole = ref[z, pl.ds(x + 8, 1), :]
        return [whole[:, i * LANES : (i + 1) * LANES] for i in range(3)]

    def split(value):
        return [value[:, i * LANES : (i + 1) * LANES] for i in range(value.shape[1] // LANES)]

    def store(ref, z, x, parts):
        for i in range(len(parts)):
            ref[z, x, :, i * LANES : (i + 1) * LANES] = parts[i]

    def edge_tile(z, x, which):
        line = z * nx + x
        above = pltpu.roll(hf[3 + which], lax.rem(LANES - 2 * line + LANES, LANES), 1)
        below = pltpu.roll(hf[which], lax.rem(2 * LANES - 2 - 2 * line, LANES), 1)
        return jnp.where(tile_lane < LANES // 2, above, below)

    def inner_tiles(z, x, value):
        inverse = tiles(dd, z, x)
        parts = split(value)
        store(f1, z, x + 2, [parts[i] * inverse[i] for i in range(2)])

    def edge_tiles(z, x, edge):
        f1[z, x + 2, :, 2 * LANES :] = edge * tiles(dd, z, x)[2]

    def forward_inner(x, carry):
        for z in range(nz):
            inner_tiles(z, x, pt[z, x].astype(F32))
        return carry

    lax.fori_loop(0, nx, forward_inner, 0)
    for copy in probe_copies[:6]:
        copy.wait_recv()

    for which in range(3):
        hf[which] = hy[which].astype(F32) * (has_x[which] * has_y[0])
        hf[3 + which] = hy[3 + which].astype(F32) * (has_x[which] * has_y[1])

    def forward_edges(x, carry):
        for z in range(nz):
            edge_tiles(z, x, edge_tile(z, x, 1))
        return carry

    lax.fori_loop(0, nx, forward_edges, 0)
    def near(ref, z, x, row, count):
        centre = split(ref[z, row])
        ahead = [pltpu.roll(part, LANES - 1, 1) for part in centre]
        behind = [pltpu.roll(part, 1, 1) for part in centre]
        east, west = split(ref[z, row + 1]), split(ref[z, row - 1])
        face_e, face_w = tiles(fx, z, x), tiles(fx, z, x - 1)
        face_n, face_s = tiles(fyp, z, x), tiles(fym, z, x)
        if z + 1 < nz:
            upper, face_u = split(ref[z + 1, row]), tiles(fz, z, x)
        if z > 0:
            lower, face_d = split(ref[z - 1, row]), tiles(fz, z - 1, x)
        sums = []
        for i in range(count):
            north = jnp.where(tile_lane == LANES - 1, ahead[(i + 1) % 3], ahead[i])
            south = jnp.where(tile_lane == 0, behind[(i + 2) % 3], behind[i])
            total = face_e[i] * east[i] + face_w[i] * west[i]
            total = total + (face_n[i] * north + face_s[i] * south)
            if z + 1 < nz:
                total = total + face_u[i] * upper[i]
            if z > 0:
                total = total + face_d[i] * lower[i]
            sums.append(total)
        return centre, sums

    def adjoint(i, carry):
        x = i - 1
        for z in range(nz):
            centre, sums = near(f1, z, x, x + 2, 3)
            diagonal, inverse, gain = tiles(dg, z, x), tiles(dd, z, x), tiles(wd, z, x)
            parts = [
                (centre[i] * diagonal[i] + sums[i]) * gain[i] * inverse[i] for i in range(3)
            ]
            store(a1, z, x + 1, parts)
        return carry

    acc[...] = jnp.zeros_like(acc)

    def finish(x):
        for z in range(nz):
            centre, sums = near(a1, z, x, x + 1, 2)
            diagonal, inverse = tiles(dg, z, x), tiles(dd, z, x)
            source = split(pt[z, x].astype(F32))
            sketch = jnp.concatenate(
                [
                    (centre[i] * diagonal[i] + sums[i]) * inverse[i] + source[i]
                    for i in range(2)
                ],
                axis=1,
            )
            high = sketch.astype(BF16)
            shl[z * nx + x, 0:k, :] = high
            shl[z * nx + x, k : 2 * k, :] = (sketch - high.astype(F32)).astype(BF16)

    def products(x, slot, apart):
        whole = [shl[z * nx + x] for z in range(nz)]
        applied = lax.dot_general(
            jnp.concatenate([part[0:k] for part in whole], axis=0),
            wt[...],
            NT,
            preferred_element_type=F32,
        )
        rows = []
        for z in range(nz):
            part = applied[z * k : (z + 1) * k]
            cuf[slot + z * apart] = part[:, leaf:]
            rows.append(part[:, :leaf].astype(BF16))
        lhs = jnp.concatenate(whole, axis=1)
        rhs = jnp.concatenate([lhs, jnp.concatenate(rows, axis=1)], axis=0)
        acc[...] += lax.dot_general(lhs, rhs, NT, preferred_element_type=F32)

    lax.fori_loop(2, nx, adjoint, 0)
    inner_rows = nx - 4
    early = nz * inner_rows // (LANES // rank)

    def finish_inner(x, carry):
        products(x - 1, x - 3, inner_rows)
        finish(x)
        return carry

    finish(2)
    lax.fori_loop(3, nx - 2, finish_inner, 0)
    products(nx - 3, nx - 5, inner_rows)

    count = LANES // rank
    slot = tile_lane // rank

    def gather(group, carry):
        parts = [cuf[group * count + j] for j in range(count)]
        step = 1
        while step < count:
            bit = (slot // step) % 2 == 0
            for i in range(count):
                if (i // step) % 2 == 0:
                    one, two = parts[i], parts[i + step]
                    parts[i] = jnp.where(bit, one, pltpu.roll(two, step * rank, 1))
                    parts[i + step] = jnp.where(bit, pltpu.roll(one, LANES - step * rank, 1), two)
            step *= 2
        for index in range(2 * levels):
            uc[index, group] = parts[index].astype(BF16)
        return carry

    lax.fori_loop(0, early, gather, 0)

    def flipped(bits):
        device = gy
        for b in range(levels):
            if bits >> b & 1:
                device = device + (1 - 2 * lax.rem(device // 2**b, 2)) * 2**b
        return device

    tree = []
    for level in range(levels):
        half = 2**level
        share = groups // half
        for bits in range(1, 2 * half):
            peer = flipped(bits)
            kind = 2 * level + (1 if bits < half else 0)
            begin = lax.rem(peer, half) * share
            copy = pltpu.make_async_remote_copy(
                src_ref=uc.at[kind, pl.ds(begin, share)],
                dst_ref=trees[level].at[bits - 1],
                send_sem=tree_send.at[2 * half - 2 - level + bits],
                recv_sem=tree_recv.at[2 * half - 2 - level + bits],
                device_id=(gx, peer),
                device_id_type=MESH,
            )
            tree.append((copy, lax.rem(peer, half) < early // share, early < share))

    for copy, ready, never in tree:
        if not never:
            pl.when(ready)(copy.start)
    for copy in probe_copies[6:]:
        copy.wait_recv()
    for z in range(nz):
        for i in range(2):
            inner_tiles(z, i - 2, xh[0, z, i].astype(F32) * has_west)
            edge_tiles(z, i - 2, edge_tile(z, nx - 2 + i, 0))
            inner_tiles(z, nx + i, xh[1, z, i].astype(F32) * has_east)
            edge_tiles(z, nx + i, edge_tile(z, i, 2))

    def adjoint_outer(i, carry):
        return adjoint(jnp.where(i < 2, i, nx - 2 + i), carry)

    def outer_row(i):
        return jnp.where(i < 2, i, nx - 4 + i)

    def finish_outer(i, carry):
        products(outer_row(i - 1), nz * inner_rows + i - 1, 4)
        finish(outer_row(i))
        return carry

    lax.fori_loop(0, 4, adjoint_outer, 0)
    finish(0)
    lax.fori_loop(1, 4, finish_outer, 0)
    products(nx - 1, nz * inner_rows + 3, 4)

    half_k, half_lanes = k // 2, LANES // 2
    half_lane = lax.broadcasted_iota(jnp.int32, (half_k, LANES), 1)
    pad = jnp.zeros((k, LANES - k), F32)

    def fold(value):
        value = jnp.concatenate([value, pad], axis=1)
        return value[:half_k] + pltpu.roll(value[half_k:], half_lanes, 1)

    def unfold(value):
        first = jnp.where(half_lane < half_lanes, value, 0.0)
        second = pltpu.roll(jnp.where(half_lane < half_lanes, 0.0, value), half_lanes, 1)
        return jnp.concatenate([first, second], axis=0) * (1.0 / cells)

    pending = []

    def send(which, stage, value):
        peers, me = stages[stage]
        packed[which, stage] = value
        gathered[which, stage, me] = value
        copies = [
            remote(
                packed.at[which, stage], gathered.at[which, stage, me],
                sum_send.at[which, stage, d], sum_recv.at[which, stage, d], peer,
            )
            for d, peer in enumerate(peers)
        ]
        pending.extend(copies)
        return copies

    def receive(which, stage, copies):
        for copy in copies:
            copy.wait_recv()
        parts = [gathered[which, stage, i] for i in range(len(copies) + 1)]
        while len(parts) > 1:
            parts = [
                parts[i] + parts[i + 1] if i + 1 < len(parts) else parts[i]
                for i in range(0, len(parts), 2)
            ]
        return parts[0]

    value = acc[...]
    total = value[0:k, 0:k] + (value[0:k, k : 2 * k] + value[k : 2 * k, 0:k]) + value[k:, k : 2 * k]
    first = send(0, 0, fold(total))
    leafpart = value[0:k, 2 * k :] + value[k:, 2 * k :]

    lax.fori_loop(early, groups, gather, 0)
    for copy, ready, never in tree:
        if never:
            copy.start()
        else:
            pl.when(jnp.logical_not(ready))(copy.start)

    first = send(0, 1, receive(0, 0, first))
    for copy, _, _ in tree:
        copy.wait_recv()
    lefts, rights = [], []
    for level in range(levels):
        half = 2**level
        share = groups // half
        begin = lax.rem(gy, half) * share
        for j in range(share):
            own = uc[2 * level + 1, begin + j].astype(F32)
            for bits in range(1, half):
                own = own + trees[level][bits - 1, j].astype(F32)
            other = trees[level][half - 1, j].astype(F32)
            for bits in range(half + 1, 2 * half):
                other = other + trees[level][bits - 1, j].astype(F32)
            lefts.append(own.astype(BF16))
            rights.append(other.astype(BF16))
    total = leafpart + lax.dot_general(
        jnp.concatenate(lefts, axis=1),
        jnp.concatenate(rights, axis=1),
        NT,
        preferred_element_type=F32,
    )
    second = send(1, 0, fold(total))
    first = send(0, 2, receive(0, 1, first))
    second = send(1, 1, receive(1, 0, second))
    matrix = unfold(receive(0, 2, first))

    row = lax.broadcasted_iota(jnp.int32, (k, LANES), 0)
    lane = lax.broadcasted_iota(jnp.int32, (k, LANES), 1)
    start = LANES // 2
    whole = jnp.where(lane < k, matrix, jnp.where(lane == row + start, 1.0, 0.0))
    blocks = [whole[8 * t : 8 * t + 8] for t in range(k // 8)]
    inverse = []
    for t in range(k // 8):
        done, scale = eliminate(blocks, t)
        inverse.append(done[:, start : start + k] * scale[:, 0:k])
        if t == k // 16:
            second = send(1, 2, receive(1, 1, second))
    inverse = jnp.concatenate(inverse, axis=0)

    high = inverse.astype(BF16)
    low = (inverse - high.astype(F32)).astype(BF16)
    lhs = jnp.concatenate(
        [
            jnp.concatenate([high, high], axis=1),
            jnp.concatenate([low, jnp.zeros_like(low)], axis=1),
        ],
        axis=0,
    )
    stores = []
    for z in range(nz):

        def one(x, carry):
            value = jnp.dot(lhs, shl[z * nx + x], preferred_element_type=F32)
            value = value[0:k] + value[k:]
            buffer[z, 0, pl.ds(x, k, stride=nx), :] = value[:, :LANES]
            buffer[z, 1, pl.ds(x, k, stride=nx), :] = value[:, LANES:]
            return carry

        lax.fori_loop(0, nx, one, 0, unroll=8)
        for i in range(2):
            copy = pltpu.make_async_copy(
                buffer.at[z, i].reshape(k, nx, LANES),
                out.at[:, z, :, i * LANES : (i + 1) * LANES],
                store_sem.at[z, i],
            )
            copy.start()
            stores.append(copy)
    middle = unfold(receive(1, 2, second))[:, 0:k]
    product = jnp.dot(inverse, middle, precision=HIGH, preferred_element_type=F32)
    product = lax.dot_general(product, inverse, NT, precision=HIGH, preferred_element_type=F32)
    projected[...] = product + jnp.where(lane[:, 0:k] == row[:, 0:k], 1.0, 0.0)
    for copy in field_copies + probe_copies + [copy for copy, _, _ in tree] + pending:
        copy.wait_send()
    for copy in stores:
        copy.wait()


def copy_kernel(pieces, basis_in, projected_in, basis, projected, wide, small, load_sem, store_sem):
    size = basis.shape[0] // pieces
    parts = [pl.ds(i * size, size) for i in range(pieces)]
    loads = [
        pltpu.make_async_copy(basis_in.at[part], wide.at[part], load_sem.at[i])
        for i, part in enumerate(parts)
    ]
    loads.insert(1, pltpu.make_async_copy(projected_in, small, load_sem.at[pieces]))
    stores = [
        pltpu.make_async_copy(wide.at[part], basis.at[part], store_sem.at[i])
        for i, part in enumerate(parts)
    ]
    stores.insert(1, pltpu.make_async_copy(small, projected, store_sem.at[pieces]))
    for load in loads:
        load.start()
    for load, store in zip(loads, stores):
        load.wait()
        store.start()
    for store in stores:
        store.wait()


def params(**more):
    return pltpu.CompilerParams(vmem_limit_bytes=56 * 2**20, **more)


def shards(
    probes, classes, class_table, weights, prior_block, prior_left, prior_right, block_ranks
):
    ng, ny = lax.axis_size("gx"), lax.axis_size("gy")
    k, nz, nx, leaf = probes.shape
    levels = ny.bit_length() - 1
    rank = prior_left.shape[1]
    lines = nz * nx
    groups = lines * rank // LANES
    cells = float(nz * nx * leaf * ng * ny)
    shape = jax.ShapeDtypeStruct
    dma = pltpu.SemaphoreType.DMA
    vmem = pltpu.VMEM
    edges = 2 * ny
    most = 8
    while most < max(ng // min(4, ng), ny // min(2, ny)):
        most *= 2

    field = vmem((nz, nx + 16, 3 * LANES), F32)
    basis, projected = pl.pallas_call(
        functools.partial(
            sketch_kernel, ng, ny, k, nz, nx, levels, leaf, groups, cells
        ),
        out_shape=(
            shape((k, nz, nx, leaf), F32),
            shape((k, k), F32),
        ),
        in_specs=[HBM] * 8,
        out_specs=(HBM, VMEM),
        scratch_shapes=[
            vmem((lines, 2 * k, leaf), BF16),
            vmem((nz, 2, k * nx, LANES), F32),
            dma((nz, 2)),
            vmem((k * lines, leaf), BF16),
            vmem(classes.shape, classes.dtype),
            pltpu.SMEM(class_table.shape, F32),
            vmem(weights.shape, F32),
            vmem(prior_block.shape, F32),
            vmem((levels, rank, leaf), F32),
            vmem((levels, rank, leaf), F32),
            pltpu.SMEM(block_ranks.shape, block_ranks.dtype),
            dma((8,)),
            vmem((nz, nx, k, leaf), BF16),
            vmem((nz, nx, leaf), F32),
            vmem((2, k * lines, LANES), F32),
            vmem((2, nz, 2, k, leaf), BF16),
            vmem((6, k, LANES), BF16),
            vmem((6, k, LANES), F32),
            vmem((2, 4 * nz, leaf), F32),
            vmem((6, nx, LANES), F32),
            vmem((2, k, LANES), BF16),
            vmem((2, 4 * nz, leaf), F32),
            vmem((2, nx, LANES), F32),
            dma((16,)),
            dma((16,)),
        ]
        + [field] * 8
        + [
            vmem((nz, nx + 4, k, 3 * LANES), F32),
            vmem((nz, nx + 2, k, 3 * LANES), F32),
            vmem((leaf + LANES, leaf), BF16),
            vmem((2 * k, 3 * k), F32),
            vmem((lines, k, LANES), F32),
            vmem((2 * levels, groups, k, LANES), BF16),
            [
                vmem((2 ** (level + 1) - 1, groups >> level, k, LANES), BF16)
                for level in range(levels)
            ],
            dma((edges,)),
            dma((edges,)),
            vmem((2, 3, k // 2, LANES), F32),
            vmem((2, 3, most, k // 2, LANES), F32),
            dma((2, 3, most)),
            dma((2, 3, most)),
        ],
        compiler_params=params(collective_id=0, has_side_effects=True),
    )(
        probes.reshape(k * lines, leaf), classes, class_table, weights, prior_block, prior_left,
        prior_right, block_ranks,
    )
    pieces = 8
    return pl.pallas_call(
        functools.partial(copy_kernel, pieces),
        out_shape=(shape((k, nz, nx, leaf), F32), shape((k, k), F32)),
        in_specs=[HBM] * 2,
        out_specs=(HBM, HBM),
        scratch_shapes=[
            vmem((k, nz, nx, leaf), F32),
            vmem((k, k), F32),
            dma((pieces + 1,)),
            dma((pieces + 1,)),
        ],
        compiler_params=params(),
    )(basis, projected)


def solution(mesh):
    return jax.shard_map(
        shards,
        mesh=mesh,
        in_specs=(
            P(None, None, "gx", "gy"),
            P(None, "gx", "gy"),
            P(),
            P(None, "gx", "gy"),
            P("gy", None),
            P(None, None, "gy"),
            P(None, None, "gy"),
            P(),
        ),
        out_specs=(P(None, None, "gx", "gy"), P()),
        check_vma=False,
    )
```

```python
import functools

import jax
import jax.numpy as jnp
from jax import lax
from jax.experimental import pallas as pl
from jax.experimental.pallas import tpu as pltpu
from jax.sharding import PartitionSpec as P

MESH = pl.DeviceIdType.MESH
HIGH = lax.Precision.HIGHEST
F32 = jnp.float32
BF16 = jnp.bfloat16
LANES = 128
VMEM = pl.BlockSpec(memory_space=pltpu.VMEM)
SMEM = pl.BlockSpec(memory_space=pltpu.SMEM)
ANY = pl.BlockSpec(memory_space=pl.ANY)
HBM = pl.BlockSpec(memory_space=pltpu.HBM)
NT = (((1,), (1,)), ((), ()))


def signal_all(devices):
    barrier = pltpu.get_barrier_semaphore()
    for device in devices:
        pl.semaphore_signal(barrier, inc=1, device_id=device, device_id_type=MESH)
    return barrier, len(devices)


def remote(src, dst, send, recv, device):
    copy = pltpu.make_async_remote_copy(
        src_ref=src, dst_ref=dst, send_sem=send, recv_sem=recv, device_id=device, device_id_type=MESH
    )
    copy.start()
    return copy


def eliminate(blocks, t):
    inner = lax.broadcasted_iota(jnp.int32, (8, LANES), 0)

    def spread(value):
        return jnp.broadcast_to(value, (8, LANES))

    columns = [spread(blocks[t][:, 8 * t + c : 8 * t + c + 1]) for c in range(8)]
    entry = [[spread(columns[c][r : r + 1, :]) for c in range(r + 1)] for r in range(8)]
    rows = [spread(blocks[t][r : r + 1, :]) for r in range(8)]
    factor = [[None] * 8 for _ in range(8)]
    inverses = []
    for q in range(8):
        inverses.append(1.0 / entry[q][q])
        for r in range(q + 1, 8):
            factor[r][q] = entry[r][q] * inverses[q]
        for r in range(q + 1, 8):
            for c in range(q + 1, r + 1):
                entry[r][c] = entry[r][c] - factor[r][q] * entry[c][q]
    for r in range(8):
        for q in range(r):
            rows[r] = rows[r] - factor[r][q] * rows[q]
    scaled = [rows[q] * inverses[q] for q in range(8)]
    for i in range(t + 1, len(blocks)):
        lefts = [spread(blocks[i][:, 8 * t + q : 8 * t + q + 1]) for q in range(8)]
        for q in range(8):
            for p in range(q):
                lefts[q] = lefts[q] - lefts[p] * factor[q][p]
        changes = [lefts[q] * scaled[q] for q in range(8)]
        while len(changes) > 1:
            changes = [changes[n] + changes[n + 1] for n in range(0, len(changes), 2)]
        blocks[i] = blocks[i] - changes[0]
    done, pivots = rows[0], entry[0][0]
    for r in range(1, 8):
        done = jnp.where(inner == r, rows[r], done)
        pivots = jnp.where(inner == r, entry[r][r], pivots)
    return done, 1.0 / jnp.sqrt(pivots)


def sketch_kernel(
    ng, ny, k, nz, nx, levels, leaf, groups, cells,
    probes_in, classes_in, table_in, weights_in, block_in, left_in, right_in, ranks_in,
    out, projected,
    shl, buffer, store_sem, probes, classes, table, weights, block, left, right, ranks, load_sem,
    pt, cond, pf, xh, hy, hf, cx, cy, hs, cxs, cys, send_sem, recv_sem,
    ce, dg, dd, wd, fx, fyp, fym, fz, f1, a1, wt, acc, cuf, uc,
    trees, tree_send, tree_recv, packed, gathered, sum_send, sum_recv,
):
    gx, gy = lax.axis_index("gx"), lax.axis_index("gy")
    east, west = lax.rem(gx + 1, ng), lax.rem(gx + ng - 1, ng)
    north, south = lax.rem(gy + 1, ny), lax.rem(gy + ny - 1, ny)
    around = [(west, gy), (east, gy)]
    for column in (south, north):
        for row in (west, gx, east):
            around.append((row, column))

    across, pair = min(4, ng), min(2, ny)
    deep, high_y = ng // across, ny // pair
    at_z, at_x = gx // across, lax.rem(gx, across)
    at_y, at_c = gy // pair, lax.rem(gy, pair)
    stages = [
        (
            [
                (
                    at_z * across + lax.rem(at_x + d % across, across),
                    at_y * pair + lax.rem(at_c + d // across, pair),
                )
                for d in range(1, across * pair)
            ],
            at_c * across + at_x,
        ),
        ([(lax.rem(at_z + d, deep) * across + at_x, gy) for d in range(1, deep)], at_z),
        ([(gx, lax.rem(at_y + d, high_y) * pair + at_c) for d in range(1, high_y)], at_y),
    ]
    column = [(gx, lax.rem(gy + d, ny)) for d in range(1, ny)]
    loads = [
        pltpu.make_async_copy(source, target, load_sem.at[i])
        for i, (source, target) in enumerate(
            [
                (classes_in, classes),
                (weights_in, weights),
                (table_in, table),
                (probes_in, probes),
                (block_in, block),
                (left_in.at[0:levels], left),
                (right_in.at[0:levels], right),
                (ranks_in, ranks),
            ]
        )
    ]
    for load in loads:
        load.start()
    barrier, count = signal_all(around + stages[0][0] + stages[1][0] + column)

    lines = nz * nx
    for load in loads[:3]:
        load.wait()

    for z in range(nz):
        picked = classes[z]
        value = jnp.zeros(picked.shape, F32)
        for index in range(table.shape[0]):
            value = jnp.where(picked == index, table[index], value)
        cond[z] = value
        cxs[0, 4 * z : 4 * z + 3, :] = value[0:3, :]
        cxs[1, 4 * z : 4 * z + 3, :] = value[nx - 3 : nx, :]
        cxs[0, 4 * z + 3 : 4 * z + 4, :] = weights[z, 0:1, :]
        cxs[1, 4 * z + 3 : 4 * z + 4, :] = weights[z, nx - 1 : nx, :]
    lane = lax.broadcasted_iota(jnp.int32, (nx, LANES), 1)
    low = jnp.zeros((nx, LANES), F32)
    high = jnp.zeros((nx, LANES), F32)
    for z in range(nz):
        here = lane // 4 == z
        last = lane % 4 == 3
        first_tile, last_tile = cond[z, :, :LANES], cond[z, :, LANES:]
        w_first, w_last = weights[z, :, :LANES], weights[z, :, LANES:]
        own = jnp.where(last, pltpu.roll(w_first, 4 * z + 3, 1), pltpu.roll(first_tile, 4 * z, 1))
        low = jnp.where(here, own, low)
        own = jnp.where(last, pltpu.roll(w_last, 4 * z + 4, 1), pltpu.roll(last_tile, 4 * z + 3, 1))
        high = jnp.where(here, own, high)
    cys[0] = low
    cys[1] = high

    loads[3].wait()
    chunk = 512

    def widen(i, carry):
        rows = pl.ds(pl.multiple_of(i * chunk, chunk), chunk)
        value = probes[rows, :].astype(F32)
        pf[0, rows, :] = value[:, :LANES]
        pf[1, rows, :] = value[:, LANES:]
        return carry

    lax.fori_loop(0, k * lines // chunk, widen, 0)

    place = lax.broadcasted_iota(jnp.int32, (k, LANES), 1) // 2

    def turn(line, carry):
        low, high = carry
        lo = pf[0, pl.ds(line, k, stride=lines), :]
        hi = pf[1, pl.ds(line, k, stride=lines), :]
        pt[line // nx, lax.rem(line, nx)] = jnp.concatenate([lo, hi], axis=1).astype(BF16)
        low = jnp.where(place == line, pltpu.roll(lo, 2 * line, 1), low)
        high = jnp.where(place == line, pltpu.roll(hi, lax.rem(2 * line + 2, LANES), 1), high)
        return low, high

    zero = jnp.zeros((k, LANES), F32)
    low, high = lax.fori_loop(0, lines, turn, (zero, zero), unroll=4)
    hs[0] = low.astype(BF16)
    hs[1] = high.astype(BF16)

    pl.semaphore_wait(barrier, count)
    field_copies = [
        remote(cxs.at[1], cx.at[0], send_sem.at[2], recv_sem.at[2], (east, gy)),
        remote(cxs.at[0], cx.at[1], send_sem.at[3], recv_sem.at[3], (west, gy)),
    ]
    probe_copies = []
    used = 4
    arrivals = [
        (side, which, row, column)
        for side, column in ((0, north), (1, south))
        for which, row in ((2, west), (1, gx), (0, east))
    ]
    for i, (side, which, row, column) in enumerate(arrivals):
        slot = side * 3 + which
        field_copies.append(
            remote(
                cys.at[1 - side], cy.at[slot], send_sem.at[4 + i], recv_sem.at[4 + i], (row, column)
            )
        )
    for i, (side, which, row, column) in enumerate(arrivals):
        slot = side * 3 + which
        probe_copies.append(
            remote(
                hs.at[1 - side], hy.at[slot], send_sem.at[10 + i], recv_sem.at[10 + i], (row, column)
            )
        )
    probe_copies += [
        remote(pt.at[:, nx - 2 : nx], xh.at[0], send_sem.at[0], recv_sem.at[0], (east, gy)),
        remote(pt.at[:, 0:2], xh.at[1], send_sem.at[1], recv_sem.at[1], (west, gy)),
    ]

    has_west = (gx > 0).astype(F32)
    has_east = (gx < ng - 1).astype(F32)
    has_south = (gy > 0).astype(F32)
    has_north = (gy < ny - 1).astype(F32)
    has_x = (has_west, 1.0, has_east)
    has_y = (has_south, has_north)
    rank = left.shape[1]
    for load in loads[4:]:
        load.wait()

    wt[0:leaf, :] = block[...].astype(BF16)
    row = lax.broadcasted_iota(jnp.int32, (rank, leaf), 0)
    for level in range(levels):
        gain = jnp.where(row < ranks[level], float(leaf * 2**level) ** -0.5, 0.0)
        at = leaf + 2 * level * rank
        wt[at : at + rank, :] = (right[level] * gain).astype(BF16)
        wt[at + rank : at + 2 * rank, :] = left[level].astype(BF16)

    for copy in field_copies:
        copy.wait_recv()

    tall = nx + 16
    wide = 3 * LANES
    lane = lax.broadcasted_iota(jnp.int32, (nx, LANES), 1)
    for z in range(nz):
        ce[z] = jnp.zeros((tall, wide), F32)
        wd[z] = jnp.zeros((tall, wide), F32)
        ce[z, 8 : 8 + nx, 0 : 2 * LANES] = cond[z]
        wd[z, 8 : 8 + nx, 0 : 2 * LANES] = weights[z]
        ce[z, 5:8, 0 : 2 * LANES] = cx[0, 4 * z : 4 * z + 3, :] * has_west
        wd[z, 7:8, 0 : 2 * LANES] = cx[0, 4 * z + 3 : 4 * z + 4, :] * has_west
        ce[z, 8 + nx : 11 + nx, 0 : 2 * LANES] = cx[1, 4 * z : 4 * z + 3, :] * has_east
        wd[z, 8 + nx : 9 + nx, 0 : 2 * LANES] = cx[1, 4 * z + 3 : 4 * z + 4, :] * has_east
        for which in range(3):
            above = cy[3 + which] * (has_x[which] * has_y[1])
            below = cy[which] * (has_x[which] * has_y[0])
            value = jnp.where(lane < 3, pltpu.roll(above, (LANES - 4 * z) % LANES, 1), 0.0)
            value = jnp.where(lane > LANES - 4, pltpu.roll(below, LANES - 3 - 4 * z, 1), value)
            if which == 0:
                ce[z, 0:8, 2 * LANES :] = value[nx - 8 :, :]
            elif which == 2:
                ce[z, 8 + nx :, 2 * LANES :] = value[:8, :]
            else:
                ce[z, 8 : 8 + nx, 2 * LANES :] = value
                value = jnp.where(lane == 0, pltpu.roll(above, LANES - 3 - 4 * z, 1), 0.0)
                value = jnp.where(lane == LANES - 1, pltpu.roll(below, LANES - 4 - 4 * z, 1), value)
                wd[z, 8 : 8 + nx, 2 * LANES :] = value
    for z in range(nz):
        centre = ce[z]
        upper = ce[z + 1] if z + 1 < nz else jnp.zeros_like(centre)
        lower = ce[z - 1] if z > 0 else jnp.zeros_like(centre)
        face_x = 0.5 * (centre + pltpu.roll(centre, tall - 1, 0))
        face_y = 0.5 * (centre + pltpu.roll(centre, wide - 1, 1))
        back_y = pltpu.roll(face_y, 1, 1)
        face_z = 0.5 * (centre + upper)
        total = 1.0 + face_x + pltpu.roll(face_x, 1, 0) + face_y + back_y
        total = total + face_z + 0.5 * (centre + lower)
        inverse = 1.0 / total
        fx[z] = face_x
        fyp[z] = face_y
        fym[z] = back_y
        fz[z] = face_z
        dg[z] = total
        dd[z] = inverse
        wd[z] = wd[z] * inverse

    tile_lane = lax.broadcasted_iota(jnp.int32, (k, LANES), 1)

    def tiles(ref, z, x):
        whole = ref[z, pl.ds(x + 8, 1), :]
        return [whole[:, i * LANES : (i + 1) * LANES] for i in range(3)]

    def split(value):
        return [value[:, i * LANES : (i + 1) * LANES] for i in range(value.shape[1] // LANES)]

    def store(ref, z, x, parts):
        for i in range(len(parts)):
            ref[z, x, :, i * LANES : (i + 1) * LANES] = parts[i]

    def edge_tile(z, x, which):
        line = z * nx + x
        above = pltpu.roll(hf[3 + which], lax.rem(LANES - 2 * line + LANES, LANES), 1)
        below = pltpu.roll(hf[which], lax.rem(2 * LANES - 2 - 2 * line, LANES), 1)
        return jnp.where(tile_lane < LANES // 2, above, below)

    def inner_tiles(z, x, value):
        inverse = tiles(dd, z, x)
        parts = split(value)
        store(f1, z, x + 2, [parts[i] * inverse[i] for i in range(2)])

    def edge_tiles(z, x, edge):
        f1[z, x + 2, :, 2 * LANES :] = edge * tiles(dd, z, x)[2]

    def forward_inner(x, carry):
        for z in range(nz):
            inner_tiles(z, x, pt[z, x].astype(F32))
        return carry

    lax.fori_loop(0, nx, forward_inner, 0)
    for copy in probe_copies[:6]:
        copy.wait_recv()

    for which in range(3):
        hf[which] = hy[which].astype(F32) * (has_x[which] * has_y[0])
        hf[3 + which] = hy[3 + which].astype(F32) * (has_x[which] * has_y[1])

    def forward_edges(x, carry):
        for z in range(nz):
            edge_tiles(z, x, edge_tile(z, x, 1))
        return carry

    lax.fori_loop(0, nx, forward_edges, 0)
    def near(ref, z, x, row, count):
        centre = split(ref[z, row])
        ahead = [pltpu.roll(part, LANES - 1, 1) for part in centre]
        behind = [pltpu.roll(part, 1, 1) for part in centre]
        east, west = split(ref[z, row + 1]), split(ref[z, row - 1])
        face_e, face_w = tiles(fx, z, x), tiles(fx, z, x - 1)
        face_n, face_s = tiles(fyp, z, x), tiles(fym, z, x)
        if z + 1 < nz:
            upper, face_u = split(ref[z + 1, row]), tiles(fz, z, x)
        if z > 0:
            lower, face_d = split(ref[z - 1, row]), tiles(fz, z - 1, x)
        sums = []
        for i in range(count):
            north = jnp.where(tile_lane == LANES - 1, ahead[(i + 1) % 3], ahead[i])
            south = jnp.where(tile_lane == 0, behind[(i + 2) % 3], behind[i])
            total = face_e[i] * east[i] + face_w[i] * west[i]
            total = total + (face_n[i] * north + face_s[i] * south)
            if z + 1 < nz:
                total = total + face_u[i] * upper[i]
            if z > 0:
                total = total + face_d[i] * lower[i]
            sums.append(total)
        return centre, sums

    def adjoint(i, carry):
        x = i - 1
        for z in range(nz):
            centre, sums = near(f1, z, x, x + 2, 3)
            diagonal, inverse, gain = tiles(dg, z, x), tiles(dd, z, x), tiles(wd, z, x)
            parts = [
                (centre[i] * diagonal[i] + sums[i]) * gain[i] * inverse[i] for i in range(3)
            ]
            store(a1, z, x + 1, parts)
        return carry

    acc[...] = jnp.zeros_like(acc)

    def finish(x):
        for z in range(nz):
            centre, sums = near(a1, z, x, x + 1, 2)
            diagonal, inverse = tiles(dg, z, x), tiles(dd, z, x)
            source = split(pt[z, x].astype(F32))
            sketch = jnp.concatenate(
                [
                    (centre[i] * diagonal[i] + sums[i]) * inverse[i] + source[i]
                    for i in range(2)
                ],
                axis=1,
            )
            high = sketch.astype(BF16)
            shl[z * nx + x, 0:k, :] = high
            shl[z * nx + x, k : 2 * k, :] = (sketch - high.astype(F32)).astype(BF16)

    def products(x, slot, apart):
        whole = [shl[z * nx + x] for z in range(nz)]
        applied = lax.dot_general(
            jnp.concatenate([part[0:k] for part in whole], axis=0),
            wt[...],
            NT,
            preferred_element_type=F32,
        )
        rows = []
        for z in range(nz):
            part = applied[z * k : (z + 1) * k]
            cuf[slot + z * apart] = part[:, leaf:]
            rows.append(part[:, :leaf].astype(BF16))
        lhs = jnp.concatenate(whole, axis=1)
        rhs = jnp.concatenate([lhs, jnp.concatenate(rows, axis=1)], axis=0)
        acc[...] += lax.dot_general(lhs, rhs, NT, preferred_element_type=F32)

    lax.fori_loop(2, nx, adjoint, 0)
    inner_rows = nx - 4
    early = nz * inner_rows // (LANES // rank)

    def finish_inner(x, carry):
        products(x - 1, x - 3, inner_rows)
        finish(x)
        return carry

    finish(2)
    lax.fori_loop(3, nx - 2, finish_inner, 0)
    products(nx - 3, nx - 5, inner_rows)

    count = LANES // rank
    slot = tile_lane // rank

    def gather(group, carry):
        parts = [cuf[group * count + j] for j in range(count)]
        step = 1
        while step < count:
            bit = (slot // step) % 2 == 0
            for i in range(count):
                if (i // step) % 2 == 0:
                    one, two = parts[i], parts[i + step]
                    parts[i] = jnp.where(bit, one, pltpu.roll(two, step * rank, 1))
                    parts[i + step] = jnp.where(bit, pltpu.roll(one, LANES - step * rank, 1), two)
            step *= 2
        for index in range(2 * levels):
            uc[index, group] = parts[index].astype(BF16)
        return carry

    lax.fori_loop(0, early, gather, 0)

    def flipped(bits):
        device = gy
        for b in range(levels):
            if bits >> b & 1:
                device = device + (1 - 2 * lax.rem(device // 2**b, 2)) * 2**b
        return device

    tree = []
    for level in range(levels):
        half = 2**level
        share = groups // half
        for bits in range(1, 2 * half):
            peer = flipped(bits)
            kind = 2 * level + (1 if bits < half else 0)
            begin = lax.rem(peer, half) * share
            copy = pltpu.make_async_remote_copy(
                src_ref=uc.at[kind, pl.ds(begin, share)],
                dst_ref=trees[level].at[bits - 1],
                send_sem=tree_send.at[2 * half - 2 - level + bits],
                recv_sem=tree_recv.at[2 * half - 2 - level + bits],
                device_id=(gx, peer),
                device_id_type=MESH,
            )
            tree.append((copy, lax.rem(peer, half) < early // share, early < share))

    for copy, ready, never in tree:
        if not never:
            pl.when(ready)(copy.start)
    for copy in probe_copies[6:]:
        copy.wait_recv()
    for z in range(nz):
        for i in range(2):
            inner_tiles(z, i - 2, xh[0, z, i].astype(F32) * has_west)
            edge_tiles(z, i - 2, edge_tile(z, nx - 2 + i, 0))
            inner_tiles(z, nx + i, xh[1, z, i].astype(F32) * has_east)
            edge_tiles(z, nx + i, edge_tile(z, i, 2))

    def adjoint_outer(i, carry):
        return adjoint(jnp.where(i < 2, i, nx - 2 + i), carry)

    def outer_row(i):
        return jnp.where(i < 2, i, nx - 4 + i)

    def finish_outer(i, carry):
        products(outer_row(i - 1), nz * inner_rows + i - 1, 4)
        finish(outer_row(i))
        return carry

    lax.fori_loop(0, 4, adjoint_outer, 0)
    finish(0)
    lax.fori_loop(1, 4, finish_outer, 0)
    products(nx - 1, nz * inner_rows + 3, 4)

    half_k, half_lanes = k // 2, LANES // 2
    half_lane = lax.broadcasted_iota(jnp.int32, (half_k, LANES), 1)
    pad = jnp.zeros((k, LANES - k), F32)

    def fold(value):
        value = jnp.concatenate([value, pad], axis=1)
        return value[:half_k] + pltpu.roll(value[half_k:], half_lanes, 1)

    def unfold(value):
        first = jnp.where(half_lane < half_lanes, value, 0.0)
        second = pltpu.roll(jnp.where(half_lane < half_lanes, 0.0, value), half_lanes, 1)
        return jnp.concatenate([first, second], axis=0) * (1.0 / cells)

    pending = []

    def send(which, stage, value):
        peers, me = stages[stage]
        packed[which, stage] = value
        gathered[which, stage, me] = value
        copies = [
            remote(
                packed.at[which, stage], gathered.at[which, stage, me],
                sum_send.at[which, stage, d], sum_recv.at[which, stage, d], peer,
            )
            for d, peer in enumerate(peers)
        ]
        pending.extend(copies)
        return copies

    def receive(which, stage, copies):
        for copy in copies:
            copy.wait_recv()
        parts = [gathered[which, stage, i] for i in range(len(copies) + 1)]
        while len(parts) > 1:
            parts = [
                parts[i] + parts[i + 1] if i + 1 < len(parts) else parts[i]
                for i in range(0, len(parts), 2)
            ]
        return parts[0]

    value = acc[...]
    total = value[0:k, 0:k] + (value[0:k, k : 2 * k] + value[k : 2 * k, 0:k]) + value[k:, k : 2 * k]
    first = send(0, 0, fold(total))
    leafpart = value[0:k, 2 * k :] + value[k:, 2 * k :]

    lax.fori_loop(early, groups, gather, 0)
    for copy, ready, never in tree:
        if never:
            copy.start()
        else:
            pl.when(jnp.logical_not(ready))(copy.start)

    first = send(0, 1, receive(0, 0, first))
    for copy, _, _ in tree:
        copy.wait_recv()
    lefts, rights = [], []
    for level in range(levels):
        half = 2**level
        share = groups // half
        begin = lax.rem(gy, half) * share
        for j in range(share):
            own = uc[2 * level + 1, begin + j].astype(F32)
            for bits in range(1, half):
                own = own + trees[level][bits - 1, j].astype(F32)
            other = trees[level][half - 1, j].astype(F32)
            for bits in range(half + 1, 2 * half):
                other = other + trees[level][bits - 1, j].astype(F32)
            lefts.append(own.astype(BF16))
            rights.append(other.astype(BF16))
    total = leafpart + lax.dot_general(
        jnp.concatenate(lefts, axis=1),
        jnp.concatenate(rights, axis=1),
        NT,
        preferred_element_type=F32,
    )
    second = send(1, 0, fold(total))
    first = send(0, 2, receive(0, 1, first))
    second = send(1, 1, receive(1, 0, second))
    matrix = unfold(receive(0, 2, first))

    row = lax.broadcasted_iota(jnp.int32, (k, LANES), 0)
    lane = lax.broadcasted_iota(jnp.int32, (k, LANES), 1)
    start = LANES // 2
    whole = jnp.where(lane < k, matrix, jnp.where(lane == row + start, 1.0, 0.0))
    blocks = [whole[8 * t : 8 * t + 8] for t in range(k // 8)]
    inverse = []
    for t in range(k // 8):
        done, scale = eliminate(blocks, t)
        inverse.append(done[:, start : start + k] * scale[:, 0:k])
        if t == k // 16:
            second = send(1, 2, receive(1, 1, second))
    inverse = jnp.concatenate(inverse, axis=0)

    high = inverse.astype(BF16)
    low = (inverse - high.astype(F32)).astype(BF16)
    lhs = jnp.concatenate(
        [
            jnp.concatenate([high, high], axis=1),
            jnp.concatenate([low, jnp.zeros_like(low)], axis=1),
        ],
        axis=0,
    )
    stores = []
    for z in range(nz):

        def one(x, carry):
            value = jnp.dot(lhs, shl[z * nx + x], preferred_element_type=F32)
            value = value[0:k] + value[k:]
            buffer[z, 0, pl.ds(x, k, stride=nx), :] = value[:, :LANES]
            buffer[z, 1, pl.ds(x, k, stride=nx), :] = value[:, LANES:]
            return carry

        lax.fori_loop(0, nx, one, 0, unroll=8)
        for i in range(2):
            copy = pltpu.make_async_copy(
                buffer.at[z, i].reshape(k, nx, LANES),
                out.at[:, z, :, i * LANES : (i + 1) * LANES],
                store_sem.at[z, i],
            )
            copy.start()
            stores.append(copy)
    middle = unfold(receive(1, 2, second))[:, 0:k]
    product = jnp.dot(inverse, middle, precision=HIGH, preferred_element_type=F32)
    product = lax.dot_general(product, inverse, NT, precision=HIGH, preferred_element_type=F32)
    projected[...] = product + jnp.where(lane[:, 0:k] == row[:, 0:k], 1.0, 0.0)
    for copy in field_copies + probe_copies + [copy for copy, _, _ in tree] + pending:
        copy.wait_send()
    for copy in stores:
        copy.wait()


def copy_kernel(pieces, basis_in, projected_in, basis, projected, wide, small, load_sem, store_sem):
    size = basis.shape[0] // pieces
    parts = [pl.ds(i * size, size) for i in range(pieces)]
    loads = [
        pltpu.make_async_copy(basis_in.at[part], wide.at[part], load_sem.at[i])
        for i, part in enumerate(parts)
    ]
    loads.insert(1, pltpu.make_async_copy(projected_in, small, load_sem.at[pieces]))
    stores = [
        pltpu.make_async_copy(wide.at[part], basis.at[part], store_sem.at[i])
        for i, part in enumerate(parts)
    ]
    stores.insert(1, pltpu.make_async_copy(small, projected, store_sem.at[pieces]))
    for load in loads:
        load.start()
    for load, store in zip(loads, stores):
        load.wait()
        store.start()
    for store in stores:
        store.wait()


def params(**more):
    return pltpu.CompilerParams(vmem_limit_bytes=56 * 2**20, **more)


def shards(
    probes, classes, class_table, weights, prior_block, prior_left, prior_right, block_ranks
):
    ng, ny = lax.axis_size("gx"), lax.axis_size("gy")
    k, nz, nx, leaf = probes.shape
    levels = ny.bit_length() - 1
    rank = prior_left.shape[1]
    lines = nz * nx
    groups = lines * rank // LANES
    cells = float(nz * nx * leaf * ng * ny)
    shape = jax.ShapeDtypeStruct
    dma = pltpu.SemaphoreType.DMA
    vmem = pltpu.VMEM
    edges = 2 * ny
    most = 8
    while most < max(ng // min(4, ng), ny // min(2, ny)):
        most *= 2

    field = vmem((nz, nx + 16, 3 * LANES), F32)
    basis, projected = pl.pallas_call(
        functools.partial(
            sketch_kernel, ng, ny, k, nz, nx, levels, leaf, groups, cells
        ),
        out_shape=(
            shape((k, nz, nx, leaf), F32),
            shape((k, k), F32),
        ),
        in_specs=[HBM] * 8,
        out_specs=(HBM, VMEM),
        scratch_shapes=[
            vmem((lines, 2 * k, leaf), BF16),
            vmem((nz, 2, k * nx, LANES), F32),
            dma((nz, 2)),
            vmem((k * lines, leaf), BF16),
            vmem(classes.shape, classes.dtype),
            pltpu.SMEM(class_table.shape, F32),
            vmem(weights.shape, F32),
            vmem(prior_block.shape, F32),
            vmem((levels, rank, leaf), F32),
            vmem((levels, rank, leaf), F32),
            pltpu.SMEM(block_ranks.shape, block_ranks.dtype),
            dma((8,)),
            vmem((nz, nx, k, leaf), BF16),
            vmem((nz, nx, leaf), F32),
            vmem((2, k * lines, LANES), F32),
            vmem((2, nz, 2, k, leaf), BF16),
            vmem((6, k, LANES), BF16),
            vmem((6, k, LANES), F32),
            vmem((2, 4 * nz, leaf), F32),
            vmem((6, nx, LANES), F32),
            vmem((2, k, LANES), BF16),
            vmem((2, 4 * nz, leaf), F32),
            vmem((2, nx, LANES), F32),
            dma((16,)),
            dma((16,)),
        ]
        + [field] * 8
        + [
            vmem((nz, nx + 4, k, 3 * LANES), F32),
            vmem((nz, nx + 2, k, 3 * LANES), F32),
            vmem((leaf + LANES, leaf), BF16),
            vmem((2 * k, 3 * k), F32),
            vmem((lines, k, LANES), F32),
            vmem((2 * levels, groups, k, LANES), BF16),
            [
                vmem((2 ** (level + 1) - 1, groups >> level, k, LANES), BF16)
                for level in range(levels)
            ],
            dma((edges,)),
            dma((edges,)),
            vmem((2, 3, k // 2, LANES), F32),
            vmem((2, 3, most, k // 2, LANES), F32),
            dma((2, 3, most)),
            dma((2, 3, most)),
        ],
        compiler_params=params(collective_id=0, has_side_effects=True),
    )(
        probes.reshape(k * lines, leaf), classes, class_table, weights, prior_block, prior_left,
        prior_right, block_ranks,
    )
    pieces = 8
    return pl.pallas_call(
        functools.partial(copy_kernel, pieces),
        out_shape=(shape((k, nz, nx, leaf), F32), shape((k, k), F32)),
        in_specs=[HBM] * 2,
        out_specs=(HBM, HBM),
        scratch_shapes=[
            vmem((k, nz, nx, leaf), F32),
            vmem((k, k), F32),
            dma((pieces + 1,)),
            dma((pieces + 1,)),
        ],
        compiler_params=params(),
    )(basis, projected)


def solution(mesh):
    return jax.shard_map(
        shards,
        mesh=mesh,
        in_specs=(
            P(None, None, "gx", "gy"),
            P(None, "gx", "gy"),
            P(),
            P(None, "gx", "gy"),
            P("gy", None),
            P(None, None, "gy"),
            P(None, None, "gy"),
            P(),
        ),
        out_specs=(P(None, None, "gx", "gy"), P()),
        check_vma=False,
    )
```

```python
import functools

import jax
import jax.numpy as jnp
from jax import lax
from jax.experimental import pallas as pl
from jax.experimental.pallas import tpu as pltpu
from jax.sharding import PartitionSpec as P

MESH = pl.DeviceIdType.MESH
HIGH = lax.Precision.HIGHEST
F32 = jnp.float32
BF16 = jnp.bfloat16
LANES = 128
VMEM = pl.BlockSpec(memory_space=pltpu.VMEM)
SMEM = pl.BlockSpec(memory_space=pltpu.SMEM)
ANY = pl.BlockSpec(memory_space=pl.ANY)
HBM = pl.BlockSpec(memory_space=pltpu.HBM)
NT = (((1,), (1,)), ((), ()))


def signal_all(devices):
    barrier = pltpu.get_barrier_semaphore()
    for device in devices:
        pl.semaphore_signal(barrier, inc=1, device_id=device, device_id_type=MESH)
    return barrier, len(devices)


def remote(src, dst, send, recv, device):
    copy = pltpu.make_async_remote_copy(
        src_ref=src, dst_ref=dst, send_sem=send, recv_sem=recv, device_id=device, device_id_type=MESH
    )
    copy.start()
    return copy


def eliminate(blocks, t):
    inner = lax.broadcasted_iota(jnp.int32, (8, LANES), 0)

    def spread(value):
        return jnp.broadcast_to(value, (8, LANES))

    columns = [spread(blocks[t][:, 8 * t + c : 8 * t + c + 1]) for c in range(8)]
    entry = [[spread(columns[c][r : r + 1, :]) for c in range(r + 1)] for r in range(8)]
    rows = [spread(blocks[t][r : r + 1, :]) for r in range(8)]
    factor = [[None] * 8 for _ in range(8)]
    inverses = []
    for q in range(8):
        inverses.append(1.0 / entry[q][q])
        for r in range(q + 1, 8):
            factor[r][q] = entry[r][q] * inverses[q]
        for r in range(q + 1, 8):
            for c in range(q + 1, r + 1):
                entry[r][c] = entry[r][c] - factor[r][q] * entry[c][q]
    for r in range(8):
        for q in range(r):
            rows[r] = rows[r] - factor[r][q] * rows[q]
    scaled = [rows[q] * inverses[q] for q in range(8)]
    for i in range(t + 1, len(blocks)):
        lefts = [spread(blocks[i][:, 8 * t + q : 8 * t + q + 1]) for q in range(8)]
        for q in range(8):
            for p in range(q):
                lefts[q] = lefts[q] - lefts[p] * factor[q][p]
        changes = [lefts[q] * scaled[q] for q in range(8)]
        while len(changes) > 1:
            changes = [changes[n] + changes[n + 1] for n in range(0, len(changes), 2)]
        blocks[i] = blocks[i] - changes[0]
    done, pivots = rows[0], entry[0][0]
    for r in range(1, 8):
        done = jnp.where(inner == r, rows[r], done)
        pivots = jnp.where(inner == r, entry[r][r], pivots)
    return done, 1.0 / jnp.sqrt(pivots)


def sketch_kernel(
    ng, ny, k, nz, nx, levels, leaf, groups, cells,
    probes_in, classes_in, table_in, weights_in, block_in, left_in, right_in, ranks_in,
    out, projected,
    shl, buffer, store_sem, probes, classes, table, weights, block, left, right, ranks, load_sem,
    pt, cond, pf, xh, hy, hf, cx, cy, hs, cxs, cys, send_sem, recv_sem,
    ce, dg, dd, wd, fx, fyp, fym, fz, f1, a1, wt, acc, cuf, uc,
    trees, tree_send, tree_recv, packed, gathered, sum_send, sum_recv,
):
    gx, gy = lax.axis_index("gx"), lax.axis_index("gy")
    east, west = lax.rem(gx + 1, ng), lax.rem(gx + ng - 1, ng)
    north, south = lax.rem(gy + 1, ny), lax.rem(gy + ny - 1, ny)
    around = [(west, gy), (east, gy)]
    for column in (south, north):
        for row in (west, gx, east):
            around.append((row, column))

    across, pair = min(4, ng), min(2, ny)
    deep, high_y = ng // across, ny // pair
    at_z, at_x = gx // across, lax.rem(gx, across)
    at_y, at_c = gy // pair, lax.rem(gy, pair)
    stages = [
        (
            [
                (
                    at_z * across + lax.rem(at_x + d % across, across),
                    at_y * pair + lax.rem(at_c + d // across, pair),
                )
                for d in range(1, across * pair)
            ],
            at_c * across + at_x,
        ),
        ([(lax.rem(at_z + d, deep) * across + at_x, gy) for d in range(1, deep)], at_z),
        ([(gx, lax.rem(at_y + d, high_y) * pair + at_c) for d in range(1, high_y)], at_y),
    ]
    column = [(gx, lax.rem(gy + d, ny)) for d in range(1, ny)]
    loads = [
        pltpu.make_async_copy(source, target, load_sem.at[i])
        for i, (source, target) in enumerate(
            [
                (classes_in, classes),
                (weights_in, weights),
                (table_in, table),
                (probes_in, probes),
                (block_in, block),
                (left_in.at[0:levels], left),
                (right_in.at[0:levels], right),
                (ranks_in, ranks),
            ]
        )
    ]
    for load in loads:
        load.start()
    barrier, count = signal_all(around + stages[0][0] + stages[1][0] + column)

    lines = nz * nx
    for load in loads[:3]:
        load.wait()

    for z in range(nz):
        picked = classes[z]
        value = jnp.zeros(picked.shape, F32)
        for index in range(table.shape[0]):
            value = jnp.where(picked == index, table[index], value)
        cond[z] = value
        cxs[0, 4 * z : 4 * z + 3, :] = value[0:3, :]
        cxs[1, 4 * z : 4 * z + 3, :] = value[nx - 3 : nx, :]
        cxs[0, 4 * z + 3 : 4 * z + 4, :] = weights[z, 0:1, :]
        cxs[1, 4 * z + 3 : 4 * z + 4, :] = weights[z, nx - 1 : nx, :]
    lane = lax.broadcasted_iota(jnp.int32, (nx, LANES), 1)
    low = jnp.zeros((nx, LANES), F32)
    high = jnp.zeros((nx, LANES), F32)
    for z in range(nz):
        here = lane // 4 == z
        last = lane % 4 == 3
        first_tile, last_tile = cond[z, :, :LANES], cond[z, :, LANES:]
        w_first, w_last = weights[z, :, :LANES], weights[z, :, LANES:]
        own = jnp.where(last, pltpu.roll(w_first, 4 * z + 3, 1), pltpu.roll(first_tile, 4 * z, 1))
        low = jnp.where(here, own, low)
        own = jnp.where(last, pltpu.roll(w_last, 4 * z + 4, 1), pltpu.roll(last_tile, 4 * z + 3, 1))
        high = jnp.where(here, own, high)
    cys[0] = low
    cys[1] = high

    loads[3].wait()
    chunk = 512

    def widen(i, carry):
        rows = pl.ds(pl.multiple_of(i * chunk, chunk), chunk)
        value = probes[rows, :].astype(F32)
        pf[0, rows, :] = value[:, :LANES]
        pf[1, rows, :] = value[:, LANES:]
        return carry

    lax.fori_loop(0, k * lines // chunk, widen, 0)

    place = lax.broadcasted_iota(jnp.int32, (k, LANES), 1) // 2

    def turn(line, carry):
        low, high = carry
        lo = pf[0, pl.ds(line, k, stride=lines), :]
        hi = pf[1, pl.ds(line, k, stride=lines), :]
        pt[line // nx, lax.rem(line, nx)] = jnp.concatenate([lo, hi], axis=1).astype(BF16)
        low = jnp.where(place == line, pltpu.roll(lo, 2 * line, 1), low)
        high = jnp.where(place == line, pltpu.roll(hi, lax.rem(2 * line + 2, LANES), 1), high)
        return low, high

    zero = jnp.zeros((k, LANES), F32)
    low, high = lax.fori_loop(0, lines, turn, (zero, zero), unroll=4)
    hs[0] = low.astype(BF16)
    hs[1] = high.astype(BF16)

    pl.semaphore_wait(barrier, count)
    field_copies = [
        remote(cxs.at[1], cx.at[0], send_sem.at[2], recv_sem.at[2], (east, gy)),
        remote(cxs.at[0], cx.at[1], send_sem.at[3], recv_sem.at[3], (west, gy)),
    ]
    probe_copies = []
    used = 4
    arrivals = [
        (side, which, row, column)
        for side, column in ((0, north), (1, south))
        for which, row in ((2, west), (1, gx), (0, east))
    ]
    for i, (side, which, row, column) in enumerate(arrivals):
        slot = side * 3 + which
        field_copies.append(
            remote(
                cys.at[1 - side], cy.at[slot], send_sem.at[4 + i], recv_sem.at[4 + i], (row, column)
            )
        )
    for i, (side, which, row, column) in enumerate(arrivals):
        slot = side * 3 + which
        probe_copies.append(
            remote(
                hs.at[1 - side], hy.at[slot], send_sem.at[10 + i], recv_sem.at[10 + i], (row, column)
            )
        )
    probe_copies += [
        remote(pt.at[:, nx - 2 : nx], xh.at[0], send_sem.at[0], recv_sem.at[0], (east, gy)),
        remote(pt.at[:, 0:2], xh.at[1], send_sem.at[1], recv_sem.at[1], (west, gy)),
    ]

    has_west = (gx > 0).astype(F32)
    has_east = (gx < ng - 1).astype(F32)
    has_south = (gy > 0).astype(F32)
    has_north = (gy < ny - 1).astype(F32)
    has_x = (has_west, 1.0, has_east)
    has_y = (has_south, has_north)
    rank = left.shape[1]
    for load in loads[4:]:
        load.wait()

    wt[0:leaf, :] = block[...].astype(BF16)
    row = lax.broadcasted_iota(jnp.int32, (rank, leaf), 0)
    for level in range(levels):
        gain = jnp.where(row < ranks[level], float(leaf * 2**level) ** -0.5, 0.0)
        at = leaf + 2 * level * rank
        wt[at : at + rank, :] = (right[level] * gain).astype(BF16)
        wt[at + rank : at + 2 * rank, :] = left[level].astype(BF16)

    for copy in field_copies:
        copy.wait_recv()

    tall = nx + 16
    wide = 3 * LANES
    lane = lax.broadcasted_iota(jnp.int32, (nx, LANES), 1)
    for z in range(nz):
        ce[z] = jnp.zeros((tall, wide), F32)
        wd[z] = jnp.zeros((tall, wide), F32)
        ce[z, 8 : 8 + nx, 0 : 2 * LANES] = cond[z]
        wd[z, 8 : 8 + nx, 0 : 2 * LANES] = weights[z]
        ce[z, 5:8, 0 : 2 * LANES] = cx[0, 4 * z : 4 * z + 3, :] * has_west
        wd[z, 7:8, 0 : 2 * LANES] = cx[0, 4 * z + 3 : 4 * z + 4, :] * has_west
        ce[z, 8 + nx : 11 + nx, 0 : 2 * LANES] = cx[1, 4 * z : 4 * z + 3, :] * has_east
        wd[z, 8 + nx : 9 + nx, 0 : 2 * LANES] = cx[1, 4 * z + 3 : 4 * z + 4, :] * has_east
        for which in range(3):
            above = cy[3 + which] * (has_x[which] * has_y[1])
            below = cy[which] * (has_x[which] * has_y[0])
            value = jnp.where(lane < 3, pltpu.roll(above, (LANES - 4 * z) % LANES, 1), 0.0)
            value = jnp.where(lane > LANES - 4, pltpu.roll(below, LANES - 3 - 4 * z, 1), value)
            if which == 0:
                ce[z, 0:8, 2 * LANES :] = value[nx - 8 :, :]
            elif which == 2:
                ce[z, 8 + nx :, 2 * LANES :] = value[:8, :]
            else:
                ce[z, 8 : 8 + nx, 2 * LANES :] = value
                value = jnp.where(lane == 0, pltpu.roll(above, LANES - 3 - 4 * z, 1), 0.0)
                value = jnp.where(lane == LANES - 1, pltpu.roll(below, LANES - 4 - 4 * z, 1), value)
                wd[z, 8 : 8 + nx, 2 * LANES :] = value
    for z in range(nz):
        centre = ce[z]
        upper = ce[z + 1] if z + 1 < nz else jnp.zeros_like(centre)
        lower = ce[z - 1] if z > 0 else jnp.zeros_like(centre)
        face_x = 0.5 * (centre + pltpu.roll(centre, tall - 1, 0))
        face_y = 0.5 * (centre + pltpu.roll(centre, wide - 1, 1))
        back_y = pltpu.roll(face_y, 1, 1)
        face_z = 0.5 * (centre + upper)
        total = 1.0 + face_x + pltpu.roll(face_x, 1, 0) + face_y + back_y
        total = total + face_z + 0.5 * (centre + lower)
        inverse = 1.0 / total
        fx[z] = face_x
        fyp[z] = face_y
        fym[z] = back_y
        fz[z] = face_z
        dg[z] = total
        dd[z] = inverse
        wd[z] = wd[z] * inverse

    tile_lane = lax.broadcasted_iota(jnp.int32, (k, LANES), 1)

    def tiles(ref, z, x):
        whole = ref[z, pl.ds(x + 8, 1), :]
        return [whole[:, i * LANES : (i + 1) * LANES] for i in range(3)]

    def split(value):
        return [value[:, i * LANES : (i + 1) * LANES] for i in range(value.shape[1] // LANES)]

    def store(ref, z, x, parts):
        for i in range(len(parts)):
            ref[z, x, :, i * LANES : (i + 1) * LANES] = parts[i]

    def edge_tile(z, x, which):
        line = z * nx + x
        above = pltpu.roll(hf[3 + which], lax.rem(LANES - 2 * line + LANES, LANES), 1)
        below = pltpu.roll(hf[which], lax.rem(2 * LANES - 2 - 2 * line, LANES), 1)
        return jnp.where(tile_lane < LANES // 2, above, below)

    def inner_tiles(z, x, value):
        inverse = tiles(dd, z, x)
        parts = split(value)
        store(f1, z, x + 2, [parts[i] * inverse[i] for i in range(2)])

    def edge_tiles(z, x, edge):
        f1[z, x + 2, :, 2 * LANES :] = edge * tiles(dd, z, x)[2]

    def forward_inner(x, carry):
        for z in range(nz):
            inner_tiles(z, x, pt[z, x].astype(F32))
        return carry

    lax.fori_loop(0, nx, forward_inner, 0, unroll=2)
    for copy in probe_copies[:6]:
        copy.wait_recv()

    for which in range(3):
        hf[which] = hy[which].astype(F32) * (has_x[which] * has_y[0])
        hf[3 + which] = hy[3 + which].astype(F32) * (has_x[which] * has_y[1])

    def forward_edges(x, carry):
        for z in range(nz):
            edge_tiles(z, x, edge_tile(z, x, 1))
        return carry

    lax.fori_loop(0, nx, forward_edges, 0, unroll=2)
    def near(ref, z, x, row, count):
        centre = split(ref[z, row])
        ahead = [pltpu.roll(part, LANES - 1, 1) for part in centre]
        behind = [pltpu.roll(part, 1, 1) for part in centre]
        east, west = split(ref[z, row + 1]), split(ref[z, row - 1])
        face_e, face_w = tiles(fx, z, x), tiles(fx, z, x - 1)
        face_n, face_s = tiles(fyp, z, x), tiles(fym, z, x)
        if z + 1 < nz:
            upper, face_u = split(ref[z + 1, row]), tiles(fz, z, x)
        if z > 0:
            lower, face_d = split(ref[z - 1, row]), tiles(fz, z - 1, x)
        sums = []
        for i in range(count):
            north = jnp.where(tile_lane == LANES - 1, ahead[(i + 1) % 3], ahead[i])
            south = jnp.where(tile_lane == 0, behind[(i + 2) % 3], behind[i])
            total = face_e[i] * east[i] + face_w[i] * west[i]
            total = total + (face_n[i] * north + face_s[i] * south)
            if z + 1 < nz:
                total = total + face_u[i] * upper[i]
            if z > 0:
                total = total + face_d[i] * lower[i]
            sums.append(total)
        return centre, sums

    def adjoint(i, carry):
        x = i - 1
        for z in range(nz):
            centre, sums = near(f1, z, x, x + 2, 3)
            diagonal, inverse, gain = tiles(dg, z, x), tiles(dd, z, x), tiles(wd, z, x)
            parts = [
                (centre[i] * diagonal[i] + sums[i]) * gain[i] * inverse[i] for i in range(3)
            ]
            store(a1, z, x + 1, parts)
        return carry

    acc[...] = jnp.zeros_like(acc)

    def finish(x):
        for z in range(nz):
            centre, sums = near(a1, z, x, x + 1, 2)
            diagonal, inverse = tiles(dg, z, x), tiles(dd, z, x)
            source = split(pt[z, x].astype(F32))
            sketch = jnp.concatenate(
                [
                    (centre[i] * diagonal[i] + sums[i]) * inverse[i] + source[i]
                    for i in range(2)
                ],
                axis=1,
            )
            high = sketch.astype(BF16)
            shl[z * nx + x, 0:k, :] = high
            shl[z * nx + x, k : 2 * k, :] = (sketch - high.astype(F32)).astype(BF16)

    def products(x, slot, apart):
        whole = [shl[z * nx + x] for z in range(nz)]
        applied = lax.dot_general(
            jnp.concatenate([part[0:k] for part in whole], axis=0),
            wt[...],
            NT,
            preferred_element_type=F32,
        )
        rows = []
        for z in range(nz):
            part = applied[z * k : (z + 1) * k]
            cuf[slot + z * apart] = part[:, leaf:]
            rows.append(part[:, :leaf].astype(BF16))
        lhs = jnp.concatenate(whole, axis=1)
        rhs = jnp.concatenate([lhs, jnp.concatenate(rows, axis=1)], axis=0)
        acc[...] += lax.dot_general(lhs, rhs, NT, preferred_element_type=F32)

    lax.fori_loop(2, nx, adjoint, 0, unroll=2)
    inner_rows = nx - 4
    early = nz * inner_rows // (LANES // rank)

    def finish_inner(x, carry):
        products(x - 1, x - 3, inner_rows)
        finish(x)
        return carry

    finish(2)
    lax.fori_loop(3, nx - 2, finish_inner, 0)
    products(nx - 3, nx - 5, inner_rows)

    count = LANES // rank
    slot = tile_lane // rank

    def gather(group, carry):
        parts = [cuf[group * count + j] for j in range(count)]
        step = 1
        while step < count:
            bit = (slot // step) % 2 == 0
            for i in range(count):
                if (i // step) % 2 == 0:
                    one, two = parts[i], parts[i + step]
                    parts[i] = jnp.where(bit, one, pltpu.roll(two, step * rank, 1))
                    parts[i + step] = jnp.where(bit, pltpu.roll(one, LANES - step * rank, 1), two)
            step *= 2
        for index in range(2 * levels):
            uc[index, group] = parts[index].astype(BF16)
        return carry

    lax.fori_loop(0, early, gather, 0, unroll=2)

    def flipped(bits):
        device = gy
        for b in range(levels):
            if bits >> b & 1:
                device = device + (1 - 2 * lax.rem(device // 2**b, 2)) * 2**b
        return device

    tree = []
    for level in range(levels):
        half = 2**level
        share = groups // half
        for bits in range(1, 2 * half):
            peer = flipped(bits)
            kind = 2 * level + (1 if bits < half else 0)
            begin = lax.rem(peer, half) * share
            copy = pltpu.make_async_remote_copy(
                src_ref=uc.at[kind, pl.ds(begin, share)],
                dst_ref=trees[level].at[bits - 1],
                send_sem=tree_send.at[2 * half - 2 - level + bits],
                recv_sem=tree_recv.at[2 * half - 2 - level + bits],
                device_id=(gx, peer),
                device_id_type=MESH,
            )
            tree.append((copy, lax.rem(peer, half) < early // share, early < share))

    for copy, ready, never in tree:
        if not never:
            pl.when(ready)(copy.start)
    for copy in probe_copies[6:]:
        copy.wait_recv()
    for z in range(nz):
        for i in range(2):
            inner_tiles(z, i - 2, xh[0, z, i].astype(F32) * has_west)
            edge_tiles(z, i - 2, edge_tile(z, nx - 2 + i, 0))
            inner_tiles(z, nx + i, xh[1, z, i].astype(F32) * has_east)
            edge_tiles(z, nx + i, edge_tile(z, i, 2))

    def adjoint_outer(i, carry):
        return adjoint(jnp.where(i < 2, i, nx - 2 + i), carry)

    def outer_row(i):
        return jnp.where(i < 2, i, nx - 4 + i)

    def finish_outer(i, carry):
        products(outer_row(i - 1), nz * inner_rows + i - 1, 4)
        finish(outer_row(i))
        return carry

    lax.fori_loop(0, 4, adjoint_outer, 0)
    finish(0)
    lax.fori_loop(1, 4, finish_outer, 0)
    products(nx - 1, nz * inner_rows + 3, 4)

    half_k, half_lanes = k // 2, LANES // 2
    half_lane = lax.broadcasted_iota(jnp.int32, (half_k, LANES), 1)
    pad = jnp.zeros((k, LANES - k), F32)

    def fold(value):
        value = jnp.concatenate([value, pad], axis=1)
        return value[:half_k] + pltpu.roll(value[half_k:], half_lanes, 1)

    def unfold(value):
        first = jnp.where(half_lane < half_lanes, value, 0.0)
        second = pltpu.roll(jnp.where(half_lane < half_lanes, 0.0, value), half_lanes, 1)
        return jnp.concatenate([first, second], axis=0) * (1.0 / cells)

    pending = []

    def send(which, stage, value):
        peers, me = stages[stage]
        packed[which, stage] = value
        gathered[which, stage, me] = value
        copies = [
            remote(
                packed.at[which, stage], gathered.at[which, stage, me],
                sum_send.at[which, stage, d], sum_recv.at[which, stage, d], peer,
            )
            for d, peer in enumerate(peers)
        ]
        pending.extend(copies)
        return copies

    def receive(which, stage, copies):
        for copy in copies:
            copy.wait_recv()
        parts = [gathered[which, stage, i] for i in range(len(copies) + 1)]
        while len(parts) > 1:
            parts = [
                parts[i] + parts[i + 1] if i + 1 < len(parts) else parts[i]
                for i in range(0, len(parts), 2)
            ]
        return parts[0]

    value = acc[...]
    total = value[0:k, 0:k] + (value[0:k, k : 2 * k] + value[k : 2 * k, 0:k]) + value[k:, k : 2 * k]
    first = send(0, 0, fold(total))
    leafpart = value[0:k, 2 * k :] + value[k:, 2 * k :]

    lax.fori_loop(early, groups, gather, 0, unroll=2)
    for copy, ready, never in tree:
        if never:
            copy.start()
        else:
            pl.when(jnp.logical_not(ready))(copy.start)

    first = send(0, 1, receive(0, 0, first))
    for copy, _, _ in tree:
        copy.wait_recv()
    lefts, rights = [], []
    for level in range(levels):
        half = 2**level
        share = groups // half
        begin = lax.rem(gy, half) * share
        for j in range(share):
            own = uc[2 * level + 1, begin + j].astype(F32)
            for bits in range(1, half):
                own = own + trees[level][bits - 1, j].astype(F32)
            other = trees[level][half - 1, j].astype(F32)
            for bits in range(half + 1, 2 * half):
                other = other + trees[level][bits - 1, j].astype(F32)
            lefts.append(own.astype(BF16))
            rights.append(other.astype(BF16))
    total = leafpart + lax.dot_general(
        jnp.concatenate(lefts, axis=1),
        jnp.concatenate(rights, axis=1),
        NT,
        preferred_element_type=F32,
    )
    second = send(1, 0, fold(total))
    first = send(0, 2, receive(0, 1, first))
    second = send(1, 1, receive(1, 0, second))
    matrix = unfold(receive(0, 2, first))

    row = lax.broadcasted_iota(jnp.int32, (k, LANES), 0)
    lane = lax.broadcasted_iota(jnp.int32, (k, LANES), 1)
    start = LANES // 2
    whole = jnp.where(lane < k, matrix, jnp.where(lane == row + start, 1.0, 0.0))
    blocks = [whole[8 * t : 8 * t + 8] for t in range(k // 8)]
    inverse = []
    for t in range(k // 8):
        done, scale = eliminate(blocks, t)
        inverse.append(done[:, start : start + k] * scale[:, 0:k])
        if t == k // 16:
            second = send(1, 2, receive(1, 1, second))
    inverse = jnp.concatenate(inverse, axis=0)

    high = inverse.astype(BF16)
    low = (inverse - high.astype(F32)).astype(BF16)
    lhs = jnp.concatenate(
        [
            jnp.concatenate([high, high], axis=1),
            jnp.concatenate([low, jnp.zeros_like(low)], axis=1),
        ],
        axis=0,
    )
    stores = []
    for z in range(nz):

        def one(x, carry):
            value = jnp.dot(lhs, shl[z * nx + x], preferred_element_type=F32)
            value = value[0:k] + value[k:]
            buffer[z, 0, pl.ds(x, k, stride=nx), :] = value[:, :LANES]
            buffer[z, 1, pl.ds(x, k, stride=nx), :] = value[:, LANES:]
            return carry

        lax.fori_loop(0, nx, one, 0, unroll=8)
        for i in range(2):
            copy = pltpu.make_async_copy(
                buffer.at[z, i].reshape(k, nx, LANES),
                out.at[:, z, :, i * LANES : (i + 1) * LANES],
                store_sem.at[z, i],
            )
            copy.start()
            stores.append(copy)
    middle = unfold(receive(1, 2, second))[:, 0:k]
    product = jnp.dot(inverse, middle, precision=HIGH, preferred_element_type=F32)
    product = lax.dot_general(product, inverse, NT, precision=HIGH, preferred_element_type=F32)
    projected[...] = product + jnp.where(lane[:, 0:k] == row[:, 0:k], 1.0, 0.0)
    for copy in field_copies + probe_copies + [copy for copy, _, _ in tree] + pending:
        copy.wait_send()
    for copy in stores:
        copy.wait()


def copy_kernel(pieces, basis_in, projected_in, basis, projected, wide, small, load_sem, store_sem):
    size = basis.shape[0] // pieces
    parts = [pl.ds(i * size, size) for i in range(pieces)]
    loads = [
        pltpu.make_async_copy(basis_in.at[part], wide.at[part], load_sem.at[i])
        for i, part in enumerate(parts)
    ]
    loads.insert(1, pltpu.make_async_copy(projected_in, small, load_sem.at[pieces]))
    stores = [
        pltpu.make_async_copy(wide.at[part], basis.at[part], store_sem.at[i])
        for i, part in enumerate(parts)
    ]
    stores.insert(1, pltpu.make_async_copy(small, projected, store_sem.at[pieces]))
    for load in loads:
        load.start()
    for load, store in zip(loads, stores):
        load.wait()
        store.start()
    for store in stores:
        store.wait()


def params(**more):
    return pltpu.CompilerParams(vmem_limit_bytes=56 * 2**20, **more)


def shards(
    probes, classes, class_table, weights, prior_block, prior_left, prior_right, block_ranks
):
    ng, ny = lax.axis_size("gx"), lax.axis_size("gy")
    k, nz, nx, leaf = probes.shape
    levels = ny.bit_length() - 1
    rank = prior_left.shape[1]
    lines = nz * nx
    groups = lines * rank // LANES
    cells = float(nz * nx * leaf * ng * ny)
    shape = jax.ShapeDtypeStruct
    dma = pltpu.SemaphoreType.DMA
    vmem = pltpu.VMEM
    edges = 2 * ny
    most = 8
    while most < max(ng // min(4, ng), ny // min(2, ny)):
        most *= 2

    field = vmem((nz, nx + 16, 3 * LANES), F32)
    basis, projected = pl.pallas_call(
        functools.partial(
            sketch_kernel, ng, ny, k, nz, nx, levels, leaf, groups, cells
        ),
        out_shape=(
            shape((k, nz, nx, leaf), F32),
            shape((k, k), F32),
        ),
        in_specs=[HBM] * 8,
        out_specs=(HBM, VMEM),
        scratch_shapes=[
            vmem((lines, 2 * k, leaf), BF16),
            vmem((nz, 2, k * nx, LANES), F32),
            dma((nz, 2)),
            vmem((k * lines, leaf), BF16),
            vmem(classes.shape, classes.dtype),
            pltpu.SMEM(class_table.shape, F32),
            vmem(weights.shape, F32),
            vmem(prior_block.shape, F32),
            vmem((levels, rank, leaf), F32),
            vmem((levels, rank, leaf), F32),
            pltpu.SMEM(block_ranks.shape, block_ranks.dtype),
            dma((8,)),
            vmem((nz, nx, k, leaf), BF16),
            vmem((nz, nx, leaf), F32),
            vmem((2, k * lines, LANES), F32),
            vmem((2, nz, 2, k, leaf), BF16),
            vmem((6, k, LANES), BF16),
            vmem((6, k, LANES), F32),
            vmem((2, 4 * nz, leaf), F32),
            vmem((6, nx, LANES), F32),
            vmem((2, k, LANES), BF16),
            vmem((2, 4 * nz, leaf), F32),
            vmem((2, nx, LANES), F32),
            dma((16,)),
            dma((16,)),
        ]
        + [field] * 8
        + [
            vmem((nz, nx + 4, k, 3 * LANES), F32),
            vmem((nz, nx + 2, k, 3 * LANES), F32),
            vmem((leaf + LANES, leaf), BF16),
            vmem((2 * k, 3 * k), F32),
            vmem((lines, k, LANES), F32),
            vmem((2 * levels, groups, k, LANES), BF16),
            [
                vmem((2 ** (level + 1) - 1, groups >> level, k, LANES), BF16)
                for level in range(levels)
            ],
            dma((edges,)),
            dma((edges,)),
            vmem((2, 3, k // 2, LANES), F32),
            vmem((2, 3, most, k // 2, LANES), F32),
            dma((2, 3, most)),
            dma((2, 3, most)),
        ],
        compiler_params=params(collective_id=0, has_side_effects=True),
    )(
        probes.reshape(k * lines, leaf), classes, class_table, weights, prior_block, prior_left,
        prior_right, block_ranks,
    )
    pieces = 8
    return pl.pallas_call(
        functools.partial(copy_kernel, pieces),
        out_shape=(shape((k, nz, nx, leaf), F32), shape((k, k), F32)),
        in_specs=[HBM] * 2,
        out_specs=(HBM, HBM),
        scratch_shapes=[
            vmem((k, nz, nx, leaf), F32),
            vmem((k, k), F32),
            dma((pieces + 1,)),
            dma((pieces + 1,)),
        ],
        compiler_params=params(),
    )(basis, projected)


def solution(mesh):
    return jax.shard_map(
        shards,
        mesh=mesh,
        in_specs=(
            P(None, None, "gx", "gy"),
            P(None, "gx", "gy"),
            P(),
            P(None, "gx", "gy"),
            P("gy", None),
            P(None, None, "gy"),
            P(None, None, "gy"),
            P(),
        ),
        out_specs=(P(None, None, "gx", "gy"), P()),
        check_vma=False,
    )
```
